32 devices in a mesh: shard: 8 (over z, y), help: 4 (over x, core).
Axes of the slice: x: 2, y: 2, z: 4, core: 2. Of those that a mesh axis runs over, the one named last changes fastest.
Arguments:
- queries: bfloat16 [8192, 768], P(('shard', 'help')), may hold values from -6 to 6
- probe_group: int32 [8192, 2], P(('shard', 'help')), may hold values from 0 to 7, all different within a row; in each aligned block of 256 rows (0 to 255, 256 to 511, ...) at most 128 rows name the same one
- probe_local: int32 [8192, 2], P(('shard', 'help')), may hold values from 0 to 3
- points: bfloat16 [32768, 768], P(('shard', 'help')), may hold values from -6 to 6
- point_cluster: int32 [8, 4096], P('shard'), may hold values from 0 to 3, never falling along the last dimension, each value on 1 to 3072 neighbouring positions
- test_matrix: bfloat16 [32, 32768], P(None, ('shard', 'help')), may hold values from -6 to 6
Outputs:
- sketch: float32 [32, 32768], P(None, ('shard', 'help'))
- regressor: float32 [32, 32, 768], P(('shard', 'help'))
The draws below stay inside these ranges and needn't reach their ends.
Inputs may be any that keep to these rules, and one draw needn't show every extreme that they name: `probe_group`: A query's 2 groups differ. Among the 256 queries of one device (aligned blocks of rows), at most 128 pairs (q,k) name one group, and in some blocks one group is named exactly 128 times.
All inputs are finite; a program needn't handle non-finite values.
Results may differ from the reference program's by a relative error of at most 0.0037.
Values may be sent and summed in bfloat16 or wider, within the bound.
No kernel may reach another device: no remote copies, remote signals or barrier semaphores. Data moves between devices by JAX's collectives and lax.ppermute only.
A program may use at most 64 MiB of HBM per device.

```python
import math
import jax
import jax.numpy as jnp
import numpy as np
from jax import lax

D = 768
R = 32
PROBES = 2
QDEV = 256
GROUPS = 8
GCL = 4
GPOINTS = 4096
CAP = 128
SEGMOST = 3072
QUERIES = 8192
POINTS = 32768


def with_ends(values, key, low, high):
    longest = values.shape.index(max(values.shape))
    spots = []
    for shift in (0, 1):
        where = [jax.random.randint(jax.random.fold_in(key, axis), (), 0, length) for axis, length in enumerate(values.shape)]
        where[longest] = (where[longest] + shift) % values.shape[longest]
        spots.append(tuple(where))
    return values.at[spots[0]].set(low).at[spots[1]].set(high)


def shard_levels(rng, extent, cuts, low, largest):
    def one(dim, parts):
        draws = jax.random.uniform(jax.random.fold_in(jax.random.fold_in(rng, 6), dim), (parts,), jnp.float32, low / len(cuts), largest / len(cuts))
        return jnp.repeat(jnp.exp(draws), extent[dim] // parts).reshape((-1,) + (1,) * (len(extent) - dim - 1))

    gain = one(*cuts[0])
    for cut in cuts[1:]:
        gain = gain * one(*cut)
    return gain


def rank_bounds(amount, slope):
    portions = [(1 << 20) // math.isqrt(grade ** slope) + 1 for grade in range(1, amount + 1)]
    spread = 1 + sum(portions) // (1 << 30)
    return np.cumsum(np.array([max(1, weight // spread) for weight in portions]))


def ranked(rng, dims, number_of, lean):
    listing = rank_bounds(number_of, lean)
    ticket = jax.random.randint(jax.random.fold_in(rng, 1), dims, 0, int(listing[number_of - 1]))
    standing = jnp.searchsorted(jnp.asarray(listing, jnp.int32), ticket, side="right")
    return jax.random.permutation(jax.random.fold_in(rng, 2), number_of)[standing].astype(jnp.int32)


def length_profile(amount, total, bound, lean):
    portions = [(1 << 20) // math.isqrt(standing ** lean) + 1 for standing in range(2, amount + 1)]
    surplus, counts = total - bound - (amount - 1), [1] * (amount - 1)
    while surplus > 0:
        candidates = [i for i in range(amount - 1) if counts[i] < bound]
        pool, remaining = sum([portions[i] for i in candidates]), surplus
        for i in candidates:
            more = min(bound - counts[i], max(1, remaining * portions[i] // pool), surplus)
            counts[i] = counts[i] + more
            surplus = surplus - more
    return np.array([bound] + counts)


def ragged(key, count, total, limit, lean):
    if count == 2:
        one = jax.random.randint(key, (), max(1, total - limit), min(limit, total - 1) + 1)
        return jnp.stack([one, total - one])
    lengths = jnp.asarray(length_profile(count, total, limit, lean), jnp.int32)
    twos = (count - 1) // 2
    source_of, sink = lengths[1:1 + 2 * twos:2], lengths[2:2 + 2 * twos:2]
    room = jnp.minimum(source_of - 1, limit - sink)
    passed = jax.random.randint(jax.random.fold_in(key, 1), (twos,), 0, 1 << 20) % (room + 1)
    lengths = lengths.at[1:1 + 2 * twos:2].set(source_of - passed).at[2:2 + 2 * twos:2].set(sink + passed)
    return lengths[jax.random.permutation(jax.random.fold_in(key, 2), count)]


def routed_block(key, own, number, rows, count, top, reach, slope):
    order = jax.random.permutation(key, count)
    heavy_load, usual = load_shares(count, rows * top, reach, slope, True), load_shares(count, rows * top, reach, slope, False)
    places = jnp.arange(count)

    def named(lengths, rotation):
        used = int((lengths > 0).sum())
        fixed = max(1, used // 4)
        moved = fixed + (places - fixed + rotation * (used - fixed)) % max(1, count - fixed)
        return jnp.zeros((count,), jnp.int32).at[order[jnp.where(places < fixed, places, moved)]].set(jnp.asarray(lengths, jnp.int32))

    lengths = jnp.where(number % 4 == 0, named(heavy_load, number // 4), named(usual, number - number // 4 - 1))
    mixed = jax.random.permutation(jax.random.fold_in(own, 3), count)
    donor, taker = mixed[0:count // 2 * 2:2], mixed[1:count // 2 * 2:2]
    slack = jnp.minimum(lengths[donor] - 1, reach - lengths[taker]) // 2
    slack = jnp.where((donor == order[0]) | (taker == order[0]) | (lengths[taker] == 0), 0, jnp.maximum(slack, 0))
    moved = jax.random.randint(jax.random.fold_in(own, 4), (count // 2,), 0, 1 << 20) % (slack + 1)
    lengths = lengths.at[donor].add(-moved).at[taker].add(moved)
    items = jnp.searchsorted(jnp.cumsum(lengths), jnp.arange(rows * top), side="right").astype(jnp.int32)
    grid = items.reshape(top, rows).T
    grid = grid[jax.random.permutation(jax.random.fold_in(own, 1), rows)]
    rotation = jax.random.randint(jax.random.fold_in(own, 2), (rows, 1), 0, top)
    return jnp.take_along_axis(grid, (jnp.arange(top)[None, :] + rotation) % top, axis=1)


def load_shares(count, total, most, skew, full):
    weights = [(1 << 20) // math.isqrt(grade ** skew) + 1 for grade in range(1, count + 1)]
    largest = most if full else min(most, max(-(-total // count), total * weights[0] // sum(weights)))
    least = 1 if total - largest >= count - 1 else 0
    given, surplus = [largest] + [least] * (count - 1), total - largest - least * (count - 1)
    while surplus > 0:
        candidates = [i for i in range(1, count) if given[i] < largest] or [i for i in range(1, count) if given[i] < most]
        mass, remaining = sum([weights[i] for i in candidates]), surplus
        for i in candidates:
            addition = min(most - given[i], max(1, remaining * weights[i] // mass), surplus)
            given[i] = given[i] + addition
            surplus = surplus - addition
    return np.array(given)


def centred(key, extent, scale, limit, split=(), kind=jnp.bfloat16):
    values = scale * jax.random.normal(key, extent, jnp.float32)
    if split:
        values = values * shard_levels(key, extent, split, -0.22, 0.18)
    return jnp.clip(values, -limit, limit).astype(kind)


def setup_inputs(seed: int = 0) -> dict:
    key_of = jax.random.split(jax.random.key(seed), 7)
    queries = centred(key_of[0], (QUERIES, D), 1.0, 6.0, ((0, 32),))
    probe_group_keys = jax.random.split(jax.random.fold_in(key_of[1], 1), QUERIES // QDEV)
    probe_group_turns = jax.random.permutation(jax.random.fold_in(key_of[1], 3), QUERIES // QDEV)
    probe_group = jax.vmap(lambda own, number: routed_block(jax.random.fold_in(key_of[1], 2), own, number, QDEV, GROUPS, PROBES, CAP, 2))(probe_group_keys, probe_group_turns).reshape((QUERIES, PROBES))
    probe_local = with_ends(ranked(key_of[2], (QUERIES, PROBES), GCL, 2), jax.random.fold_in(key_of[2], 3), 0, GCL - 1).astype(jnp.int32)
    points = centred(key_of[3], (POINTS, D), 1.0, 6.0, ((0, 32),))
    point_cluster = jax.vmap(lambda own: jnp.searchsorted(jnp.cumsum(ragged(own, GCL, GPOINTS, SEGMOST, 2)), jnp.arange(GPOINTS), side="right"))(jax.random.split(key_of[4], GROUPS)).reshape((GROUPS, GPOINTS)).astype(jnp.int32)
    test_matrix = centred(key_of[5], (R, POINTS), 1.0, 6.0, ((1, 32),))
    return {"queries": queries, "probe_group": probe_group, "probe_local": probe_local, "points": points, "point_cluster": point_cluster, "test_matrix": test_matrix}


def masked_scores(point_rows, point_ids, query_rows, query_ids):
    feature_width = point_rows.shape[1]
    block_rows = min(512, point_rows.shape[0])
    factor = feature_width ** (-0.5)

    def score_piece(pieces):
        piece_x, piece_ids = pieces
        product = lax.dot_general(piece_x, query_rows, (((1,), (1,)), ((), ())), preferred_element_type=jnp.float32) * factor
        return jnp.where(piece_ids[:, None] == query_ids[None, :], product, 0.0).astype(jnp.bfloat16)
    stacked = lax.map(score_piece, (point_rows.reshape(-1, block_rows, feature_width), point_ids.reshape(-1, block_rows)))
    return stacked.reshape(point_rows.shape[0], query_rows.shape[0])

def reference(queries, probe_group, probe_local, points, point_cluster, test_matrix):
    senders = QUERIES // QDEV
    per_sender = QDEV * PROBES
    target = probe_group.reshape(senders, per_sender)
    member = probe_local.reshape(-1)
    onehot_dest = (target[:, :, None] == jnp.arange(GROUPS, dtype=jnp.int32)[None, None, :]).astype(jnp.int32)
    ranking = lax.optimization_barrier(jnp.sum((jnp.cumsum(onehot_dest, axis=1).astype(jnp.int32) - onehot_dest) * onehot_dest, axis=2)).astype(jnp.int32)
    position = jnp.arange(senders, dtype=jnp.int32)[:, None] * CAP + ranking
    flat_index = jnp.arange(senders * per_sender, dtype=jnp.int32).reshape(senders, per_sender)
    slot_table = jnp.full((GROUPS, senders * CAP), -1, jnp.int32).at[target, position].set(flat_index)
    labels = jnp.arange(GCL, dtype=jnp.int32)

    def one_group(group_index):
        slot_index = slot_table[group_index]
        live_slot = slot_index >= 0
        safe_index = jnp.maximum(slot_index, 0)
        query_rows = jnp.where(live_slot[:, None], queries[safe_index // PROBES], jnp.zeros((), jnp.bfloat16))
        query_ids = jnp.where(live_slot, member[safe_index], -1)
        first_point = (group_index * GPOINTS).astype(jnp.int32)
        point_rows = lax.dynamic_slice_in_dim(points, first_point, GPOINTS, 0)
        point_ids = point_cluster[group_index]
        omega_rows = lax.dynamic_slice_in_dim(test_matrix, first_point, GPOINTS, 1)
        scores = masked_scores(point_rows, point_ids, query_rows, query_ids)
        lifted = jnp.dot(omega_rows, scores, preferred_element_type=jnp.float32).astype(jnp.bfloat16)
        product = lax.dot_general(lifted, scores, (((1,), (1,)), ((), ())), preferred_element_type=jnp.float32)
        query_hot = (query_ids[None, :] == labels[:, None]).astype(jnp.float32)
        point_hot = (point_ids[None, :] == labels[:, None]).astype(jnp.float32)
        queried = lax.optimization_barrier(jnp.sum(query_hot, axis=1))
        resident = lax.optimization_barrier(jnp.sum(point_hot, axis=1))
        factor = 1.0 / jnp.sqrt((queried + 1.0) * (queried + resident))
        sketch = product * lax.optimization_barrier(jnp.sum(factor[:, None] * point_hot, axis=0))[None, :]
        rounded = sketch.astype(jnp.bfloat16)
        weighted = (point_hot.astype(jnp.bfloat16)[:, None, :] * rounded[None, :, :]).reshape(GCL * R, GPOINTS)
        summed = jnp.dot(weighted, point_rows, preferred_element_type=jnp.float32).reshape(GCL, R, -1)
        regress = summed * (1.0 / jnp.sqrt(resident))[:, None, None]
        return (sketch, regress)
    sketches, regressors = lax.map(one_group, jnp.arange(GROUPS, dtype=jnp.int32))
    sketch_all = jnp.transpose(sketches, (1, 0, 2)).reshape(R, -1)
    return (sketch_all, regressors.reshape(-1, R, regressors.shape[3]))
```

```python
import functools

import jax
import jax.numpy as jnp
from jax import lax
from jax.experimental import pallas as pl
from jax.experimental.pallas import tpu as pltpu
from jax.sharding import PartitionSpec as P

F32 = jnp.float32
BF16 = jnp.bfloat16
LANES = 128
PARTIAL = BF16


def contract(a, b, dims):
    return lax.dot_general(a, b, (dims, ((), ())), preferred_element_type=F32)


def halves(value):
    high = value.astype(BF16)
    return high, (value - high.astype(F32)).astype(BF16)


def lift_kernel(helpers, ids_ref, test_ref, points_ref, own_ref, *send_refs):
    helper = lax.axis_index("help")
    count = points_ref.shape[0]
    ids = ids_ref[:, pl.ds(pl.multiple_of(helper * count, LANES), count)]
    test = test_ref[...]
    rows = [
        jnp.where(ids == (helper ^ d), test, jnp.zeros((), BF16)) for d in range(helpers)
    ]
    total = contract(jnp.concatenate(rows, axis=0), points_ref[...], ((1,), (0,)))
    rank = test.shape[0]
    own_ref[...] = total[:rank]
    for d in range(1, helpers):
        send_refs[d - 1][...] = total[d * rank : (d + 1) * rank].astype(send_refs[d - 1].dtype)


def score_kernel(groups, helpers, *refs):
    tests = refs[:groups]
    queries = refs[groups : groups + helpers]
    probes = refs[groups + helpers : groups + 2 * helpers]
    outs = refs[groups + 2 * helpers :]
    shard, helper = lax.axis_index("shard"), lax.axis_index("help")
    rank, width = tests[0].shape
    lifter = jnp.concatenate([t[...] for t in tests], axis=0)
    total = None
    tally = [None] * groups
    for q_ref, id_ref in zip(queries, probes):
        rows = q_ref[...]
        lifted = contract(lifter, rows, ((1,), (1,)))
        first, second = id_ref[0:1, :], id_ref[1:2, :]
        kept = []
        for d in range(groups):
            cluster = (shard ^ d) * helpers + helper
            hit = (first == cluster) | (second == cluster)
            kept.append(jnp.where(hit, lifted[d * rank : (d + 1) * rank], 0.0))
            here = jnp.sum(hit.astype(F32), axis=1, keepdims=True)
            tally[d] = here if tally[d] is None else tally[d] + here
        high, low = halves(jnp.concatenate(kept, axis=0))
        part = contract(high, rows, ((1,), (0,))) + contract(low, rows, ((1,), (0,)))
        total = part if total is None else total + part
    line = lax.broadcasted_iota(jnp.int32, (rank, LANES), 0)
    for d in range(groups):
        outs[d][:, :width] = total[d * rank : (d + 1) * rank].astype(BF16)
        many = jnp.floor(tally[d] * (1.0 / 256.0))
        rest = tally[d] - 256.0 * many
        outs[d][:, width:] = jnp.where(line == 0, many, jnp.where(line == 1, rest, 0.0)).astype(BF16)


def scale_kernel(groups, ids_ref, *refs):
    helper = lax.axis_index("help")
    parts, out_ref = refs[:groups], refs[groups]
    width = out_ref.shape[1]
    total = parts[0][...].astype(F32)
    for part in parts[1:]:
        total = total + part[...].astype(F32)
    queried = 256.0 * total[0:1, width : width + 1] + total[1:2, width : width + 1]
    resident = jnp.sum((ids_ref[...] == helper).astype(F32), axis=1, keepdims=True)
    factor = lax.rsqrt((queried + 1.0) * (queried + resident)) * (1.0 / width)
    out_ref[...] = (total[:, :width] * factor).astype(out_ref.dtype)


def sketch_kernel(helpers, ids_ref, points_ref, *refs):
    scaled = refs[:helpers]
    sketch_ref, own_ref, *send_refs = refs[helpers:]
    helper = lax.axis_index("help")
    count = points_ref.shape[0]
    rank = sketch_ref.shape[0]
    everyone = ids_ref[...]
    ids = ids_ref[:, pl.ds(pl.multiple_of(helper * count, LANES), count)]
    points = points_ref[...]
    product = contract(jnp.concatenate([s[...] for s in scaled], axis=0), points, ((1,), (1,)))
    sketch = jnp.zeros((rank, count), F32)
    for d in range(helpers):
        sketch = jnp.where(ids == (helper ^ d), product[d * rank : (d + 1) * rank], sketch)
    sketch_ref[...] = sketch
    rounded = sketch.astype(BF16)
    rows = [
        jnp.where(ids == (helper ^ d), rounded, jnp.zeros((), BF16)) for d in range(helpers)
    ]
    summed = contract(jnp.concatenate(rows, axis=0), points, ((1,), (0,)))
    for d in range(helpers):
        resident = jnp.sum((everyone == (helper ^ d)).astype(F32), axis=1, keepdims=True)
        block = summed[d * rank : (d + 1) * rank] * lax.rsqrt(resident)
        if d == 0:
            own_ref[...] = block
        else:
            send_refs[d - 1][...] = block.astype(send_refs[d - 1].dtype)


def swap(value, axis, d):
    size = lax.axis_size(axis)
    return lax.ppermute(value, axis, [(i, i ^ d) for i in range(size)])


def shards(queries, probe_group, probe_local, points, point_cluster, test_matrix):
    groups = lax.axis_size("shard")
    helpers = lax.axis_size("help")
    rank = test_matrix.shape[0]
    own_points, width = points.shape
    block = jax.ShapeDtypeStruct((rank, width), F32)
    sent = jax.ShapeDtypeStruct((rank, width), PARTIAL)
    params = pltpu.CompilerParams(vmem_limit_bytes=48 * 1024 * 1024)

    own, *out = pl.pallas_call(
        functools.partial(lift_kernel, helpers),
        out_shape=[block] + [sent] * (helpers - 1),
        compiler_params=params,
        name="lift",
    )(point_cluster, test_matrix, points)
    got = [swap(out[d - 1], "help", d) for d in range(1, helpers)]

    probes = (probe_group * helpers + probe_local).T
    peer_probes = [probes] + [swap(probes, "help", d) for d in range(1, helpers)]
    peer_rows = [queries] + [swap(queries, "help", d) for d in range(1, helpers)]

    lifter = own
    for part in got:
        lifter = lifter + part.astype(F32)
    lifter = lifter.astype(BF16)
    lifters = [lifter] + [swap(lifter, "shard", d) for d in range(1, groups)]

    moments = pl.pallas_call(
        functools.partial(score_kernel, groups, helpers),
        out_shape=[jax.ShapeDtypeStruct((rank, width + LANES), BF16)] * groups,
        compiler_params=params,
        name="score",
    )(*lifters, *peer_rows, *peer_probes)
    moments = [moments[0]] + [swap(moments[d], "shard", d) for d in range(1, groups)]

    scaled = pl.pallas_call(
        functools.partial(scale_kernel, groups),
        out_shape=jax.ShapeDtypeStruct((rank, width), BF16),
        compiler_params=params,
        name="scale",
    )(point_cluster, *moments)
    scaled = [scaled] + [swap(scaled, "help", d) for d in range(1, helpers)]

    sketch, own, *out = pl.pallas_call(
        functools.partial(sketch_kernel, helpers),
        out_shape=[jax.ShapeDtypeStruct((rank, own_points), F32), block] + [sent] * (helpers - 1),
        compiler_params=params,
        name="sketch",
    )(point_cluster, points, *scaled)
    regressor = own
    for d in range(1, helpers):
        regressor = regressor + swap(out[d - 1], "help", d).astype(F32)
    return sketch, regressor[None]


def solution(mesh):
    in_specs = (
        P(("shard", "help"), None),
        P(("shard", "help"), None),
        P(("shard", "help"), None),
        P(("shard", "help"), None),
        P("shard", None),
        P(None, ("shard", "help")),
    )
    out_specs = (P(None, ("shard", "help")), P(("shard", "help"), None, None))
    return jax.shard_map(shards, mesh=mesh, in_specs=in_specs, out_specs=out_specs, check_vma=False)
```

```python
import functools

import jax
import jax.numpy as jnp
from jax import lax
from jax.experimental import pallas as pl
from jax.experimental.pallas import tpu as pltpu
from jax.sharding import PartitionSpec as P

F32 = jnp.float32
BF16 = jnp.bfloat16
LANES = 128
TILE = 16
INNER = 2
CHUNKS = 4
FIRST = 60

HBM = pl.BlockSpec(memory_space=pltpu.HBM)
PARAMS = pltpu.CompilerParams(vmem_limit_bytes=32 * 1024 * 1024)


def contract(a, b, dims):
    return lax.dot_general(a, b, (dims, ((), ())), preferred_element_type=F32)


def halves(value):
    high = value.astype(BF16)
    return high, (value - high.astype(F32)).astype(BF16)


def lift_kernel(helpers, rows_hbm, group_hbm, local_hbm, ids_hbm, test_hbm, points_hbm, packed_ref, own_ref, *refs):
    send_refs = refs[: helpers - 1]
    mark_ref, resident_ref, group_ref, local_ref, ids_ref, test_ref, points_ref, sems = refs[helpers - 1 :]
    helper = lax.axis_index("help")
    asked, width = rows_hbm.shape
    rank, count = test_ref.shape
    piece = count // CHUNKS
    pairs = [(ids_hbm, ids_ref), (test_hbm, test_ref)]
    for k in range(CHUNKS):
        part = pl.ds(k * piece, piece)
        pairs.append((points_hbm.at[part], points_ref.at[part]))
    pairs += [(group_hbm, group_ref), (local_hbm, local_ref), (rows_hbm, packed_ref.at[pl.ds(0, asked)])]
    copies = [pltpu.make_async_copy(*pair, sems.at[k]) for k, pair in enumerate(pairs)]
    for copy in copies:
        copy.start()
    copies[0].wait()
    everyone = ids_ref[...]
    mark = ids_ref[:, pl.ds(pl.multiple_of(helper * count, LANES), count)] ^ helper
    mark_ref[...] = mark
    for d in range(helpers):
        many = jnp.sum((everyone == (helper ^ d)).astype(F32), axis=1, keepdims=True)
        resident_ref[d : d + 1, :] = jnp.broadcast_to(many, (1, LANES))
    copies[1].wait()
    test = test_ref[...]
    rows = jnp.concatenate([jnp.where(mark == d, test, jnp.zeros((), BF16)) for d in range(helpers)], axis=0)
    total = None
    for k in range(CHUNKS):
        copies[2 + k].wait()
        part = slice(k * piece, (k + 1) * piece)
        more = contract(rows[:, part], points_ref[part, :], ((1,), (0,)))
        total = more if total is None else total + more
    own_ref[...] = total[:rank]
    for d in range(1, helpers):
        send_refs[d - 1][...] = total[d * rank : (d + 1) * rank].astype(BF16)
    copies[-3].wait()
    copies[-2].wait()
    cluster = (group_ref[...] * helpers + local_ref[...]).astype(F32)
    spare = jnp.zeros((1, width - 2 * asked), F32)
    line = jnp.concatenate([cluster[0:1], cluster[1:2], spare], axis=1)
    packed_ref[asked:, :] = jnp.broadcast_to(line, (TILE, width)).astype(BF16)
    copies[-1].wait()


def score_kernel(planes, helpers, blocks, mine_ref, theirs_ref, *refs):
    queries, rest = refs[:blocks], refs[blocks:]
    shard, helper = lax.axis_index("shard"), lax.axis_index("help")
    span, width = mine_ref.shape
    rank = span // planes
    count = queries[0].shape[0] - TILE
    lifter = jnp.concatenate([mine_ref[...], theirs_ref[...]], axis=0)
    clusters = [
        ((shard ^ (INNER * d)) * helpers + (helper ^ side)).astype(F32) for side in (0, 1) for d in range(planes)
    ]
    total, tally = None, [None] * len(clusters)
    for q_ref in queries:
        rows = q_ref[:count, :]
        line = q_ref[count : count + TILE, :][0:1].astype(F32)
        first, second = line[:, :count], line[:, count : 2 * count]
        lifted = contract(lifter, rows, ((1,), (1,)))
        kept = []
        for k, cluster in enumerate(clusters):
            hit = (first == cluster) | (second == cluster)
            kept.append(jnp.where(hit, lifted[k * rank : (k + 1) * rank], 0.0))
            here = hit.astype(F32)
            tally[k] = here if tally[k] is None else tally[k] + here
        high, low = halves(jnp.concatenate(kept, axis=0))
        part = contract(high, rows, ((1,), (0,))) + contract(low, rows, ((1,), (0,)))
        total = part if total is None else total + part
    named = jnp.concatenate(
        [jnp.broadcast_to(jnp.sum(t, axis=1, keepdims=True), (rank, LANES)) for t in tally], axis=0
    )
    if len(rest) == 1:
        rest[0][:, :width] = total
        rest[0][:, width:] = named
    else:
        before, *outs = rest
        for side, out in enumerate(outs):
            part = slice(side * span, (side + 1) * span)
            out[:, :width] = before[part, :width] + total[part]
            out[:, width:] = before[part, width:] + named[part]


def fold_kernel(planes, mine_ref, theirs_ref, own_ref, *send_refs):
    rank, wide = own_ref.shape
    width = wide - LANES
    line = lax.broadcasted_iota(jnp.int32, (rank, LANES), 0)
    for d in range(planes):
        part = slice(d * rank, (d + 1) * rank)
        total = mine_ref[part, :] + theirs_ref[part, :]
        if d == 0:
            own_ref[...] = total
        else:
            many = jnp.floor(total[:, width:] * (1.0 / 256.0))
            rest = total[:, width:] - 256.0 * many
            send_refs[d - 1][:, :width] = total[:, :width].astype(BF16)
            send_refs[d - 1][:, width:] = jnp.where(line == 0, many, jnp.where(line == 1, rest, 0.0)).astype(BF16)


def scale_kernel(resident_ref, own_ref, *refs):
    *parts, out_ref = refs
    width = out_ref.shape[1]
    total = own_ref[:, :width]
    queried = own_ref[0:1, width : width + 1]
    for part in parts:
        total = total + part[:, :width].astype(F32)
        tile = part[:, width:].astype(F32)
        queried = queried + 256.0 * tile[0:1, 0:1] + tile[1:2, 0:1]
    resident = resident_ref[0:1, 0:1]
    factor = lax.rsqrt((queried + 1.0) * (queried + resident)) * (1.0 / width)
    out_ref[...] = (total * factor).astype(out_ref.dtype)


def sketch_kernel(helpers, mark_ref, resident_ref, points_ref, *refs):
    scaled = refs[:helpers]
    sketch_ref, own_ref, *send_refs = refs[helpers:]
    rank, count = sketch_ref.shape
    mark = mark_ref[...]
    points = points_ref[...]
    product = contract(jnp.concatenate([s[...] for s in scaled], axis=0), points, ((1,), (1,)))
    sketch = product[:rank]
    for d in range(1, helpers):
        sketch = jnp.where(mark == d, product[d * rank : (d + 1) * rank], sketch)
    sketch_ref[...] = sketch
    rounded = sketch.astype(BF16)
    rows = [jnp.where(mark == d, rounded, jnp.zeros((), BF16)) for d in range(helpers)]
    summed = contract(jnp.concatenate(rows, axis=0), points, ((1,), (0,)))
    for d in range(helpers):
        block = summed[d * rank : (d + 1) * rank] * lax.rsqrt(resident_ref[d : d + 1, 0:1])
        if d == 0:
            own_ref[...] = block
        else:
            send_refs[d - 1][...] = block.astype(BF16)


def swap(value, axis, d):
    return lax.ppermute(value, axis, [(i, i ^ d) for i in range(lax.axis_size(axis))])


def pool_queries(packed, lifter, groups, helpers):
    index = range(groups * helpers)
    one = [(i, i ^ (2 if i % 2 == 0 else helpers)) for i in index]
    two = [(i, i ^ (helpers if i % 2 == 0 else 2)) for i in index]
    both = ("shard", "help")
    near = lax.ppermute(packed, both, one)
    far = lax.ppermute(packed, both, two)
    near, far, _ = lax.optimization_barrier((near, far, lifter))
    return near, far, lax.ppermute(near, both, two)


def shards(queries, probe_group, probe_local, points, point_cluster, test_matrix):
    groups = lax.axis_size("shard")
    helpers = lax.axis_size("help")
    planes = groups // INNER
    count = queries.shape[0]
    rank = test_matrix.shape[0]
    own_points, width = points.shape
    block = jax.ShapeDtypeStruct((rank, width), F32)
    sent = jax.ShapeDtypeStruct((rank, width), BF16)

    packed, own, *out, mark, resident = pl.pallas_call(
        functools.partial(lift_kernel, helpers),
        out_shape=[jax.ShapeDtypeStruct((count + TILE, width), BF16), block]
        + [sent] * (helpers - 1)
        + [jax.ShapeDtypeStruct((1, own_points), jnp.int32), jax.ShapeDtypeStruct((8, LANES), F32)],
        in_specs=[HBM] * 6,
        scratch_shapes=[
            pltpu.VMEM((2, count), jnp.int32),
            pltpu.VMEM((2, count), jnp.int32),
            pltpu.VMEM(point_cluster.shape, jnp.int32),
            pltpu.VMEM(test_matrix.shape, BF16),
            pltpu.VMEM(points.shape, BF16),
            pltpu.SemaphoreType.DMA((5 + CHUNKS,)),
        ],
        compiler_params=pltpu.CompilerParams(vmem_limit_bytes=FIRST << 20),
        name="lift",
    )(queries, probe_group.T, probe_local.T, point_cluster, test_matrix, points)
    lifter = own
    for d in range(1, helpers):
        lifter = lifter + swap(out[d - 1], "help", d).astype(F32)
    lifter = lifter.astype(BF16)
    lifters = [lifter] + [swap(lifter, "shard", INNER * d) for d in range(1, planes)]
    near, far, across = pool_queries(packed, lifters[1], groups, helpers)
    mine = jnp.concatenate(lifters, axis=0)
    theirs = swap(mine, "help", 1)

    wide = width + LANES
    begun = pl.pallas_call(
        functools.partial(score_kernel, planes, helpers, 3),
        out_shape=jax.ShapeDtypeStruct((2 * planes * rank, wide), F32),
        compiler_params=PARAMS,
        name="score",
    )(mine, theirs, packed, near, far)
    moments, passed = pl.pallas_call(
        functools.partial(score_kernel, planes, helpers, 1),
        out_shape=[jax.ShapeDtypeStruct((planes * rank, wide), F32)] * 2,
        compiler_params=PARAMS,
        name="score_last",
    )(mine, theirs, across, begun)
    folded = pl.pallas_call(
        functools.partial(fold_kernel, planes),
        out_shape=[jax.ShapeDtypeStruct((rank, wide), F32)]
        + [jax.ShapeDtypeStruct((rank, wide), BF16)] * (planes - 1),
        compiler_params=PARAMS,
        name="fold",
    )(moments, swap(passed, "help", 1))
    moments = [folded[0]] + [swap(folded[d], "shard", INNER * d) for d in range(1, planes)]

    scaled = pl.pallas_call(
        scale_kernel,
        out_shape=sent,
        compiler_params=PARAMS,
        name="scale",
    )(resident, *moments)
    scaled = [scaled] + [swap(scaled, "help", d) for d in range(1, helpers)]

    sketch, own, *out = pl.pallas_call(
        functools.partial(sketch_kernel, helpers),
        out_shape=[jax.ShapeDtypeStruct((rank, own_points), F32), block] + [sent] * (helpers - 1),
        compiler_params=PARAMS,
        name="sketch",
    )(mark, resident, points, *scaled)
    regressor = own
    for d in range(1, helpers):
        regressor = regressor + swap(out[d - 1], "help", d).astype(F32)
    return sketch, regressor[None]


def solution(mesh):
    in_specs = (
        P(("shard", "help"), None),
        P(("shard", "help"), None),
        P(("shard", "help"), None),
        P(("shard", "help"), None),
        P("shard", None),
        P(None, ("shard", "help")),
    )
    out_specs = (P(None, ("shard", "help")), P(("shard", "help"), None, None))
    return jax.shard_map(shards, mesh=mesh, in_specs=in_specs, out_specs=out_specs, check_vma=False)
```

```python
import functools

import jax
import jax.numpy as jnp
from jax import lax
from jax.experimental import pallas as pl
from jax.experimental.pallas import tpu as pltpu
from jax.sharding import PartitionSpec as P

F32 = jnp.float32
BF16 = jnp.bfloat16
LANES = 128
TILE = 16
INNER = 2
CHUNKS = 4
FIRST = 60

ANY = pl.BlockSpec(memory_space=pl.ANY)
HBM = pl.BlockSpec(memory_space=pltpu.HBM)
PARAMS = pltpu.CompilerParams(vmem_limit_bytes=32 * 1024 * 1024)


def contract(a, b, dims):
    return lax.dot_general(a, b, (dims, ((), ())), preferred_element_type=F32)


def halves(value):
    high = value.astype(BF16)
    return high, (value - high.astype(F32)).astype(BF16)


def slabs(ref, rows, width):
    return jnp.concatenate([ref[k * rows : (k + 1) * rows, :] for k in range(width // LANES)], axis=1)


def order(helpers):
    return [*range(0, helpers, 2), *range(1, helpers, 2)]


def lift_kernel(helpers, *refs):
    rows_hbm, group_hbm, local_hbm, ids_hbm, test_hbm, points_hbm = refs[:6]
    packed_ref, keep_ref, pass_ref, mark_ref, resident_ref = refs[6:11]
    group_ref, local_ref, ids_ref, test_ref, points_ref, sems = refs[11:]
    helper = lax.axis_index("help")
    asked, width = rows_hbm.shape
    rank, count = test_ref.shape
    piece = count // CHUNKS
    pairs = [(ids_hbm, ids_ref), (test_hbm, test_ref)]
    for k in range(CHUNKS):
        part = pl.ds(k * piece, piece)
        pairs.append((points_hbm.at[part], points_ref.at[part]))
    pairs += [(group_hbm, group_ref), (local_hbm, local_ref)]
    for k in range(width // LANES):
        pairs.append((rows_hbm.at[:, pl.ds(k * LANES, LANES)], packed_ref.at[pl.ds(k * asked, asked)]))
    copies = [pltpu.make_async_copy(*pair, sems.at[k]) for k, pair in enumerate(pairs)]
    for copy in copies:
        copy.start()
    copies[0].wait()
    everyone = ids_ref[...]
    mark = ids_ref[:, pl.ds(pl.multiple_of(helper * count, LANES), count)] ^ helper
    mark_ref[...] = mark
    for d in range(helpers):
        many = jnp.sum((everyone == (helper ^ d)).astype(F32), axis=1, keepdims=True)
        resident_ref[d : d + 1, :] = jnp.broadcast_to(many, (1, LANES))
    copies[1].wait()
    test = test_ref[...]
    offsets = order(helpers)
    rows = jnp.concatenate([jnp.where(mark == d, test, jnp.zeros((), BF16)) for d in offsets], axis=0)
    total = None
    for k in range(CHUNKS):
        copies[2 + k].wait()
        part = slice(k * piece, (k + 1) * piece)
        more = contract(rows[:, part], points_ref[part, :], ((1,), (0,)))
        total = more if total is None else total + more
    keep_ref[...] = total[: keep_ref.shape[0]]
    pass_ref[...] = total[keep_ref.shape[0] :]
    for copy in copies[2 + CHUNKS :]:
        copy.wait()
    cluster = (group_ref[...] * helpers + local_ref[...]).astype(F32)
    line = [cluster[k : k + 1, j : j + LANES] for k in (0, 1) for j in range(0, asked, LANES)]
    line.append(jnp.zeros((TILE - len(line), LANES), F32))
    packed_ref[asked * width // LANES :, :] = jnp.concatenate(line, axis=0).astype(BF16)


def gate_kernel(*refs):
    pass


def gate(value, *others):
    return pl.pallas_call(
        gate_kernel,
        out_shape=jax.ShapeDtypeStruct(value.shape, value.dtype),
        in_specs=[ANY] * (1 + len(others)),
        out_specs=ANY,
        input_output_aliases={0: 0},
        cost_estimate=pl.CostEstimate(flops=10**10, bytes_accessed=10**7, transcendentals=0),
        name="gate",
    )(value, *others)


def score_kernel(planes, helpers, blocks, mine_ref, theirs_ref, *refs):
    queries, rest = refs[:blocks], refs[blocks:]
    shard, helper = lax.axis_index("shard"), lax.axis_index("help")
    span, width = mine_ref.shape
    rank = span // planes
    count = (queries[0].shape[0] - TILE) * LANES // width
    pieces = count // LANES
    lifter = jnp.concatenate([mine_ref[...], theirs_ref[...]], axis=0)
    clusters = [
        ((shard ^ (INNER * d)) * helpers + (helper ^ side)).astype(F32) for side in (0, 1) for d in range(planes)
    ]
    total, tally = None, [None] * len(clusters)
    for q_ref in queries:
        rows = slabs(q_ref, count, width)
        tile = q_ref[count * width // LANES :, :].astype(F32)
        first, second = (
            jnp.concatenate([tile[k * pieces + j : k * pieces + j + 1] for j in range(pieces)], axis=1) for k in (0, 1)
        )
        lifted = contract(lifter, rows, ((1,), (1,)))
        kept = []
        for k, cluster in enumerate(clusters):
            hit = (first == cluster) | (second == cluster)
            kept.append(jnp.where(hit, lifted[k * rank : (k + 1) * rank], 0.0))
            here = hit.astype(F32)
            tally[k] = here if tally[k] is None else tally[k] + here
        high, low = halves(jnp.concatenate(kept, axis=0))
        part = contract(high, rows, ((1,), (0,))) + contract(low, rows, ((1,), (0,)))
        total = part if total is None else total + part
    named = jnp.concatenate(
        [jnp.broadcast_to(jnp.sum(t, axis=1, keepdims=True), (rank, LANES)) for t in tally], axis=0
    )
    if len(rest) == 1:
        rest[0][:, :width] = total
        rest[0][:, width:] = named
    else:
        before, *outs = rest
        for side, out in enumerate(outs):
            part = slice(side * span, (side + 1) * span)
            out[:, :width] = before[part, :width] + total[part]
            out[:, width:] = before[part, width:] + named[part]


def fold_kernel(planes, mine_ref, theirs_ref, own_ref, *send_refs):
    rank, wide = own_ref.shape
    width = wide - LANES
    line = lax.broadcasted_iota(jnp.int32, (TILE, LANES), 0)
    for d in range(planes):
        part = slice(d * rank, (d + 1) * rank)
        total = mine_ref[part, :] + theirs_ref[part, :]
        if d == 0:
            own_ref[...] = total
        else:
            ref = send_refs[d - 1]
            for k in range(width // LANES):
                ref[k * rank : (k + 1) * rank, :] = total[:, k * LANES : (k + 1) * LANES].astype(BF16)
            named = total[:TILE, width:]
            many = jnp.floor(named * (1.0 / 256.0))
            rest = named - 256.0 * many
            ref[rank * width // LANES :, :] = jnp.where(line == 0, many, jnp.where(line == 1, rest, 0.0)).astype(BF16)


def scale_kernel(resident_ref, own_ref, *refs):
    *parts, out_ref = refs
    rank, width = out_ref.shape
    total = own_ref[:, :width]
    queried = own_ref[0:1, width : width + 1]
    for part in parts:
        total = total + slabs(part, rank, width).astype(F32)
        tile = part[rank * width // LANES :, :].astype(F32)
        queried = queried + 256.0 * tile[0:1, 0:1] + tile[1:2, 0:1]
    resident = resident_ref[0:1, 0:1]
    factor = lax.rsqrt((queried + 1.0) * (queried + resident)) * (1.0 / width)
    out_ref[...] = (total * factor).astype(out_ref.dtype)


def sketch_kernel(helpers, mark_ref, resident_ref, points_ref, mine_ref, theirs_ref, sketch_ref, keep_ref, pass_ref):
    rank, count = sketch_ref.shape
    offsets = order(helpers)
    mark = mark_ref[...]
    points = points_ref[...]
    product = contract(jnp.concatenate([mine_ref[...], theirs_ref[...]], axis=0), points, ((1,), (1,)))
    sketch = product[:rank]
    for k, d in enumerate(offsets[1:], 1):
        sketch = jnp.where(mark == d, product[k * rank : (k + 1) * rank], sketch)
    sketch_ref[...] = sketch
    rounded = sketch.astype(BF16)
    rows = [jnp.where(mark == d, rounded, jnp.zeros((), BF16)) for d in offsets]
    summed = contract(jnp.concatenate(rows, axis=0), points, ((1,), (0,)))
    blocks = [
        summed[k * rank : (k + 1) * rank] * lax.rsqrt(resident_ref[d : d + 1, 0:1]) for k, d in enumerate(offsets)
    ]
    kept = helpers // 2
    keep_ref[...] = jnp.concatenate(blocks[:kept], axis=0)
    pass_ref[...] = jnp.concatenate(blocks[kept:], axis=0)


def swap(value, axis, d):
    return lax.ppermute(value, axis, [(i, i ^ d) for i in range(lax.axis_size(axis))])


def gather_to_owner(keep, passed, rank, helpers):
    both = keep + swap(passed, "help", 1)
    blocks = [both[k * rank : (k + 1) * rank] for k in range(helpers // 2)]
    sent = [block.astype(BF16) for block in blocks[1:]]
    return blocks[0], [swap(block, "help", 2 * k) for k, block in enumerate(sent, 1)], sent


def shards(queries, probe_group, probe_local, points, point_cluster, test_matrix):
    groups = lax.axis_size("shard")
    helpers = lax.axis_size("help")
    planes = groups // INNER
    count = queries.shape[0]
    rank = test_matrix.shape[0]
    own_points, width = points.shape
    kept = jax.ShapeDtypeStruct((helpers // 2 * rank, width), F32)

    packed, keep, passed, mark, resident = pl.pallas_call(
        functools.partial(lift_kernel, helpers),
        out_shape=[
            jax.ShapeDtypeStruct((count * width // LANES + TILE, LANES), BF16),
            kept,
            kept,
            jax.ShapeDtypeStruct((1, own_points), jnp.int32),
            jax.ShapeDtypeStruct((8, LANES), F32),
        ],
        in_specs=[HBM] * 6,
        scratch_shapes=[
            pltpu.VMEM((2, count), jnp.int32),
            pltpu.VMEM((2, count), jnp.int32),
            pltpu.VMEM(point_cluster.shape, jnp.int32),
            pltpu.VMEM(test_matrix.shape, BF16),
            pltpu.VMEM(points.shape, BF16),
            pltpu.SemaphoreType.DMA((4 + CHUNKS + width // LANES,)),
        ],
        compiler_params=pltpu.CompilerParams(vmem_limit_bytes=FIRST << 20),
        name="lift",
    )(queries, probe_group.T, probe_local.T, point_cluster, test_matrix, points)
    own, others, leaving = gather_to_owner(keep, passed, rank, helpers)

    index, axes = range(groups * helpers), ("shard", "help")
    one = [(i, i ^ (2 if i % 2 == 0 else helpers)) for i in index]
    two = [(i, i ^ (helpers if i % 2 == 0 else 2)) for i in index]
    packed = gate(packed, *leaving)
    near = lax.ppermute(packed, axes, one)
    far = lax.ppermute(packed, axes, two)

    for part in others:
        own = own + part.astype(F32)
    lifter = own.astype(BF16)
    lifters = [lifter] + [swap(lifter, "shard", INNER * d) for d in range(1, planes)]
    near = gate(near, lifter)
    across = lax.ppermute(near, axes, two)
    mine = jnp.concatenate(lifters, axis=0)
    theirs = swap(mine, "help", 1)

    wide = width + LANES
    begun = pl.pallas_call(
        functools.partial(score_kernel, planes, helpers, 3),
        out_shape=jax.ShapeDtypeStruct((2 * planes * rank, wide), F32),
        compiler_params=PARAMS,
        name="score",
    )(mine, theirs, packed, near, far)
    moments, passed = pl.pallas_call(
        functools.partial(score_kernel, planes, helpers, 1),
        out_shape=[jax.ShapeDtypeStruct((planes * rank, wide), F32)] * 2,
        compiler_params=PARAMS,
        name="score_last",
    )(mine, theirs, across, begun)
    folded = pl.pallas_call(
        functools.partial(fold_kernel, planes),
        out_shape=[jax.ShapeDtypeStruct((rank, wide), F32)]
        + [jax.ShapeDtypeStruct((rank * width // LANES + TILE, LANES), BF16)] * (planes - 1),
        compiler_params=PARAMS,
        name="fold",
    )(moments, swap(passed, "help", 1))
    moments = [folded[0]] + [swap(folded[d], "shard", INNER * d) for d in range(1, planes)]

    scaled = pl.pallas_call(
        scale_kernel,
        out_shape=jax.ShapeDtypeStruct((rank, width), BF16),
        compiler_params=PARAMS,
        name="scale",
    )(resident, *moments)
    scaled = jnp.concatenate([scaled] + [swap(scaled, "help", d) for d in range(2, helpers, 2)], axis=0)

    sketch, keep, passed = pl.pallas_call(
        functools.partial(sketch_kernel, helpers),
        out_shape=[jax.ShapeDtypeStruct((rank, own_points), F32), kept, kept],
        compiler_params=PARAMS,
        name="sketch",
    )(mark, resident, points, scaled, swap(scaled, "help", 1))
    regressor, others, _ = gather_to_owner(keep, passed, rank, helpers)
    for part in others:
        regressor = regressor + part.astype(F32)
    return sketch, regressor[None]


def solution(mesh):
    in_specs = (
        P(("shard", "help"), None),
        P(("shard", "help"), None),
        P(("shard", "help"), None),
        P(("shard", "help"), None),
        P("shard", None),
        P(None, ("shard", "help")),
    )
    out_specs = (P(None, ("shard", "help")), P(("shard", "help"), None, None))
    return jax.shard_map(shards, mesh=mesh, in_specs=in_specs, out_specs=out_specs, check_vma=False)
```

```python
import functools

import jax
import jax.numpy as jnp
from jax import lax
from jax.experimental import pallas as pl
from jax.experimental.pallas import tpu as pltpu
from jax.sharding import PartitionSpec as P

F32 = jnp.float32
BF16 = jnp.bfloat16
LANES = 128
TILE = 16
CHUNKS = 4
INNER = 2
FIRST = 60

ANY = pl.BlockSpec(memory_space=pl.ANY)
VMEM = pl.BlockSpec(memory_space=pltpu.VMEM)
HBM = pl.BlockSpec(memory_space=pltpu.HBM)
PARAMS = pltpu.CompilerParams(vmem_limit_bytes=32 * 1024 * 1024)


def contract(a, b, dims):
    return lax.dot_general(a, b, (dims, ((), ())), preferred_element_type=F32)


def halves(value):
    high = value.astype(BF16)
    return high, (value - high.astype(F32)).astype(BF16)


def slabs(ref, rows, width):
    return jnp.concatenate([ref[k * rows : (k + 1) * rows, :] for k in range(width // LANES)], axis=1)


def order(helpers):
    return [*range(0, helpers, 2), *range(1, helpers, 2)]


def lift_kernel(helpers, *refs):
    rows_hbm, group_hbm, local_hbm, ids_hbm, test_hbm, points_hbm = refs[:6]
    packed_ref, keep_ref, pass_ref, mark_ref, resident_ref = refs[6:11]
    group_ref, local_ref, ids_ref, test_ref, points_ref, sems = refs[11:]
    helper = lax.axis_index("help")
    asked, width = rows_hbm.shape
    rank, count = test_ref.shape
    piece = count // CHUNKS
    pairs = [(ids_hbm, ids_ref), (test_hbm, test_ref)]
    for k in range(CHUNKS):
        part = pl.ds(k * piece, piece)
        pairs.append((points_hbm.at[part], points_ref.at[part]))
    pairs += [(group_hbm, group_ref), (local_hbm, local_ref)]
    for k in range(width // LANES):
        pairs.append((rows_hbm.at[:, pl.ds(k * LANES, LANES)], packed_ref.at[pl.ds(k * asked, asked)]))
    copies = [pltpu.make_async_copy(*pair, sems.at[k]) for k, pair in enumerate(pairs)]
    for copy in copies:
        copy.start()
    copies[0].wait()
    everyone = ids_ref[...]
    mark = ids_ref[:, pl.ds(pl.multiple_of(helper * count, LANES), count)] ^ helper
    mark_ref[...] = mark
    for d in range(helpers):
        many = jnp.sum((everyone == (helper ^ d)).astype(F32), axis=1, keepdims=True)
        resident_ref[d : d + 1, :] = jnp.broadcast_to(many, (1, LANES))
    copies[1].wait()
    test = test_ref[...]
    offsets = order(helpers)
    rows = jnp.concatenate([jnp.where(mark == d, test, jnp.zeros((), BF16)) for d in offsets], axis=0)
    total = None
    for k in range(CHUNKS):
        copies[2 + k].wait()
        part = slice(k * piece, (k + 1) * piece)
        more = contract(rows[:, part], points_ref[part, :], ((1,), (0,)))
        total = more if total is None else total + more
    keep_ref[...] = total[: keep_ref.shape[0]]
    pass_ref[...] = total[keep_ref.shape[0] :]
    for copy in copies[2 + CHUNKS :]:
        copy.wait()
    cluster = (group_ref[...] * helpers + local_ref[...]).astype(F32)
    line = [cluster[k : k + 1, j : j + LANES] for k in (0, 1) for j in range(0, asked, LANES)]
    line.append(jnp.zeros((TILE - len(line), LANES), F32))
    packed_ref[asked * width // LANES :, :] = jnp.concatenate(line, axis=0).astype(BF16)


def join_kernel(keep_ref, got_ref, own_ref, *send_refs):
    rank = own_ref.shape[0]
    own_ref[...] = keep_ref[:rank, :] + got_ref[:rank, :]
    for k, ref in enumerate(send_refs, 1):
        part = slice(k * rank, (k + 1) * rank)
        ref[...] = (keep_ref[part, :] + got_ref[part, :]).astype(BF16)


def gate_kernel(*refs):
    pass


def gate(value, *others):
    return pl.pallas_call(
        gate_kernel,
        out_shape=jax.ShapeDtypeStruct(value.shape, value.dtype),
        in_specs=[ANY] * (1 + len(others)),
        out_specs=ANY,
        input_output_aliases={0: 0},
        cost_estimate=pl.CostEstimate(flops=10**10, bytes_accessed=10**7, transcendentals=0),
        name="gate",
    )(value, *others)


def score_kernel(planes, helpers, blocks, mine_ref, theirs_ref, *refs):
    queries, rest = refs[:blocks], refs[blocks:]
    shard, helper = lax.axis_index("shard"), lax.axis_index("help")
    span, width = mine_ref.shape
    rank = span // planes
    count = (queries[0].shape[0] - TILE) * LANES // width
    pieces = count // LANES
    lifter = jnp.concatenate([mine_ref[...], theirs_ref[...]], axis=0)
    clusters = [
        ((shard ^ (INNER * d)) * helpers + (helper ^ side)).astype(F32) for side in (0, 1) for d in range(planes)
    ]
    total, tally = None, [None] * len(clusters)
    for q_ref in queries:
        rows = slabs(q_ref, count, width)
        tile = q_ref[count * width // LANES :, :].astype(F32)
        first, second = (
            jnp.concatenate([tile[k * pieces + j : k * pieces + j + 1] for j in range(pieces)], axis=1) for k in (0, 1)
        )
        lifted = contract(lifter, rows, ((1,), (1,)))
        kept = []
        for k, cluster in enumerate(clusters):
            hit = (first == cluster) | (second == cluster)
            kept.append(jnp.where(hit, lifted[k * rank : (k + 1) * rank], 0.0))
            here = hit.astype(F32)
            tally[k] = here if tally[k] is None else tally[k] + here
        high, low = halves(jnp.concatenate(kept, axis=0))
        part = contract(high, rows, ((1,), (0,))) + contract(low, rows, ((1,), (0,)))
        total = part if total is None else total + part
    named = jnp.concatenate(
        [jnp.broadcast_to(jnp.sum(t, axis=1, keepdims=True), (rank, LANES)) for t in tally], axis=0
    )
    if len(rest) == 1:
        rest[0][:, :width] = total
        rest[0][:, width:] = named
    else:
        before, *outs = rest
        for side, out in enumerate(outs):
            part = slice(side * span, (side + 1) * span)
            out[:, :width] = before[part, :width] + total[part]
            out[:, width:] = before[part, width:] + named[part]


def fold_kernel(planes, mine_ref, theirs_ref, own_ref, *send_refs):
    rank, wide = own_ref.shape
    width = wide - LANES
    line = lax.broadcasted_iota(jnp.int32, (TILE, LANES), 0)
    for d in range(planes):
        part = slice(d * rank, (d + 1) * rank)
        total = mine_ref[part, :] + theirs_ref[part, :]
        if d == 0:
            own_ref[...] = total
        else:
            ref = send_refs[d - 1]
            for k in range(width // LANES):
                ref[k * rank : (k + 1) * rank, :] = total[:, k * LANES : (k + 1) * LANES].astype(BF16)
            named = total[:TILE, width:]
            many = jnp.floor(named * (1.0 / 256.0))
            rest = named - 256.0 * many
            ref[rank * width // LANES :, :] = jnp.where(line == 0, many, jnp.where(line == 1, rest, 0.0)).astype(BF16)


def scale_kernel(resident_ref, own_ref, *refs):
    *parts, out_ref = refs
    rank, width = out_ref.shape
    total = own_ref[:, :width]
    queried = own_ref[0:1, width : width + 1]
    for part in parts:
        total = total + slabs(part, rank, width).astype(F32)
        tile = part[rank * width // LANES :, :].astype(F32)
        queried = queried + 256.0 * tile[0:1, 0:1] + tile[1:2, 0:1]
    resident = resident_ref[0:1, 0:1]
    factor = lax.rsqrt((queried + 1.0) * (queried + resident)) * (1.0 / width)
    out_ref[...] = (total * factor).astype(out_ref.dtype)


def sketch_kernel(helpers, mark_ref, resident_ref, points_ref, *refs):
    scaled, sketch_ref, outs = refs[:helpers], refs[helpers], refs[helpers + 1 :]
    rank, count = sketch_ref.shape
    mark = mark_ref[...]
    points = points_ref[...]
    product = contract(jnp.concatenate([s[...] for s in scaled], axis=0), points, ((1,), (1,)))
    sketch = product[:rank]
    for d in range(1, helpers):
        sketch = jnp.where(mark == d, product[d * rank : (d + 1) * rank], sketch)
    sketch_ref[...] = sketch
    rounded = sketch.astype(BF16)
    rows = [jnp.where(mark == d, rounded, jnp.zeros((), BF16)) for d in range(helpers)]
    summed = contract(jnp.concatenate(rows, axis=0), points, ((1,), (0,)))
    for d, out in enumerate(outs):
        block = summed[d * rank : (d + 1) * rank] * lax.rsqrt(resident_ref[d : d + 1, 0:1])
        out[...] = block.astype(out.dtype)


def swap(value, axis, d):
    return lax.ppermute(value, axis, [(i, i ^ d) for i in range(lax.axis_size(axis))])


def shards(queries, probe_group, probe_local, points, point_cluster, test_matrix):
    groups = lax.axis_size("shard")
    helpers = lax.axis_size("help")
    planes = groups // INNER
    count = queries.shape[0]
    rank = test_matrix.shape[0]
    own_points, width = points.shape
    kept = jax.ShapeDtypeStruct((helpers // 2 * rank, width), F32)

    packed, keep, passed, mark, resident = pl.pallas_call(
        functools.partial(lift_kernel, helpers),
        out_shape=[
            jax.ShapeDtypeStruct((count * width // LANES + TILE, LANES), BF16),
            kept,
            kept,
            jax.ShapeDtypeStruct((1, own_points), jnp.int32),
            jax.ShapeDtypeStruct((8, LANES), F32),
        ],
        in_specs=[HBM] * 6,
        scratch_shapes=[
            pltpu.VMEM((2, count), jnp.int32),
            pltpu.VMEM((2, count), jnp.int32),
            pltpu.VMEM(point_cluster.shape, jnp.int32),
            pltpu.VMEM(test_matrix.shape, BF16),
            pltpu.VMEM(points.shape, BF16),
            pltpu.SemaphoreType.DMA((4 + CHUNKS + width // LANES,)),
        ],
        compiler_params=pltpu.CompilerParams(vmem_limit_bytes=FIRST << 20),
        name="lift",
    )(queries, probe_group.T, probe_local.T, point_cluster, test_matrix, points)
    own, *leaving = pl.pallas_call(
        join_kernel,
        out_shape=[jax.ShapeDtypeStruct((rank, width), F32)]
        + [jax.ShapeDtypeStruct((rank, width), BF16)] * (helpers // 2 - 1),
        compiler_params=PARAMS,
        name="join",
    )(keep, swap(passed, "help", 1))
    for k, part in enumerate(leaving, 1):
        own = own + swap(part, "help", 2 * k).astype(F32)
    lifter = own.astype(BF16)
    mine = jnp.concatenate([lifter] + [swap(lifter, "shard", INNER * d) for d in range(1, planes)], axis=0)
    theirs = swap(mine, "help", 1)

    index, axes = range(groups * helpers), ("shard", "help")
    one = [(i, i ^ (2 if i % 2 == 0 else helpers)) for i in index]
    two = [(i, i ^ (helpers if i % 2 == 0 else 2)) for i in index]
    far = lax.ppermute(packed, axes, two)
    near = gate(lax.ppermute(packed, axes, one), mine)
    across = lax.ppermute(near, axes, two)

    wide = width + LANES
    begun = pl.pallas_call(
        functools.partial(score_kernel, planes, helpers, 3),
        out_shape=jax.ShapeDtypeStruct((2 * planes * rank, wide), F32),
        compiler_params=PARAMS,
        name="score",
    )(mine, theirs, packed, near, far)
    moments, passed = pl.pallas_call(
        functools.partial(score_kernel, planes, helpers, 1),
        out_shape=[jax.ShapeDtypeStruct((planes * rank, wide), F32)] * 2,
        compiler_params=PARAMS,
        name="score_last",
    )(mine, theirs, across, begun)
    folded = pl.pallas_call(
        functools.partial(fold_kernel, planes),
        out_shape=[jax.ShapeDtypeStruct((rank, wide), F32)]
        + [jax.ShapeDtypeStruct((rank * width // LANES + TILE, LANES), BF16)] * (planes - 1),
        compiler_params=PARAMS,
        name="fold",
    )(moments, swap(passed, "help", 1))
    moments = [folded[0]] + [swap(folded[d], "shard", INNER * d) for d in range(1, planes)]

    scaled = pl.pallas_call(
        scale_kernel,
        out_shape=jax.ShapeDtypeStruct((rank, width), BF16),
        compiler_params=PARAMS,
        name="scale",
    )(resident, *moments)
    scaled = [scaled] + [swap(scaled, "help", d) for d in range(1, helpers)]

    block = jax.ShapeDtypeStruct((rank, width), F32)
    sent = jax.ShapeDtypeStruct((rank, width), BF16)
    sketch, regressor, *parts = pl.pallas_call(
        functools.partial(sketch_kernel, helpers),
        out_shape=[jax.ShapeDtypeStruct((rank, own_points), F32), block, block] + [sent] * (helpers - 2),
        compiler_params=PARAMS,
        name="sketch",
    )(mark, resident, points, *scaled)
    for d, part in enumerate(parts, 1):
        regressor = regressor + swap(part, "help", d).astype(F32)
    return sketch, regressor[None]


def solution(mesh):
    in_specs = (
        P(("shard", "help"), None),
        P(("shard", "help"), None),
        P(("shard", "help"), None),
        P(("shard", "help"), None),
        P("shard", None),
        P(None, ("shard", "help")),
    )
    out_specs = (P(None, ("shard", "help")), P(("shard", "help"), None, None))
    return jax.shard_map(shards, mesh=mesh, in_specs=in_specs, out_specs=out_specs, check_vma=False)
```

```python
import functools

import jax
import jax.numpy as jnp
from jax import lax
from jax.experimental import pallas as pl
from jax.experimental.pallas import tpu as pltpu
from jax.sharding import PartitionSpec as P

F32 = jnp.float32
BF16 = jnp.bfloat16
LANES = 128
TILE = 16
CHUNKS = 4
INNER = 2
FIRST = 60

ANY = pl.BlockSpec(memory_space=pl.ANY)
VMEM = pl.BlockSpec(memory_space=pltpu.VMEM)
HBM = pl.BlockSpec(memory_space=pltpu.HBM)
PARAMS = pltpu.CompilerParams(vmem_limit_bytes=32 * 1024 * 1024)


def contract(a, b, dims):
    return lax.dot_general(a, b, (dims, ((), ())), preferred_element_type=F32)


def halves(value):
    high = value.astype(BF16)
    return high, (value - high.astype(F32)).astype(BF16)


def slabs(ref, rows, width):
    return jnp.concatenate([ref[k * rows : (k + 1) * rows, :] for k in range(width // LANES)], axis=1)


def order(helpers):
    return [*range(0, helpers, 2), *range(1, helpers, 2)]


def lift_kernel(helpers, *refs):
    rows_hbm, group_hbm, local_hbm, ids_hbm, test_hbm, points_hbm = refs[:6]
    packed_ref, keep_ref, pass_ref, mark_ref, resident_ref = refs[6:11]
    group_ref, local_ref, ids_ref, test_ref, points_ref, sems = refs[11:]
    helper = lax.axis_index("help")
    asked, width = rows_hbm.shape
    rank, count = test_ref.shape
    piece = count // CHUNKS
    pairs = [(ids_hbm, ids_ref), (test_hbm, test_ref)]
    for k in range(CHUNKS):
        part = pl.ds(k * piece, piece)
        pairs.append((points_hbm.at[part], points_ref.at[part]))
    pairs += [(group_hbm, group_ref), (local_hbm, local_ref)]
    for k in range(width // LANES):
        pairs.append((rows_hbm.at[:, pl.ds(k * LANES, LANES)], packed_ref.at[pl.ds(k * asked, asked)]))
    copies = [pltpu.make_async_copy(*pair, sems.at[k]) for k, pair in enumerate(pairs)]
    for copy in copies:
        copy.start()
    copies[0].wait()
    everyone = ids_ref[...]
    mark = ids_ref[:, pl.ds(pl.multiple_of(helper * count, LANES), count)] ^ helper
    mark_ref[...] = mark
    for d in range(helpers):
        many = jnp.sum((everyone == (helper ^ d)).astype(F32), axis=1, keepdims=True)
        resident_ref[d : d + 1, :] = jnp.broadcast_to(many, (1, LANES))
    copies[1].wait()
    test = test_ref[...]
    offsets = order(helpers)
    rows = jnp.concatenate([jnp.where(mark == d, test, jnp.zeros((), BF16)) for d in offsets], axis=0)
    total = None
    for k in range(CHUNKS):
        copies[2 + k].wait()
        part = slice(k * piece, (k + 1) * piece)
        more = contract(rows[:, part], points_ref[part, :], ((1,), (0,)))
        total = more if total is None else total + more
    keep_ref[...] = total[: keep_ref.shape[0]]
    pass_ref[...] = total[keep_ref.shape[0] :]
    for copy in copies[2 + CHUNKS :]:
        copy.wait()
    cluster = (group_ref[...] * helpers + local_ref[...]).astype(F32)
    line = [cluster[k : k + 1, j : j + LANES] for k in (0, 1) for j in range(0, asked, LANES)]
    line.append(jnp.zeros((TILE - len(line), LANES), F32))
    packed_ref[asked * width // LANES :, :] = jnp.concatenate(line, axis=0).astype(BF16)


def join_kernel(keep_ref, got_ref, own_ref, *send_refs):
    rank = own_ref.shape[0]
    own_ref[...] = keep_ref[:rank, :] + got_ref[:rank, :]
    for k, ref in enumerate(send_refs, 1):
        part = slice(k * rank, (k + 1) * rank)
        ref[...] = (keep_ref[part, :] + got_ref[part, :]).astype(BF16)


def gate_kernel(*refs):
    pass


def gate(values, *others):
    return pl.pallas_call(
        gate_kernel,
        out_shape=[jax.ShapeDtypeStruct(value.shape, value.dtype) for value in values],
        in_specs=[ANY] * (len(values) + len(others)),
        out_specs=[ANY] * len(values),
        input_output_aliases={k: k for k in range(len(values))},
        compiler_params=pltpu.CompilerParams(vmem_limit_bytes=1 << 20),
        name="gate",
    )(*values, *others)


def score_kernel(planes, helpers, blocks, mine_ref, theirs_ref, *refs):
    queries, rest = refs[:blocks], refs[blocks:]
    shard, helper = lax.axis_index("shard"), lax.axis_index("help")
    span, width = mine_ref.shape
    rank = span // planes
    count = (queries[0].shape[0] - TILE) * LANES // width
    pieces = count // LANES
    lifter = jnp.concatenate([mine_ref[...], theirs_ref[...]], axis=0)
    clusters = [
        ((shard ^ (INNER * d)) * helpers + (helper ^ side)).astype(F32) for side in (0, 1) for d in range(planes)
    ]
    total, tally = None, [None] * len(clusters)
    for q_ref in queries:
        rows = slabs(q_ref, count, width)
        tile = q_ref[count * width // LANES :, :].astype(F32)
        first, second = (
            jnp.concatenate([tile[k * pieces + j : k * pieces + j + 1] for j in range(pieces)], axis=1) for k in (0, 1)
        )
        lifted = contract(lifter, rows, ((1,), (1,)))
        kept = []
        for k, cluster in enumerate(clusters):
            hit = (first == cluster) | (second == cluster)
            kept.append(jnp.where(hit, lifted[k * rank : (k + 1) * rank], 0.0))
            here = hit.astype(F32)
            tally[k] = here if tally[k] is None else tally[k] + here
        high, low = halves(jnp.concatenate(kept, axis=0))
        part = contract(high, rows, ((1,), (0,))) + contract(low, rows, ((1,), (0,)))
        total = part if total is None else total + part
    named = jnp.concatenate(
        [jnp.broadcast_to(jnp.sum(t, axis=1, keepdims=True), (rank, LANES)) for t in tally], axis=0
    )
    if len(rest) == 1:
        rest[0][:, :width] = total
        rest[0][:, width:] = named
    else:
        before, *outs = rest
        for side, out in enumerate(outs):
            part = slice(side * span, (side + 1) * span)
            out[:, :width] = before[part, :width] + total[part]
            out[:, width:] = before[part, width:] + named[part]


def fold_kernel(planes, mine_ref, theirs_ref, own_ref, *send_refs):
    rank, wide = own_ref.shape
    width = wide - LANES
    line = lax.broadcasted_iota(jnp.int32, (TILE, LANES), 0)
    for d in range(planes):
        part = slice(d * rank, (d + 1) * rank)
        total = mine_ref[part, :] + theirs_ref[part, :]
        if d == 0:
            own_ref[...] = total
        else:
            ref = send_refs[d - 1]
            for k in range(width // LANES):
                ref[k * rank : (k + 1) * rank, :] = total[:, k * LANES : (k + 1) * LANES].astype(BF16)
            named = total[:TILE, width:]
            many = jnp.floor(named * (1.0 / 256.0))
            rest = named - 256.0 * many
            ref[rank * width // LANES :, :] = jnp.where(line == 0, many, jnp.where(line == 1, rest, 0.0)).astype(BF16)


def scale_kernel(resident_ref, own_ref, *refs):
    *parts, out_ref = refs
    rank, width = out_ref.shape
    total = own_ref[:, :width]
    queried = own_ref[0:1, width : width + 1]
    for part in parts:
        total = total + slabs(part, rank, width).astype(F32)
        tile = part[rank * width // LANES :, :].astype(F32)
        queried = queried + 256.0 * tile[0:1, 0:1] + tile[1:2, 0:1]
    resident = resident_ref[0:1, 0:1]
    factor = lax.rsqrt((queried + 1.0) * (queried + resident)) * (1.0 / width)
    out_ref[...] = (total * factor).astype(out_ref.dtype)


def sketch_kernel(helpers, mark_ref, resident_ref, points_ref, *refs):
    scaled, sketch_ref, outs = refs[:helpers], refs[helpers], refs[helpers + 1 :]
    rank, count = sketch_ref.shape
    mark = mark_ref[...]
    points = points_ref[...]
    product = contract(jnp.concatenate([s[...] for s in scaled], axis=0), points, ((1,), (1,)))
    sketch = product[:rank]
    for d in range(1, helpers):
        sketch = jnp.where(mark == d, product[d * rank : (d + 1) * rank], sketch)
    sketch_ref[...] = sketch
    rounded = sketch.astype(BF16)
    rows = [jnp.where(mark == d, rounded, jnp.zeros((), BF16)) for d in range(helpers)]
    summed = contract(jnp.concatenate(rows, axis=0), points, ((1,), (0,)))
    for d, out in enumerate(outs):
        block = summed[d * rank : (d + 1) * rank] * lax.rsqrt(resident_ref[d : d + 1, 0:1])
        out[...] = block.astype(out.dtype)


def swap(value, axis, d):
    return lax.ppermute(value, axis, [(i, i ^ d) for i in range(lax.axis_size(axis))])


def shards(queries, probe_group, probe_local, points, point_cluster, test_matrix):
    groups = lax.axis_size("shard")
    helpers = lax.axis_size("help")
    planes = groups // INNER
    count = queries.shape[0]
    rank = test_matrix.shape[0]
    own_points, width = points.shape
    kept = jax.ShapeDtypeStruct((helpers // 2 * rank, width), F32)

    packed, keep, passed, mark, resident = pl.pallas_call(
        functools.partial(lift_kernel, helpers),
        out_shape=[
            jax.ShapeDtypeStruct((count * width // LANES + TILE, LANES), BF16),
            kept,
            kept,
            jax.ShapeDtypeStruct((1, own_points), jnp.int32),
            jax.ShapeDtypeStruct((8, LANES), F32),
        ],
        in_specs=[HBM] * 6,
        scratch_shapes=[
            pltpu.VMEM((2, count), jnp.int32),
            pltpu.VMEM((2, count), jnp.int32),
            pltpu.VMEM(point_cluster.shape, jnp.int32),
            pltpu.VMEM(test_matrix.shape, BF16),
            pltpu.VMEM(points.shape, BF16),
            pltpu.SemaphoreType.DMA((4 + CHUNKS + width // LANES,)),
        ],
        compiler_params=pltpu.CompilerParams(vmem_limit_bytes=FIRST << 20),
        name="lift",
    )(queries, probe_group.T, probe_local.T, point_cluster, test_matrix, points)
    own, *leaving = pl.pallas_call(
        join_kernel,
        out_shape=[jax.ShapeDtypeStruct((rank, width), F32)]
        + [jax.ShapeDtypeStruct((rank, width), BF16)] * (helpers // 2 - 1),
        compiler_params=PARAMS,
        name="join",
    )(keep, swap(passed, "help", 1))
    for k, part in enumerate(leaving, 1):
        own = own + swap(part, "help", 2 * k).astype(F32)
    lifter = own.astype(BF16)
    mine = jnp.concatenate([lifter] + [swap(lifter, "shard", INNER * d) for d in range(1, planes)], axis=0)
    theirs = swap(mine, "help", 1)

    index, axes = range(groups * helpers), ("shard", "help")
    one = [(i, i ^ (2 if i % 2 == 0 else helpers)) for i in index]
    two = [(i, i ^ (helpers if i % 2 == 0 else 2)) for i in index]
    near, far = gate([lax.ppermute(packed, axes, turn) for turn in (one, two)], mine)
    across = lax.ppermute(near, axes, two)

    wide = width + LANES
    begun = pl.pallas_call(
        functools.partial(score_kernel, planes, helpers, 3),
        out_shape=jax.ShapeDtypeStruct((2 * planes * rank, wide), F32),
        compiler_params=PARAMS,
        name="score",
    )(mine, theirs, packed, near, far)
    moments, passed = pl.pallas_call(
        functools.partial(score_kernel, planes, helpers, 1),
        out_shape=[jax.ShapeDtypeStruct((planes * rank, wide), F32)] * 2,
        compiler_params=PARAMS,
        name="score_last",
    )(mine, theirs, across, begun)
    folded = pl.pallas_call(
        functools.partial(fold_kernel, planes),
        out_shape=[jax.ShapeDtypeStruct((rank, wide), F32)]
        + [jax.ShapeDtypeStruct((rank * width // LANES + TILE, LANES), BF16)] * (planes - 1),
        compiler_params=PARAMS,
        name="fold",
    )(moments, swap(passed, "help", 1))
    moments = [folded[0]] + [swap(folded[d], "shard", INNER * d) for d in range(1, planes)]

    scaled = pl.pallas_call(
        scale_kernel,
        out_shape=jax.ShapeDtypeStruct((rank, width), BF16),
        compiler_params=PARAMS,
        name="scale",
    )(resident, *moments)
    scaled = [scaled] + [swap(scaled, "help", d) for d in range(1, helpers)]

    block = jax.ShapeDtypeStruct((rank, width), F32)
    sent = jax.ShapeDtypeStruct((rank, width), BF16)
    sketch, regressor, *parts = pl.pallas_call(
        functools.partial(sketch_kernel, helpers),
        out_shape=[jax.ShapeDtypeStruct((rank, own_points), F32), block, block] + [sent] * (helpers - 2),
        compiler_params=PARAMS,
        name="sketch",
    )(mark, resident, points, *scaled)
    for d, part in enumerate(parts, 1):
        regressor = regressor + swap(part, "help", d).astype(F32)
    return sketch, regressor[None]


def solution(mesh):
    in_specs = (
        P(("shard", "help"), None),
        P(("shard", "help"), None),
        P(("shard", "help"), None),
        P(("shard", "help"), None),
        P("shard", None),
        P(None, ("shard", "help")),
    )
    out_specs = (P(None, ("shard", "help")), P(("shard", "help"), None, None))
    return jax.shard_map(shards, mesh=mesh, in_specs=in_specs, out_specs=out_specs, check_vma=False)
```

```python
import functools

import jax
import jax.numpy as jnp
from jax import lax
from jax.experimental import pallas as pl
from jax.experimental.pallas import tpu as pltpu
from jax.sharding import PartitionSpec as P

F32 = jnp.float32
BF16 = jnp.bfloat16
LANES = 128
TILE = 16
CHUNKS = 4
INNER = 2
FIRST = 60

ANY = pl.BlockSpec(memory_space=pl.ANY)
VMEM = pl.BlockSpec(memory_space=pltpu.VMEM)
HBM = pl.BlockSpec(memory_space=pltpu.HBM)
PARAMS = pltpu.CompilerParams(vmem_limit_bytes=32 * 1024 * 1024)


def contract(a, b, dims):
    return lax.dot_general(a, b, (dims, ((), ())), preferred_element_type=F32)


def halves(value):
    high = value.astype(BF16)
    return high, (value - high.astype(F32)).astype(BF16)


def slabs(ref, rows, width):
    return jnp.concatenate([ref[k * rows : (k + 1) * rows, :] for k in range(width // LANES)], axis=1)


def lift_kernel(helpers, *refs):
    rows_hbm, group_hbm, local_hbm, ids_hbm, test_hbm, points_hbm = refs[:6]
    packed_ref, mark_ref, resident_ref = refs[6:9]
    outs = refs[9 : 9 + helpers]
    group_ref, local_ref, ids_ref, test_ref, points_ref, sems = refs[9 + helpers :]
    helper = lax.axis_index("help")
    asked, width = rows_hbm.shape
    rank, count = test_ref.shape
    piece = count // CHUNKS
    pairs = [(ids_hbm, ids_ref), (test_hbm, test_ref)]
    for k in range(CHUNKS):
        part = pl.ds(k * piece, piece)
        pairs.append((points_hbm.at[part], points_ref.at[part]))
    pairs += [(group_hbm, group_ref), (local_hbm, local_ref)]
    for k in range(width // LANES):
        pairs.append((rows_hbm.at[:, pl.ds(k * LANES, LANES)], packed_ref.at[pl.ds(k * asked, asked)]))
    copies = [pltpu.make_async_copy(*pair, sems.at[k]) for k, pair in enumerate(pairs)]
    for copy in copies:
        copy.start()
    copies[0].wait()
    everyone = ids_ref[...]
    mark = ids_ref[:, pl.ds(pl.multiple_of(helper * count, LANES), count)] ^ helper
    mark_ref[...] = mark
    for d in range(helpers):
        many = jnp.sum((everyone == (helper ^ d)).astype(F32), axis=1, keepdims=True)
        resident_ref[d : d + 1, :] = jnp.broadcast_to(many, (1, LANES))
    copies[1].wait()
    test = test_ref[...]
    rows = jnp.concatenate([jnp.where(mark == d, test, jnp.zeros((), BF16)) for d in range(helpers)], axis=0)
    total = None
    for k in range(CHUNKS):
        copies[2 + k].wait()
        part = slice(k * piece, (k + 1) * piece)
        more = contract(rows[:, part], points_ref[part, :], ((1,), (0,)))
        total = more if total is None else total + more
    for d, out in enumerate(outs):
        out[...] = total[d * rank : (d + 1) * rank].astype(out.dtype)
    for copy in copies[2 + CHUNKS :]:
        copy.wait()
    cluster = (group_ref[...] * helpers + local_ref[...]).astype(F32)
    line = [cluster[k : k + 1, j : j + LANES] for k in (0, 1) for j in range(0, asked, LANES)]
    line.append(jnp.zeros((TILE - len(line), LANES), F32))
    packed_ref[asked * width // LANES :, :] = jnp.concatenate(line, axis=0).astype(BF16)


def join_kernel(*refs):
    *parts, out = refs
    total = parts[0][...]
    for part in parts[1:]:
        total = total + part[...].astype(F32)
    out[...] = total.astype(out.dtype)


def gate_kernel(*refs):
    pass


def gate(values, *others):
    return pl.pallas_call(
        gate_kernel,
        out_shape=[jax.ShapeDtypeStruct(value.shape, value.dtype) for value in values],
        in_specs=[ANY] * (len(values) + len(others)),
        out_specs=[ANY] * len(values),
        input_output_aliases={k: k for k in range(len(values))},
        compiler_params=pltpu.CompilerParams(vmem_limit_bytes=1 << 20),
        name="gate",
    )(*values, *others)


def score_kernel(planes, helpers, blocks, mine_ref, theirs_ref, *refs):
    queries, rest = refs[:blocks], refs[blocks:]
    shard, helper = lax.axis_index("shard"), lax.axis_index("help")
    span, width = mine_ref.shape
    rank = span // planes
    count = (queries[0].shape[0] - TILE) * LANES // width
    pieces = count // LANES
    lifter = jnp.concatenate([mine_ref[...], theirs_ref[...]], axis=0)
    clusters = [
        ((shard ^ (INNER * d)) * helpers + (helper ^ side)).astype(F32) for side in (0, 1) for d in range(planes)
    ]
    total, tally = None, [None] * len(clusters)
    for q_ref in queries:
        rows = slabs(q_ref, count, width)
        tile = q_ref[count * width // LANES :, :].astype(F32)
        first, second = (
            jnp.concatenate([tile[k * pieces + j : k * pieces + j + 1] for j in range(pieces)], axis=1) for k in (0, 1)
        )
        lifted = contract(lifter, rows, ((1,), (1,)))
        kept = []
        for k, cluster in enumerate(clusters):
            hit = (first == cluster) | (second == cluster)
            kept.append(jnp.where(hit, lifted[k * rank : (k + 1) * rank], 0.0))
            here = hit.astype(F32)
            tally[k] = here if tally[k] is None else tally[k] + here
        high, low = halves(jnp.concatenate(kept, axis=0))
        part = contract(high, rows, ((1,), (0,))) + contract(low, rows, ((1,), (0,)))
        total = part if total is None else total + part
    named = jnp.concatenate(
        [jnp.broadcast_to(jnp.sum(t, axis=1, keepdims=True), (rank, LANES)) for t in tally], axis=0
    )
    if len(rest) == 1:
        rest[0][:, :width] = total
        rest[0][:, width:] = named
    else:
        before, *outs = rest
        for side, out in enumerate(outs):
            part = slice(side * span, (side + 1) * span)
            out[:, :width] = before[part, :width] + total[part]
            out[:, width:] = before[part, width:] + named[part]


def fold_kernel(planes, mine_ref, theirs_ref, own_ref, *send_refs):
    rank, wide = own_ref.shape
    width = wide - LANES
    line = lax.broadcasted_iota(jnp.int32, (TILE, LANES), 0)
    for d in range(planes):
        part = slice(d * rank, (d + 1) * rank)
        total = mine_ref[part, :] + theirs_ref[part, :]
        if d == 0:
            own_ref[...] = total
        else:
            ref = send_refs[d - 1]
            for k in range(width // LANES):
                ref[k * rank : (k + 1) * rank, :] = total[:, k * LANES : (k + 1) * LANES].astype(BF16)
            named = total[:TILE, width:]
            many = jnp.floor(named * (1.0 / 256.0))
            rest = named - 256.0 * many
            ref[rank * width // LANES :, :] = jnp.where(line == 0, many, jnp.where(line == 1, rest, 0.0)).astype(BF16)


def scale_kernel(resident_ref, own_ref, *refs):
    *parts, out_ref = refs
    rank, width = out_ref.shape
    total = own_ref[:, :width]
    queried = own_ref[0:1, width : width + 1]
    for part in parts:
        total = total + slabs(part, rank, width).astype(F32)
        tile = part[rank * width // LANES :, :].astype(F32)
        queried = queried + 256.0 * tile[0:1, 0:1] + tile[1:2, 0:1]
    resident = resident_ref[0:1, 0:1]
    factor = lax.rsqrt((queried + 1.0) * (queried + resident)) * (1.0 / width)
    out_ref[...] = (total * factor).astype(out_ref.dtype)


def sketch_kernel(helpers, mark_ref, resident_ref, points_ref, *refs):
    scaled, sketch_ref, outs = refs[:helpers], refs[helpers], refs[helpers + 1 :]
    rank, count = sketch_ref.shape
    mark = mark_ref[...]
    points = points_ref[...]
    product = contract(jnp.concatenate([s[...] for s in scaled], axis=0), points, ((1,), (1,)))
    sketch = product[:rank]
    for d in range(1, helpers):
        sketch = jnp.where(mark == d, product[d * rank : (d + 1) * rank], sketch)
    sketch_ref[...] = sketch
    rounded = sketch.astype(BF16)
    rows = [jnp.where(mark == d, rounded, jnp.zeros((), BF16)) for d in range(helpers)]
    summed = contract(jnp.concatenate(rows, axis=0), points, ((1,), (0,)))
    for d, out in enumerate(outs):
        block = summed[d * rank : (d + 1) * rank] * lax.rsqrt(resident_ref[d : d + 1, 0:1])
        out[...] = block.astype(out.dtype)


def swap(value, axis, d):
    return lax.ppermute(value, axis, [(i, i ^ d) for i in range(lax.axis_size(axis))])


def shards(queries, probe_group, probe_local, points, point_cluster, test_matrix):
    groups = lax.axis_size("shard")
    helpers = lax.axis_size("help")
    planes = groups // INNER
    count = queries.shape[0]
    rank = test_matrix.shape[0]
    own_points, width = points.shape
    block = jax.ShapeDtypeStruct((rank, width), F32)
    sent = jax.ShapeDtypeStruct((rank, width), BF16)

    packed, mark, resident, own, *parts = pl.pallas_call(
        functools.partial(lift_kernel, helpers),
        out_shape=[
            jax.ShapeDtypeStruct((count * width // LANES + TILE, LANES), BF16),
            jax.ShapeDtypeStruct((1, own_points), jnp.int32),
            jax.ShapeDtypeStruct((8, LANES), F32),
            block,
            block,
        ]
        + [sent] * (helpers - 2),
        in_specs=[HBM] * 6,
        scratch_shapes=[
            pltpu.VMEM((2, count), jnp.int32),
            pltpu.VMEM((2, count), jnp.int32),
            pltpu.VMEM(point_cluster.shape, jnp.int32),
            pltpu.VMEM(test_matrix.shape, BF16),
            pltpu.VMEM(points.shape, BF16),
            pltpu.SemaphoreType.DMA((4 + CHUNKS + width // LANES,)),
        ],
        compiler_params=pltpu.CompilerParams(vmem_limit_bytes=FIRST << 20),
        name="lift",
    )(queries, probe_group.T, probe_local.T, point_cluster, test_matrix, points)
    lifter = pl.pallas_call(
        join_kernel,
        out_shape=sent,
        compiler_params=PARAMS,
        name="join",
    )(own, *[swap(part, "help", d) for d, part in enumerate(parts, 1)])
    mine = jnp.concatenate([lifter] + [swap(lifter, "shard", INNER * d) for d in range(1, planes)], axis=0)
    theirs = swap(mine, "help", 1)

    index, axes = range(groups * helpers), ("shard", "help")
    one = [(i, i ^ (2 if i % 2 == 0 else helpers)) for i in index]
    two = [(i, i ^ (helpers if i % 2 == 0 else 2)) for i in index]
    near, far = gate([lax.ppermute(packed, axes, turn) for turn in (one, two)], theirs)
    across = lax.ppermute(near, axes, two)

    wide = width + LANES
    begun = pl.pallas_call(
        functools.partial(score_kernel, planes, helpers, 3),
        out_shape=jax.ShapeDtypeStruct((2 * planes * rank, wide), F32),
        compiler_params=PARAMS,
        name="score",
    )(mine, theirs, packed, near, far)
    moments, passed = pl.pallas_call(
        functools.partial(score_kernel, planes, helpers, 1),
        out_shape=[jax.ShapeDtypeStruct((planes * rank, wide), F32)] * 2,
        compiler_params=PARAMS,
        name="score_last",
    )(mine, theirs, across, begun)
    folded = pl.pallas_call(
        functools.partial(fold_kernel, planes),
        out_shape=[jax.ShapeDtypeStruct((rank, wide), F32)]
        + [jax.ShapeDtypeStruct((rank * width // LANES + TILE, LANES), BF16)] * (planes - 1),
        compiler_params=PARAMS,
        name="fold",
    )(moments, swap(passed, "help", 1))
    moments = [folded[0]] + [swap(folded[d], "shard", INNER * d) for d in range(1, planes)]

    scaled = pl.pallas_call(
        scale_kernel,
        out_shape=jax.ShapeDtypeStruct((rank, width), BF16),
        compiler_params=PARAMS,
        name="scale",
    )(resident, *moments)
    scaled = [scaled] + [swap(scaled, "help", d) for d in range(1, helpers)]

    sketch, regressor, *parts = pl.pallas_call(
        functools.partial(sketch_kernel, helpers),
        out_shape=[jax.ShapeDtypeStruct((rank, own_points), F32), block, block] + [sent] * (helpers - 2),
        compiler_params=PARAMS,
        name="sketch",
    )(mark, resident, points, *scaled)
    for d, part in enumerate(parts, 1):
        regressor = regressor + swap(part, "help", d).astype(F32)
    return sketch, regressor[None]


def solution(mesh):
    in_specs = (
        P(("shard", "help"), None),
        P(("shard", "help"), None),
        P(("shard", "help"), None),
        P(("shard", "help"), None),
        P("shard", None),
        P(None, ("shard", "help")),
    )
    out_specs = (P(None, ("shard", "help")), P(("shard", "help"), None, None))
    return jax.shard_map(shards, mesh=mesh, in_specs=in_specs, out_specs=out_specs, check_vma=False)
```

```python
import functools

import jax
import jax.numpy as jnp
from jax import lax
from jax.experimental import pallas as pl
from jax.experimental.pallas import tpu as pltpu
from jax.sharding import PartitionSpec as P

F32 = jnp.float32
BF16 = jnp.bfloat16
LANES = 128
TILE = 16
CHUNKS = 4
INNER = 2
FIRST = 60

ANY = pl.BlockSpec(memory_space=pl.ANY)
VMEM = pl.BlockSpec(memory_space=pltpu.VMEM)
HBM = pl.BlockSpec(memory_space=pltpu.HBM)
PARAMS = pltpu.CompilerParams(vmem_limit_bytes=32 * 1024 * 1024)


def contract(a, b, dims):
    return lax.dot_general(a, b, (dims, ((), ())), preferred_element_type=F32)


def halves(value):
    high = value.astype(BF16)
    return high, (value - high.astype(F32)).astype(BF16)


def slabs(ref, rows, width):
    return jnp.concatenate([ref[k * rows : (k + 1) * rows, :] for k in range(width // LANES)], axis=1)


def lift_kernel(helpers, *refs):
    rows_hbm, group_hbm, local_hbm, ids_hbm, test_hbm, points_hbm = refs[:6]
    packed_ref, mark_ref, resident_ref = refs[6:9]
    outs = refs[9 : 9 + helpers]
    group_ref, local_ref, ids_ref, test_ref, points_ref, sems = refs[9 + helpers :]
    helper = lax.axis_index("help")
    asked, width = rows_hbm.shape
    rank, count = test_ref.shape
    piece = count // CHUNKS
    pairs = [(ids_hbm, ids_ref), (test_hbm, test_ref)]
    for k in range(CHUNKS):
        part = pl.ds(k * piece, piece)
        pairs.append((points_hbm.at[part], points_ref.at[part]))
    pairs += [(group_hbm, group_ref), (local_hbm, local_ref)]
    for k in range(width // LANES):
        pairs.append((rows_hbm.at[:, pl.ds(k * LANES, LANES)], packed_ref.at[pl.ds(k * asked, asked)]))
    copies = [pltpu.make_async_copy(*pair, sems.at[k]) for k, pair in enumerate(pairs)]
    for copy in copies:
        copy.start()
    copies[0].wait()
    everyone = ids_ref[...]
    mark = ids_ref[:, pl.ds(pl.multiple_of(helper * count, LANES), count)] ^ helper
    mark_ref[...] = mark
    for d in range(helpers):
        many = jnp.sum((everyone == (helper ^ d)).astype(F32), axis=1, keepdims=True)
        resident_ref[d : d + 1, :] = jnp.broadcast_to(many, (1, LANES))
    copies[1].wait()
    test = test_ref[...]
    rows = jnp.concatenate([jnp.where(mark == d, test, jnp.zeros((), BF16)) for d in range(helpers)], axis=0)
    total = None
    for k in range(CHUNKS):
        copies[2 + k].wait()
        part = slice(k * piece, (k + 1) * piece)
        more = contract(rows[:, part], points_ref[part, :], ((1,), (0,)))
        total = more if total is None else total + more
    for d, out in enumerate(outs):
        out[...] = total[d * rank : (d + 1) * rank].astype(out.dtype)
    for copy in copies[2 + CHUNKS :]:
        copy.wait()
    cluster = (group_ref[...] * helpers + local_ref[...]).astype(F32)
    line = [cluster[k : k + 1, j : j + LANES] for k in (0, 1) for j in range(0, asked, LANES)]
    line.append(jnp.zeros((TILE - len(line), LANES), F32))
    packed_ref[asked * width // LANES :, :] = jnp.concatenate(line, axis=0).astype(BF16)


def join_kernel(*refs):
    *parts, out = refs
    total = parts[0][...]
    for part in parts[1:]:
        total = total + part[...].astype(F32)
    out[...] = total.astype(out.dtype)


def gate_kernel(*refs):
    pass


def gate(values, *others):
    return pl.pallas_call(
        gate_kernel,
        out_shape=[jax.ShapeDtypeStruct(value.shape, value.dtype) for value in values],
        in_specs=[ANY] * (len(values) + len(others)),
        out_specs=[ANY] * len(values),
        input_output_aliases={k: k for k in range(len(values))},
        compiler_params=pltpu.CompilerParams(vmem_limit_bytes=1 << 20),
        name="gate",
    )(*values, *others)


def score_kernel(planes, helpers, blocks, mine_ref, theirs_ref, *refs):
    queries, rest = refs[:blocks], refs[blocks:]
    shard, helper = lax.axis_index("shard"), lax.axis_index("help")
    span, width = mine_ref.shape
    rank = span // planes
    count = (queries[0].shape[0] - TILE) * LANES // width
    pieces = count // LANES
    lifter = jnp.concatenate([mine_ref[...], theirs_ref[...]], axis=0)
    clusters = [
        ((shard ^ (INNER * d)) * helpers + (helper ^ side)).astype(F32) for side in (0, 1) for d in range(planes)
    ]
    total, tally = None, [None] * len(clusters)
    for q_ref in queries:
        rows = slabs(q_ref, count, width)
        tile = q_ref[count * width // LANES :, :].astype(F32)
        first, second = (
            jnp.concatenate([tile[k * pieces + j : k * pieces + j + 1] for j in range(pieces)], axis=1) for k in (0, 1)
        )
        lifted = contract(lifter, rows, ((1,), (1,)))
        kept = []
        for k, cluster in enumerate(clusters):
            hit = (first == cluster) | (second == cluster)
            kept.append(jnp.where(hit, lifted[k * rank : (k + 1) * rank], 0.0))
            here = hit.astype(F32)
            tally[k] = here if tally[k] is None else tally[k] + here
        high, low = halves(jnp.concatenate(kept, axis=0))
        part = contract(high, rows, ((1,), (0,))) + contract(low, rows, ((1,), (0,)))
        total = part if total is None else total + part
    named = jnp.concatenate(
        [jnp.broadcast_to(jnp.sum(t, axis=1, keepdims=True), (rank, LANES)) for t in tally], axis=0
    )
    if len(rest) == 1:
        rest[0][:, :width] = total
        rest[0][:, width:] = named
    else:
        before, *outs = rest
        for side, out in enumerate(outs):
            part = slice(side * span, (side + 1) * span)
            out[:, :width] = before[part, :width] + total[part]
            out[:, width:] = before[part, width:] + named[part]


def fold_kernel(planes, mine_ref, theirs_ref, own_ref, send_ref):
    rank, wide = own_ref.shape
    width = wide - LANES
    plane = lax.axis_index("shard") // INNER
    line = lax.broadcasted_iota(jnp.int32, (TILE, LANES), 0)
    send_ref[plane] = jnp.zeros(send_ref.shape[1:], BF16)
    for d in range(planes):
        part = slice(d * rank, (d + 1) * rank)
        total = mine_ref[part, :] + theirs_ref[part, :]
        if d == 0:
            own_ref[...] = total
        else:
            named = total[:TILE, width:]
            many = jnp.floor(named * (1.0 / 256.0))
            tile = jnp.where(line == 0, many, jnp.where(line == 1, named - 256.0 * many, 0.0))
            columns = [total[:, k : k + LANES] for k in range(0, width, LANES)]
            send_ref[plane ^ d] = jnp.concatenate(columns + [tile], axis=0).astype(BF16)


def scale_kernel(resident_ref, own_ref, got_ref, out_ref):
    rank, width = out_ref.shape
    total = own_ref[:, :width]
    queried = own_ref[0:1, width : width + 1]
    for k in range(got_ref.shape[0]):
        part = got_ref[k].astype(F32)
        total = total + slabs(part, rank, width)
        tile = part[rank * width // LANES :, :]
        queried = queried + 256.0 * tile[0:1, 0:1] + tile[1:2, 0:1]
    resident = resident_ref[0:1, 0:1]
    factor = lax.rsqrt((queried + 1.0) * (queried + resident)) * (1.0 / width)
    out_ref[...] = (total * factor).astype(out_ref.dtype)


def sketch_kernel(helpers, mark_ref, resident_ref, points_ref, *refs):
    scaled, (sketch_ref, own_ref, send_ref) = refs[:helpers], refs[helpers:]
    helper = lax.axis_index("help")
    rank, count = sketch_ref.shape
    mark = mark_ref[...]
    points = points_ref[...]
    product = contract(jnp.concatenate([s[...] for s in scaled], axis=0), points, ((1,), (1,)))
    sketch = product[:rank]
    for d in range(1, helpers):
        sketch = jnp.where(mark == d, product[d * rank : (d + 1) * rank], sketch)
    sketch_ref[...] = sketch
    rounded = sketch.astype(BF16)
    rows = [jnp.where(mark == d, rounded, jnp.zeros((), BF16)) for d in range(helpers)]
    summed = contract(jnp.concatenate(rows, axis=0), points, ((1,), (0,)))
    for d in range(helpers):
        block = summed[d * rank : (d + 1) * rank] * lax.rsqrt(resident_ref[d : d + 1, 0:1])
        if d == 0:
            own_ref[...] = block
        send_ref[helper ^ d] = (block if d else jnp.zeros_like(block)).astype(BF16)


def swap(value, axis, d):
    return lax.ppermute(value, axis, [(i, i ^ d) for i in range(lax.axis_size(axis))])


def shards(queries, probe_group, probe_local, points, point_cluster, test_matrix):
    groups = lax.axis_size("shard")
    helpers = lax.axis_size("help")
    planes = groups // INNER
    count = queries.shape[0]
    rank = test_matrix.shape[0]
    own_points, width = points.shape
    block = jax.ShapeDtypeStruct((rank, width), F32)
    sent = jax.ShapeDtypeStruct((rank, width), BF16)

    packed, mark, resident, own, *parts = pl.pallas_call(
        functools.partial(lift_kernel, helpers),
        out_shape=[
            jax.ShapeDtypeStruct((count * width // LANES + TILE, LANES), BF16),
            jax.ShapeDtypeStruct((1, own_points), jnp.int32),
            jax.ShapeDtypeStruct((8, LANES), F32),
            block,
            block,
        ]
        + [sent] * (helpers - 2),
        in_specs=[HBM] * 6,
        scratch_shapes=[
            pltpu.VMEM((2, count), jnp.int32),
            pltpu.VMEM((2, count), jnp.int32),
            pltpu.VMEM(point_cluster.shape, jnp.int32),
            pltpu.VMEM(test_matrix.shape, BF16),
            pltpu.VMEM(points.shape, BF16),
            pltpu.SemaphoreType.DMA((4 + CHUNKS + width // LANES,)),
        ],
        compiler_params=pltpu.CompilerParams(vmem_limit_bytes=FIRST << 20),
        name="lift",
    )(queries, probe_group.T, probe_local.T, point_cluster, test_matrix, points)
    lifter = pl.pallas_call(
        join_kernel,
        out_shape=sent,
        compiler_params=PARAMS,
        name="join",
    )(own, *[swap(part, "help", d) for d, part in enumerate(parts, 1)])
    mine = jnp.concatenate([lifter] + [swap(lifter, "shard", INNER * d) for d in range(1, planes)], axis=0)
    theirs = swap(mine, "help", 1)

    index, axes = range(groups * helpers), ("shard", "help")
    one = [(i, i ^ (2 if i % 2 == 0 else helpers)) for i in index]
    two = [(i, i ^ (helpers if i % 2 == 0 else 2)) for i in index]
    near, far = gate([lax.ppermute(packed, axes, turn) for turn in (one, two)], theirs)
    across = lax.ppermute(near, axes, two)

    wide = width + LANES
    begun = pl.pallas_call(
        functools.partial(score_kernel, planes, helpers, 3),
        out_shape=jax.ShapeDtypeStruct((2 * planes * rank, wide), F32),
        compiler_params=PARAMS,
        name="score",
    )(mine, theirs, packed, near, far)
    moments, passed = pl.pallas_call(
        functools.partial(score_kernel, planes, helpers, 1),
        out_shape=[jax.ShapeDtypeStruct((planes * rank, wide), F32)] * 2,
        compiler_params=PARAMS,
        name="score_last",
    )(mine, theirs, across, begun)
    folded = pl.pallas_call(
        functools.partial(fold_kernel, planes),
        out_shape=[jax.ShapeDtypeStruct((rank, wide), F32)]
        + [jax.ShapeDtypeStruct((planes, rank * width // LANES + TILE, LANES), BF16)],
        compiler_params=PARAMS,
        name="fold",
    )(moments, swap(passed, "help", 1))
    lines = [[k + INNER * p for p in range(planes)] for k in range(INNER)]
    got = lax.all_to_all(folded[1], "shard", 0, 0, axis_index_groups=lines, tiled=True)

    scaled = pl.pallas_call(
        scale_kernel,
        out_shape=jax.ShapeDtypeStruct((rank, width), BF16),
        compiler_params=PARAMS,
        name="scale",
    )(resident, folded[0], got)
    scaled = [scaled] + [swap(scaled, "help", d) for d in range(1, helpers)]

    sketch, regressor, parts = pl.pallas_call(
        functools.partial(sketch_kernel, helpers),
        out_shape=[
            jax.ShapeDtypeStruct((rank, own_points), F32),
            block,
            jax.ShapeDtypeStruct((helpers, rank, width), BF16),
        ],
        compiler_params=PARAMS,
        name="sketch",
    )(mark, resident, points, *scaled)
    parts = lax.all_to_all(parts, "help", 0, 0, tiled=True)
    regressor = regressor + jnp.sum(parts.astype(F32), axis=0)
    return sketch, regressor[None]


def solution(mesh):
    in_specs = (
        P(("shard", "help"), None),
        P(("shard", "help"), None),
        P(("shard", "help"), None),
        P(("shard", "help"), None),
        P("shard", None),
        P(None, ("shard", "help")),
    )
    out_specs = (P(None, ("shard", "help")), P(("shard", "help"), None, None))
    return jax.shard_map(shards, mesh=mesh, in_specs=in_specs, out_specs=out_specs, check_vma=False)
```

```python
import functools

import jax
import jax.numpy as jnp
from jax import lax
from jax.experimental import pallas as pl
from jax.experimental.pallas import tpu as pltpu
from jax.sharding import PartitionSpec as P

F32 = jnp.float32
BF16 = jnp.bfloat16
LANES = 128
TILE = 16
CHUNKS = 4
INNER = 2

ANY = pl.BlockSpec(memory_space=pl.ANY)
VMEM = pl.BlockSpec(memory_space=pltpu.VMEM)
VMEM = pl.BlockSpec(memory_space=pltpu.VMEM)
HBM = pl.BlockSpec(memory_space=pltpu.HBM)
PARAMS = pltpu.CompilerParams(vmem_limit_bytes=32 * 1024 * 1024)


def in_hbm(value):
    return pltpu.with_memory_space_constraint(value, pltpu.HBM)


def contract(a, b, dims):
    return lax.dot_general(a, b, (dims, ((), ())), preferred_element_type=F32)


def halves(value):
    high = value.astype(BF16)
    return high, (value - high.astype(F32)).astype(BF16)


def slabs(ref, rows, width):
    return jnp.concatenate([ref[k * rows : (k + 1) * rows, :] for k in range(width // LANES)], axis=1)


def lift_kernel(helpers, *refs):
    rows_hbm, group_hbm, local_hbm, ids_hbm, test_hbm, points_hbm = refs[:6]
    packed_ref, mark_ref, resident_ref = refs[6:9]
    outs = refs[9 : 9 + helpers]
    group_ref, local_ref, ids_ref, test_ref, points_ref, sems = refs[9 + helpers :]
    helper = lax.axis_index("help")
    asked, width = rows_hbm.shape
    rank, count = test_ref.shape
    piece = count // CHUNKS
    pairs = [(ids_hbm, ids_ref), (test_hbm, test_ref)]
    for k in range(CHUNKS):
        part = pl.ds(k * piece, piece)
        pairs.append((points_hbm.at[part], points_ref.at[part]))
    pairs += [(group_hbm, group_ref), (local_hbm, local_ref)]
    for k in range(width // LANES):
        pairs.append((rows_hbm.at[:, pl.ds(k * LANES, LANES)], packed_ref.at[pl.ds(k * asked, asked)]))
    copies = [pltpu.make_async_copy(*pair, sems.at[k]) for k, pair in enumerate(pairs)]
    for copy in copies:
        copy.start()
    copies[0].wait()
    everyone = ids_ref[...]
    mark = ids_ref[:, pl.ds(pl.multiple_of(helper * count, LANES), count)] ^ helper
    mark_ref[...] = mark
    for d in range(helpers):
        many = jnp.sum((everyone == (helper ^ d)).astype(F32), axis=1, keepdims=True)
        resident_ref[d : d + 1, :] = jnp.broadcast_to(many, (1, LANES))
    copies[1].wait()
    test = test_ref[...]
    rows = jnp.concatenate([jnp.where(mark == d, test, jnp.zeros((), BF16)) for d in range(helpers)], axis=0)
    total = None
    for k in range(CHUNKS):
        copies[2 + k].wait()
        part = slice(k * piece, (k + 1) * piece)
        more = contract(rows[:, part], points_ref[part, :], ((1,), (0,)))
        total = more if total is None else total + more
    for d, out in enumerate(outs):
        out[...] = total[d * rank : (d + 1) * rank].astype(out.dtype)
    for copy in copies[2 + CHUNKS :]:
        copy.wait()
    cluster = (group_ref[...] * helpers + local_ref[...]).astype(F32)
    line = [cluster[k : k + 1, j : j + LANES] for k in (0, 1) for j in range(0, asked, LANES)]
    line.append(jnp.zeros((TILE - len(line), LANES), F32))
    packed_ref[asked * width // LANES :, :] = jnp.concatenate(line, axis=0).astype(BF16)


def join_kernel(*refs):
    *parts, out = refs
    total = parts[0][...]
    for part in parts[1:]:
        total = total + part[...].astype(F32)
    out[...] = total.astype(out.dtype)


def gate_kernel(*refs):
    pass


def gate(values, *others):
    return pl.pallas_call(
        gate_kernel,
        out_shape=[jax.ShapeDtypeStruct(value.shape, value.dtype) for value in values],
        in_specs=[ANY] * (len(values) + len(others)),
        out_specs=[ANY] * len(values),
        input_output_aliases={k: k for k in range(len(values))},
        compiler_params=pltpu.CompilerParams(vmem_limit_bytes=1 << 20),
        name="gate",
    )(*values, *others)


def score_kernel(planes, helpers, blocks, mine_ref, theirs_ref, *refs):
    queries, rest = refs[:blocks], refs[blocks:]
    shard, helper = lax.axis_index("shard"), lax.axis_index("help")
    span, width = mine_ref.shape
    rank = span // planes
    count = (queries[0].shape[0] - TILE) * LANES // width
    pieces = count // LANES
    lifter = jnp.concatenate([mine_ref[...], theirs_ref[...]], axis=0)
    clusters = [
        ((shard ^ (INNER * d)) * helpers + (helper ^ side)).astype(F32) for side in (0, 1) for d in range(planes)
    ]
    total, tally = None, [None] * len(clusters)
    for q_ref in queries:
        rows = slabs(q_ref, count, width)
        tile = q_ref[count * width // LANES :, :].astype(F32)
        first, second = (
            jnp.concatenate([tile[k * pieces + j : k * pieces + j + 1] for j in range(pieces)], axis=1) for k in (0, 1)
        )
        lifted = contract(lifter, rows, ((1,), (1,)))
        kept = []
        for k, cluster in enumerate(clusters):
            hit = (first == cluster) | (second == cluster)
            kept.append(jnp.where(hit, lifted[k * rank : (k + 1) * rank], 0.0))
            here = hit.astype(F32)
            tally[k] = here if tally[k] is None else tally[k] + here
        high, low = halves(jnp.concatenate(kept, axis=0))
        part = contract(high, rows, ((1,), (0,))) + contract(low, rows, ((1,), (0,)))
        total = part if total is None else total + part
    named = jnp.concatenate(
        [jnp.broadcast_to(jnp.sum(t, axis=1, keepdims=True), (rank, LANES)) for t in tally], axis=0
    )
    if len(rest) == 1:
        rest[0][:, :width] = total
        rest[0][:, width:] = named
    else:
        before, *outs = rest
        for side, out in enumerate(outs):
            part = slice(side * span, (side + 1) * span)
            out[:, :width] = before[part, :width] + total[part]
            out[:, width:] = before[part, width:] + named[part]


def fold_kernel(planes, mine_ref, theirs_ref, own_ref, *send_refs):
    rank, wide = own_ref.shape
    width = wide - LANES
    line = lax.broadcasted_iota(jnp.int32, (TILE, LANES), 0)
    for d in range(planes):
        part = slice(d * rank, (d + 1) * rank)
        total = mine_ref[part, :] + theirs_ref[part, :]
        if d == 0:
            own_ref[...] = total
        else:
            ref = send_refs[d - 1]
            for k in range(width // LANES):
                ref[k * rank : (k + 1) * rank, :] = total[:, k * LANES : (k + 1) * LANES].astype(BF16)
            named = total[:TILE, width:]
            many = jnp.floor(named * (1.0 / 256.0))
            rest = named - 256.0 * many
            ref[rank * width // LANES :, :] = jnp.where(line == 0, many, jnp.where(line == 1, rest, 0.0)).astype(BF16)


def scale_kernel(resident_ref, own_ref, *refs):
    *parts, out_ref = refs
    rank, width = out_ref.shape
    total = own_ref[:, :width]
    queried = own_ref[0:1, width : width + 1]
    for part in parts:
        total = total + slabs(part, rank, width).astype(F32)
        tile = part[rank * width // LANES :, :].astype(F32)
        queried = queried + 256.0 * tile[0:1, 0:1] + tile[1:2, 0:1]
    resident = resident_ref[0:1, 0:1]
    factor = lax.rsqrt((queried + 1.0) * (queried + resident)) * (1.0 / width)
    out_ref[...] = (total * factor).astype(out_ref.dtype)


def sketch_kernel(helpers, mark_ref, resident_ref, points_ref, *refs):
    scaled, sketch_hbm, outs = refs[:helpers], refs[helpers], refs[helpers + 1 : -2]
    sketch_ref, sem = refs[-2:]
    rank, count = sketch_ref.shape
    mark = mark_ref[...]
    points = points_ref[...]
    product = contract(jnp.concatenate([s[...] for s in scaled], axis=0), points, ((1,), (1,)))
    sketch = product[:rank]
    for d in range(1, helpers):
        sketch = jnp.where(mark == d, product[d * rank : (d + 1) * rank], sketch)
    sketch_ref[...] = sketch
    leaving = pltpu.make_async_copy(sketch_ref, sketch_hbm, sem)
    leaving.start()
    rounded = sketch.astype(BF16)
    rows = [jnp.where(mark == d, rounded, jnp.zeros((), BF16)) for d in range(helpers)]
    summed = contract(jnp.concatenate(rows, axis=0), points, ((1,), (0,)))
    for d, out in enumerate(outs):
        block = summed[d * rank : (d + 1) * rank] * lax.rsqrt(resident_ref[d : d + 1, 0:1])
        out[...] = block.astype(out.dtype)
    leaving.wait()


def swap(value, axis, d):
    return lax.ppermute(value, axis, [(i, i ^ d) for i in range(lax.axis_size(axis))])


def swaps(values, axis, unit=1):
    return [swap(value, axis, unit * d) for d, value in reversed([*enumerate(values, 1)])]


def shards(queries, probe_group, probe_local, points, point_cluster, test_matrix):
    groups = lax.axis_size("shard")
    helpers = lax.axis_size("help")
    planes = groups // INNER
    count = queries.shape[0]
    rank = test_matrix.shape[0]
    own_points, width = points.shape
    block = jax.ShapeDtypeStruct((rank, width), F32)
    sent = jax.ShapeDtypeStruct((rank, width), BF16)

    packed, mark, resident, own, *parts = pl.pallas_call(
        functools.partial(lift_kernel, helpers),
        out_shape=[
            jax.ShapeDtypeStruct((count * width // LANES + TILE, LANES), BF16),
            jax.ShapeDtypeStruct((1, own_points), jnp.int32),
            jax.ShapeDtypeStruct((8, LANES), F32),
            block,
            block,
        ]
        + [sent] * (helpers - 2),
        in_specs=[HBM] * 6,
        scratch_shapes=[
            pltpu.VMEM((2, count), jnp.int32),
            pltpu.VMEM((2, count), jnp.int32),
            pltpu.VMEM(point_cluster.shape, jnp.int32),
            pltpu.VMEM(test_matrix.shape, BF16),
            pltpu.VMEM(points.shape, BF16),
            pltpu.SemaphoreType.DMA((4 + CHUNKS + width // LANES,)),
        ],
        compiler_params=PARAMS,
        name="lift",
    )(*[in_hbm(a) for a in (queries, probe_group.T, probe_local.T, point_cluster, test_matrix, points)])
    lifter = pl.pallas_call(
        join_kernel,
        out_shape=sent,
        compiler_params=PARAMS,
        name="join",
    )(own, *swaps(parts, "help"))
    mine = jnp.concatenate([lifter] + [swap(lifter, "shard", INNER * d) for d in range(1, planes)], axis=0)
    theirs = swap(mine, "help", 1)

    index, axes = range(groups * helpers), ("shard", "help")
    one = [(i, i ^ (2 if i % 2 == 0 else helpers)) for i in index]
    two = [(i, i ^ (helpers if i % 2 == 0 else 2)) for i in index]
    near, far = gate([lax.ppermute(packed, axes, turn) for turn in (one, two)], theirs)
    across = lax.ppermute(near, axes, two)

    wide = width + LANES
    begun = pl.pallas_call(
        functools.partial(score_kernel, planes, helpers, 3),
        out_shape=jax.ShapeDtypeStruct((2 * planes * rank, wide), F32),
        compiler_params=PARAMS,
        name="score",
    )(mine, theirs, packed, near, far)
    moments, passed = pl.pallas_call(
        functools.partial(score_kernel, planes, helpers, 1),
        out_shape=[jax.ShapeDtypeStruct((planes * rank, wide), F32)] * 2,
        compiler_params=PARAMS,
        name="score_last",
    )(mine, theirs, across, begun)
    folded = pl.pallas_call(
        functools.partial(fold_kernel, planes),
        out_shape=[jax.ShapeDtypeStruct((rank, wide), F32)]
        + [jax.ShapeDtypeStruct((rank * width // LANES + TILE, LANES), BF16)] * (planes - 1),
        compiler_params=PARAMS,
        name="fold",
    )(moments, swap(passed, "help", 1))
    moments = [folded[0]] + swaps(folded[1:], "shard", INNER)

    scaled = pl.pallas_call(
        scale_kernel,
        out_shape=jax.ShapeDtypeStruct((rank, width), BF16),
        compiler_params=PARAMS,
        name="scale",
    )(resident, *moments)
    scaled = [scaled] + [swap(scaled, "help", d) for d in range(1, helpers)]

    sketch, regressor, *parts = pl.pallas_call(
        functools.partial(sketch_kernel, helpers),
        out_shape=[jax.ShapeDtypeStruct((rank, own_points), F32), block, block] + [sent] * (helpers - 2),
        out_specs=[HBM] + [VMEM] * helpers,
        scratch_shapes=[pltpu.VMEM((rank, own_points), F32), pltpu.SemaphoreType.DMA],
        compiler_params=PARAMS,
        name="sketch",
    )(mark, resident, points, *scaled)
    for part in swaps(parts, "help"):
        regressor = regressor + part.astype(F32)
    return sketch, regressor[None]


def solution(mesh):
    in_specs = (
        P(("shard", "help"), None),
        P(("shard", "help"), None),
        P(("shard", "help"), None),
        P(("shard", "help"), None),
        P("shard", None),
        P(None, ("shard", "help")),
    )
    out_specs = (P(None, ("shard", "help")), P(("shard", "help"), None, None))
    return jax.shard_map(shards, mesh=mesh, in_specs=in_specs, out_specs=out_specs, check_vma=False)
```

```python
import functools

import jax
import jax.numpy as jnp
from jax import lax
from jax.experimental import pallas as pl
from jax.experimental.pallas import tpu as pltpu
from jax.sharding import PartitionSpec as P

F32 = jnp.float32
BF16 = jnp.bfloat16
LANES = 128
TILE = 16
CHUNKS = 4
INNER = 2

ANY = pl.BlockSpec(memory_space=pl.ANY)
VMEM = pl.BlockSpec(memory_space=pltpu.VMEM)
VMEM = pl.BlockSpec(memory_space=pltpu.VMEM)
HBM = pl.BlockSpec(memory_space=pltpu.HBM)
PARAMS = pltpu.CompilerParams(vmem_limit_bytes=32 * 1024 * 1024)


def in_hbm(value):
    return pltpu.with_memory_space_constraint(value, pltpu.HBM)


def contract(a, b, dims):
    return lax.dot_general(a, b, (dims, ((), ())), preferred_element_type=F32)


def halves(value):
    high = value.astype(BF16)
    return high, (value - high.astype(F32)).astype(BF16)


def slabs(ref, rows, width):
    return jnp.concatenate([ref[k * rows : (k + 1) * rows, :] for k in range(width // LANES)], axis=1)


def lift_kernel(helpers, *refs):
    rows_hbm, group_hbm, local_hbm, ids_hbm, test_hbm, points_hbm = refs[:6]
    packed_ref, mark_ref, resident_ref = refs[6:9]
    outs = refs[9 : 9 + helpers]
    group_ref, local_ref, ids_ref, test_ref, points_ref, sems = refs[9 + helpers :]
    helper = lax.axis_index("help")
    asked, width = rows_hbm.shape
    rank, count = test_ref.shape
    piece = count // CHUNKS
    pairs = [(ids_hbm, ids_ref), (test_hbm, test_ref)]
    for k in range(CHUNKS):
        part = pl.ds(k * piece, piece)
        pairs.append((points_hbm.at[part], points_ref.at[part]))
    pairs += [(group_hbm, group_ref), (local_hbm, local_ref)]
    for k in range(width // LANES):
        pairs.append((rows_hbm.at[:, pl.ds(k * LANES, LANES)], packed_ref.at[pl.ds(k * asked, asked)]))
    copies = [pltpu.make_async_copy(*pair, sems.at[k]) for k, pair in enumerate(pairs)]
    for copy in copies:
        copy.start()
    copies[0].wait()
    everyone = ids_ref[...]
    mark = ids_ref[:, pl.ds(pl.multiple_of(helper * count, LANES), count)] ^ helper
    mark_ref[...] = mark
    for d in range(helpers):
        many = jnp.sum((everyone == (helper ^ d)).astype(F32), axis=1, keepdims=True)
        resident_ref[d : d + 1, :] = jnp.broadcast_to(many, (1, LANES))
    copies[1].wait()
    test = test_ref[...]
    rows = jnp.concatenate([jnp.where(mark == d, test, jnp.zeros((), BF16)) for d in range(helpers)], axis=0)
    total = None
    for k in range(CHUNKS):
        copies[2 + k].wait()
        part = slice(k * piece, (k + 1) * piece)
        more = contract(rows[:, part], points_ref[part, :], ((1,), (0,)))
        total = more if total is None else total + more
    for d, out in enumerate(outs):
        out[...] = total[d * rank : (d + 1) * rank].astype(out.dtype)
    for copy in copies[2 + CHUNKS :]:
        copy.wait()
    cluster = (group_ref[...] * helpers + local_ref[...]).astype(F32)
    line = [cluster[k : k + 1, j : j + LANES] for k in (0, 1) for j in range(0, asked, LANES)]
    line.append(jnp.zeros((TILE - len(line), LANES), F32))
    packed_ref[asked * width // LANES :, :] = jnp.concatenate(line, axis=0).astype(BF16)


def join_kernel(*refs):
    *parts, out = refs
    total = parts[0][...]
    for part in parts[1:]:
        total = total + part[...].astype(F32)
    out[...] = total.astype(out.dtype)


def stack_kernel(*refs):
    *parts, out = refs
    rank = parts[0].shape[0]
    for k, part in enumerate(parts):
        out[k * rank : (k + 1) * rank, :] = part[...]


def gate_kernel(*refs):
    pass


def gate(values, *others):
    return pl.pallas_call(
        gate_kernel,
        out_shape=[jax.ShapeDtypeStruct(value.shape, value.dtype) for value in values],
        in_specs=[ANY] * (len(values) + len(others)),
        out_specs=[ANY] * len(values),
        input_output_aliases={k: k for k in range(len(values))},
        compiler_params=pltpu.CompilerParams(vmem_limit_bytes=1 << 20),
        name="gate",
    )(*values, *others)


def score_kernel(planes, helpers, blocks, mine_ref, theirs_ref, *refs):
    queries, rest = refs[:blocks], refs[blocks:]
    shard, helper = lax.axis_index("shard"), lax.axis_index("help")
    span, width = mine_ref.shape
    rank = span // planes
    count = (queries[0].shape[0] - TILE) * LANES // width
    pieces = count // LANES
    lifter = jnp.concatenate([mine_ref[...], theirs_ref[...]], axis=0)
    clusters = [
        ((shard ^ (INNER * d)) * helpers + (helper ^ side)).astype(F32) for side in (0, 1) for d in range(planes)
    ]
    total, tally = None, [None] * len(clusters)
    for q_ref in queries:
        rows = slabs(q_ref, count, width)
        tile = q_ref[count * width // LANES :, :].astype(F32)
        first, second = (
            jnp.concatenate([tile[k * pieces + j : k * pieces + j + 1] for j in range(pieces)], axis=1) for k in (0, 1)
        )
        lifted = contract(lifter, rows, ((1,), (1,)))
        kept = []
        for k, cluster in enumerate(clusters):
            hit = (first == cluster) | (second == cluster)
            kept.append(jnp.where(hit, lifted[k * rank : (k + 1) * rank], 0.0))
            here = hit.astype(F32)
            tally[k] = here if tally[k] is None else tally[k] + here
        high, low = halves(jnp.concatenate(kept, axis=0))
        part = contract(high, rows, ((1,), (0,))) + contract(low, rows, ((1,), (0,)))
        total = part if total is None else total + part
    named = jnp.concatenate(
        [jnp.broadcast_to(jnp.sum(t, axis=1, keepdims=True), (rank, LANES)) for t in tally], axis=0
    )
    if len(rest) == 1:
        rest[0][:, :width] = total
        rest[0][:, width:] = named
    else:
        before, *outs = rest
        for side, out in enumerate(outs):
            part = slice(side * span, (side + 1) * span)
            out[:, :width] = before[part, :width] + total[part]
            out[:, width:] = before[part, width:] + named[part]


def fold_kernel(planes, mine_ref, theirs_ref, own_ref, *send_refs):
    rank, wide = own_ref.shape
    width = wide - LANES
    line = lax.broadcasted_iota(jnp.int32, (TILE, LANES), 0)
    for d in range(planes):
        part = slice(d * rank, (d + 1) * rank)
        total = mine_ref[part, :] + theirs_ref[part, :]
        if d == 0:
            own_ref[...] = total
        else:
            ref = send_refs[d - 1]
            for k in range(width // LANES):
                ref[k * rank : (k + 1) * rank, :] = total[:, k * LANES : (k + 1) * LANES].astype(BF16)
            named = total[:TILE, width:]
            many = jnp.floor(named * (1.0 / 256.0))
            rest = named - 256.0 * many
            ref[rank * width // LANES :, :] = jnp.where(line == 0, many, jnp.where(line == 1, rest, 0.0)).astype(BF16)


def scale_kernel(resident_ref, own_ref, *refs):
    *parts, out_ref = refs
    rank, width = out_ref.shape
    total = own_ref[:, :width]
    queried = own_ref[0:1, width : width + 1]
    for part in parts:
        total = total + slabs(part, rank, width).astype(F32)
        tile = part[rank * width // LANES :, :].astype(F32)
        queried = queried + 256.0 * tile[0:1, 0:1] + tile[1:2, 0:1]
    resident = resident_ref[0:1, 0:1]
    factor = lax.rsqrt((queried + 1.0) * (queried + resident)) * (1.0 / width)
    out_ref[...] = (total * factor).astype(out_ref.dtype)


def sketch_kernel(helpers, mark_ref, resident_ref, points_ref, *refs):
    scaled, sketch_hbm, outs = refs[:helpers], refs[helpers], refs[helpers + 1 : -2]
    sketch_ref, sem = refs[-2:]
    rank, count = sketch_ref.shape
    mark = mark_ref[...]
    points = points_ref[...]
    product = contract(jnp.concatenate([s[...] for s in scaled], axis=0), points, ((1,), (1,)))
    sketch = product[:rank]
    for d in range(1, helpers):
        sketch = jnp.where(mark == d, product[d * rank : (d + 1) * rank], sketch)
    sketch_ref[...] = sketch
    leaving = pltpu.make_async_copy(sketch_ref, sketch_hbm, sem)
    leaving.start()
    rounded = sketch.astype(BF16)
    rows = [jnp.where(mark == d, rounded, jnp.zeros((), BF16)) for d in range(helpers)]
    summed = contract(jnp.concatenate(rows, axis=0), points, ((1,), (0,)))
    for d, out in enumerate(outs):
        block = summed[d * rank : (d + 1) * rank] * lax.rsqrt(resident_ref[d : d + 1, 0:1])
        out[...] = block.astype(out.dtype)
    leaving.wait()


def swap(value, axis, d):
    return lax.ppermute(value, axis, [(i, i ^ d) for i in range(lax.axis_size(axis))])


def swaps(values, axis, unit=1):
    return [swap(value, axis, unit * d) for d, value in reversed([*enumerate(values, 1)])]


def shards(queries, probe_group, probe_local, points, point_cluster, test_matrix):
    groups = lax.axis_size("shard")
    helpers = lax.axis_size("help")
    planes = groups // INNER
    count = queries.shape[0]
    rank = test_matrix.shape[0]
    own_points, width = points.shape
    block = jax.ShapeDtypeStruct((rank, width), F32)
    sent = jax.ShapeDtypeStruct((rank, width), BF16)

    packed, mark, resident, own, *parts = pl.pallas_call(
        functools.partial(lift_kernel, helpers),
        out_shape=[
            jax.ShapeDtypeStruct((count * width // LANES + TILE, LANES), BF16),
            jax.ShapeDtypeStruct((1, own_points), jnp.int32),
            jax.ShapeDtypeStruct((8, LANES), F32),
            block,
            block,
        ]
        + [sent] * (helpers - 2),
        in_specs=[HBM] * 6,
        scratch_shapes=[
            pltpu.VMEM((2, count), jnp.int32),
            pltpu.VMEM((2, count), jnp.int32),
            pltpu.VMEM(point_cluster.shape, jnp.int32),
            pltpu.VMEM(test_matrix.shape, BF16),
            pltpu.VMEM(points.shape, BF16),
            pltpu.SemaphoreType.DMA((4 + CHUNKS + width // LANES,)),
        ],
        compiler_params=PARAMS,
        name="lift",
    )(*[in_hbm(a) for a in (queries, probe_group.T, probe_local.T, point_cluster, test_matrix, points)])
    lifter = pl.pallas_call(
        join_kernel,
        out_shape=sent,
        compiler_params=PARAMS,
        name="join",
    )(own, *swaps(parts, "help"))
    mine = pl.pallas_call(
        stack_kernel,
        out_shape=jax.ShapeDtypeStruct((planes * rank, width), BF16),
        compiler_params=PARAMS,
        cost_estimate=pl.CostEstimate(flops=35 * 10**8, bytes_accessed=10**5, transcendentals=0),
        name="stack",
    )(lifter, *[swap(lifter, "shard", INNER * d) for d in range(1, planes)])
    theirs = swap(mine, "help", 1)

    index, axes = range(groups * helpers), ("shard", "help")
    one = [(i, i ^ (2 if i % 2 == 0 else helpers)) for i in index]
    two = [(i, i ^ (helpers if i % 2 == 0 else 2)) for i in index]
    far, near = gate([lax.ppermute(packed, axes, turn) for turn in (one, two)], mine)
    across = lax.ppermute(near, axes, one)

    wide = width + LANES
    begun = pl.pallas_call(
        functools.partial(score_kernel, planes, helpers, 3),
        out_shape=jax.ShapeDtypeStruct((2 * planes * rank, wide), F32),
        compiler_params=PARAMS,
        name="score",
    )(mine, theirs, packed, near, far)
    moments, passed = pl.pallas_call(
        functools.partial(score_kernel, planes, helpers, 1),
        out_shape=[jax.ShapeDtypeStruct((planes * rank, wide), F32)] * 2,
        compiler_params=PARAMS,
        name="score_last",
    )(mine, theirs, across, begun)
    folded = pl.pallas_call(
        functools.partial(fold_kernel, planes),
        out_shape=[jax.ShapeDtypeStruct((rank, wide), F32)]
        + [jax.ShapeDtypeStruct((rank * width // LANES + TILE, LANES), BF16)] * (planes - 1),
        compiler_params=PARAMS,
        name="fold",
    )(moments, swap(passed, "help", 1))
    moments = [folded[0]] + swaps(folded[1:], "shard", INNER)

    scaled = pl.pallas_call(
        scale_kernel,
        out_shape=jax.ShapeDtypeStruct((rank, width), BF16),
        compiler_params=PARAMS,
        name="scale",
    )(resident, *moments)
    scaled = [scaled] + [swap(scaled, "help", d) for d in range(1, helpers)]

    sketch, regressor, *parts = pl.pallas_call(
        functools.partial(sketch_kernel, helpers),
        out_shape=[jax.ShapeDtypeStruct((rank, own_points), F32), block, block] + [sent] * (helpers - 2),
        out_specs=[HBM] + [VMEM] * helpers,
        scratch_shapes=[pltpu.VMEM((rank, own_points), F32), pltpu.SemaphoreType.DMA],
        compiler_params=PARAMS,
        name="sketch",
    )(mark, resident, points, *scaled)
    for part in swaps(parts, "help"):
        regressor = regressor + part.astype(F32)
    return sketch, regressor[None]


def solution(mesh):
    in_specs = (
        P(("shard", "help"), None),
        P(("shard", "help"), None),
        P(("shard", "help"), None),
        P(("shard", "help"), None),
        P("shard", None),
        P(None, ("shard", "help")),
    )
    out_specs = (P(None, ("shard", "help")), P(("shard", "help"), None, None))
    return jax.shard_map(shards, mesh=mesh, in_specs=in_specs, out_specs=out_specs, check_vma=False)
```

```python
import functools

import jax
import jax.numpy as jnp
from jax import lax
from jax.experimental import pallas as pl
from jax.experimental.pallas import tpu as pltpu
from jax.sharding import PartitionSpec as P

F32 = jnp.float32
BF16 = jnp.bfloat16
LANES = 128
TILE = 16
CHUNKS = 4
INNER = 2

ANY = pl.BlockSpec(memory_space=pl.ANY)
VMEM = pl.BlockSpec(memory_space=pltpu.VMEM)
VMEM = pl.BlockSpec(memory_space=pltpu.VMEM)
HBM = pl.BlockSpec(memory_space=pltpu.HBM)
PARAMS = pltpu.CompilerParams(vmem_limit_bytes=32 * 1024 * 1024)


def in_hbm(value):
    return pltpu.with_memory_space_constraint(value, pltpu.HBM)


def contract(a, b, dims):
    return lax.dot_general(a, b, (dims, ((), ())), preferred_element_type=F32)


def halves(value):
    high = value.astype(BF16)
    return high, (value - high.astype(F32)).astype(BF16)


def slabs(ref, rows, width):
    return jnp.concatenate([ref[k * rows : (k + 1) * rows, :] for k in range(width // LANES)], axis=1)


def lift_kernel(helpers, *refs):
    rows_hbm, group_hbm, local_hbm, ids_hbm, test_hbm, points_hbm = refs[:6]
    packed_ref, mark_ref, resident_ref = refs[6:9]
    outs = refs[9 : 9 + helpers]
    group_ref, local_ref, ids_ref, test_ref, points_ref, sems = refs[9 + helpers :]
    helper = lax.axis_index("help")
    asked, width = rows_hbm.shape
    rank, count = test_ref.shape
    piece = count // CHUNKS
    pairs = [(ids_hbm, ids_ref), (test_hbm, test_ref)]
    for k in range(CHUNKS):
        part = pl.ds(k * piece, piece)
        pairs.append((points_hbm.at[part], points_ref.at[part]))
    pairs += [(group_hbm, group_ref), (local_hbm, local_ref)]
    for k in range(width // LANES):
        pairs.append((rows_hbm.at[:, pl.ds(k * LANES, LANES)], packed_ref.at[pl.ds(k * asked, asked)]))
    copies = [pltpu.make_async_copy(*pair, sems.at[k]) for k, pair in enumerate(pairs)]
    for copy in copies:
        copy.start()
    copies[0].wait()
    everyone = ids_ref[...]
    mark = ids_ref[:, pl.ds(pl.multiple_of(helper * count, LANES), count)] ^ helper
    mark_ref[...] = mark
    for d in range(helpers):
        many = jnp.sum((everyone == (helper ^ d)).astype(F32), axis=1, keepdims=True)
        resident_ref[d : d + 1, :] = jnp.broadcast_to(many, (1, LANES))
    copies[1].wait()
    test = test_ref[...]
    rows = jnp.concatenate([jnp.where(mark == d, test, jnp.zeros((), BF16)) for d in range(helpers)], axis=0)
    total = None
    for k in range(CHUNKS):
        copies[2 + k].wait()
        part = slice(k * piece, (k + 1) * piece)
        more = contract(rows[:, part], points_ref[part, :], ((1,), (0,)))
        total = more if total is None else total + more
    for d, out in enumerate(outs):
        out[...] = total[d * rank : (d + 1) * rank].astype(out.dtype)
    for copy in copies[2 + CHUNKS :]:
        copy.wait()
    cluster = (group_ref[...] * helpers + local_ref[...]).astype(F32)
    line = [cluster[k : k + 1, j : j + LANES] for k in (0, 1) for j in range(0, asked, LANES)]
    line.append(jnp.zeros((TILE - len(line), LANES), F32))
    packed_ref[asked * width // LANES :, :] = jnp.concatenate(line, axis=0).astype(BF16)


def join_kernel(*refs):
    *parts, out = refs
    total = parts[0][...]
    for part in parts[1:]:
        total = total + part[...].astype(F32)
    out[...] = total.astype(out.dtype)


def stack_kernel(*refs):
    *parts, out = refs
    rank = parts[0].shape[0]
    for k, part in enumerate(parts):
        out[k * rank : (k + 1) * rank, :] = part[...]


def gate_kernel(*refs):
    pass


def gate(values, *others):
    return pl.pallas_call(
        gate_kernel,
        out_shape=[jax.ShapeDtypeStruct(value.shape, value.dtype) for value in values],
        in_specs=[ANY] * (len(values) + len(others)),
        out_specs=[ANY] * len(values),
        input_output_aliases={k: k for k in range(len(values))},
        compiler_params=pltpu.CompilerParams(vmem_limit_bytes=1 << 20),
        name="gate",
    )(*values, *others)


def score_kernel(planes, helpers, blocks, mine_ref, theirs_ref, *refs):
    queries, rest = refs[:blocks], refs[blocks:]
    shard, helper = lax.axis_index("shard"), lax.axis_index("help")
    span, width = mine_ref.shape
    rank = span // planes
    count = (queries[0].shape[0] - TILE) * LANES // width
    pieces = count // LANES
    lifter = jnp.concatenate([mine_ref[...], theirs_ref[...]], axis=0)
    clusters = [
        ((shard ^ (INNER * d)) * helpers + (helper ^ side)).astype(F32) for side in (0, 1) for d in range(planes)
    ]
    total, tally = None, [None] * len(clusters)
    for q_ref in queries:
        rows = slabs(q_ref, count, width)
        tile = q_ref[count * width // LANES :, :].astype(F32)
        first, second = (
            jnp.concatenate([tile[k * pieces + j : k * pieces + j + 1] for j in range(pieces)], axis=1) for k in (0, 1)
        )
        lifted = contract(lifter, rows, ((1,), (1,)))
        kept = []
        for k, cluster in enumerate(clusters):
            hit = (first == cluster) | (second == cluster)
            kept.append(jnp.where(hit, lifted[k * rank : (k + 1) * rank], 0.0))
            here = hit.astype(F32)
            tally[k] = here if tally[k] is None else tally[k] + here
        high, low = halves(jnp.concatenate(kept, axis=0))
        part = contract(high, rows, ((1,), (0,))) + contract(low, rows, ((1,), (0,)))
        total = part if total is None else total + part
    named = jnp.concatenate(
        [jnp.broadcast_to(jnp.sum(t, axis=1, keepdims=True), (rank, LANES)) for t in tally], axis=0
    )
    if len(rest) == 1:
        rest[0][:, :width] = total
        rest[0][:, width:] = named
    else:
        before, *outs = rest
        for side, out in enumerate(outs):
            part = slice(side * span, (side + 1) * span)
            out[:, :width] = before[part, :width] + total[part]
            out[:, width:] = before[part, width:] + named[part]


def fold_kernel(planes, mine_ref, theirs_ref, own_ref, *send_refs):
    rank, wide = own_ref.shape
    width = wide - LANES
    line = lax.broadcasted_iota(jnp.int32, (TILE, LANES), 0)
    for d in range(planes):
        part = slice(d * rank, (d + 1) * rank)
        total = mine_ref[part, :] + theirs_ref[part, :]
        if d == 0:
            own_ref[...] = total
        else:
            ref = send_refs[d - 1]
            for k in range(width // LANES):
                ref[k * rank : (k + 1) * rank, :] = total[:, k * LANES : (k + 1) * LANES].astype(BF16)
            named = total[:TILE, width:]
            many = jnp.floor(named * (1.0 / 256.0))
            rest = named - 256.0 * many
            ref[rank * width // LANES :, :] = jnp.where(line == 0, many, jnp.where(line == 1, rest, 0.0)).astype(BF16)


def scale_kernel(resident_ref, own_ref, *refs):
    *parts, out_ref = refs
    rank, width = out_ref.shape
    total = own_ref[:, :width]
    queried = own_ref[0:1, width : width + 1]
    for part in parts:
        total = total + slabs(part, rank, width).astype(F32)
        tile = part[rank * width // LANES :, :].astype(F32)
        queried = queried + 256.0 * tile[0:1, 0:1] + tile[1:2, 0:1]
    resident = resident_ref[0:1, 0:1]
    factor = lax.rsqrt((queried + 1.0) * (queried + resident)) * (1.0 / width)
    out_ref[...] = (total * factor).astype(out_ref.dtype)


def sketch_kernel(helpers, mark_ref, resident_ref, points_ref, *refs):
    scaled, sketch_hbm, outs = refs[:helpers], refs[helpers], refs[helpers + 1 : -2]
    sketch_ref, sem = refs[-2:]
    rank, count = sketch_ref.shape
    mark = mark_ref[...]
    points = points_ref[...]
    product = contract(jnp.concatenate([s[...] for s in scaled], axis=0), points, ((1,), (1,)))
    sketch = product[:rank]
    for d in range(1, helpers):
        sketch = jnp.where(mark == d, product[d * rank : (d + 1) * rank], sketch)
    sketch_ref[...] = sketch
    leaving = pltpu.make_async_copy(sketch_ref, sketch_hbm, sem)
    leaving.start()
    rounded = sketch.astype(BF16)
    rows = [jnp.where(mark == d, rounded, jnp.zeros((), BF16)) for d in range(helpers)]
    summed = contract(jnp.concatenate(rows, axis=0), points, ((1,), (0,)))
    for d, out in enumerate(outs):
        block = summed[d * rank : (d + 1) * rank] * lax.rsqrt(resident_ref[d : d + 1, 0:1])
        out[...] = block.astype(out.dtype)
    leaving.wait()


def swap(value, axis, d):
    return lax.ppermute(value, axis, [(i, i ^ d) for i in range(lax.axis_size(axis))])


def swaps(values, axis, unit=1):
    return [swap(value, axis, unit * d) for d, value in reversed([*enumerate(values, 1)])]


def shards(queries, probe_group, probe_local, points, point_cluster, test_matrix):
    groups = lax.axis_size("shard")
    helpers = lax.axis_size("help")
    planes = groups // INNER
    count = queries.shape[0]
    rank = test_matrix.shape[0]
    own_points, width = points.shape
    block = jax.ShapeDtypeStruct((rank, width), F32)
    sent = jax.ShapeDtypeStruct((rank, width), BF16)

    packed, mark, resident, own, *parts = pl.pallas_call(
        functools.partial(lift_kernel, helpers),
        out_shape=[
            jax.ShapeDtypeStruct((count * width // LANES + TILE, LANES), BF16),
            jax.ShapeDtypeStruct((1, own_points), jnp.int32),
            jax.ShapeDtypeStruct((8, LANES), F32),
            block,
            block,
        ]
        + [sent] * (helpers - 2),
        in_specs=[HBM] * 6,
        scratch_shapes=[
            pltpu.VMEM((2, count), jnp.int32),
            pltpu.VMEM((2, count), jnp.int32),
            pltpu.VMEM(point_cluster.shape, jnp.int32),
            pltpu.VMEM(test_matrix.shape, BF16),
            pltpu.VMEM(points.shape, BF16),
            pltpu.SemaphoreType.DMA((4 + CHUNKS + width // LANES,)),
        ],
        compiler_params=PARAMS,
        name="lift",
    )(*[in_hbm(a) for a in (queries, probe_group.T, probe_local.T, point_cluster, test_matrix, points)])
    lifter = pl.pallas_call(
        join_kernel,
        out_shape=sent,
        compiler_params=PARAMS,
        cost_estimate=pl.CostEstimate(flops=4 * 10**9, bytes_accessed=10**5, transcendentals=0),
        name="join",
    )(own, *swaps(parts, "help"))
    lifters = [lifter] + [swap(lifter, "shard", INNER * d) for d in range(1, planes)]
    mine = pl.pallas_call(
        stack_kernel,
        out_shape=jax.ShapeDtypeStruct((planes * rank, width), BF16),
        compiler_params=PARAMS,
        cost_estimate=pl.CostEstimate(flops=35*10**8, bytes_accessed=10**5, transcendentals=0),
        name="stack",
    )(*lifters)
    theirs = swap(mine, "help", 1)

    index, axes = range(groups * helpers), ("shard", "help")
    one = [(i, i ^ (2 if i % 2 == 0 else helpers)) for i in index]
    two = [(i, i ^ (helpers if i % 2 == 0 else 2)) for i in index]
    far = lax.ppermute(packed, axes, one)
    (near,) = gate([lax.ppermute(packed, axes, two)], lifters[-1])
    across = lax.ppermute(near, axes, one)

    wide = width + LANES
    begun = pl.pallas_call(
        functools.partial(score_kernel, planes, helpers, 3),
        out_shape=jax.ShapeDtypeStruct((2 * planes * rank, wide), F32),
        compiler_params=PARAMS,
        name="score",
    )(mine, theirs, packed, near, far)
    moments, passed = pl.pallas_call(
        functools.partial(score_kernel, planes, helpers, 1),
        out_shape=[jax.ShapeDtypeStruct((planes * rank, wide), F32)] * 2,
        compiler_params=PARAMS,
        name="score_last",
    )(mine, theirs, across, begun)
    folded = pl.pallas_call(
        functools.partial(fold_kernel, planes),
        out_shape=[jax.ShapeDtypeStruct((rank, wide), F32)]
        + [jax.ShapeDtypeStruct((rank * width // LANES + TILE, LANES), BF16)] * (planes - 1),
        compiler_params=PARAMS,
        name="fold",
    )(moments, swap(passed, "help", 1))
    moments = [folded[0]] + swaps(folded[1:], "shard", INNER)

    scaled = pl.pallas_call(
        scale_kernel,
        out_shape=jax.ShapeDtypeStruct((rank, width), BF16),
        compiler_params=PARAMS,
        name="scale",
    )(resident, *moments)
    scaled = [scaled] + [swap(scaled, "help", d) for d in range(1, helpers)]

    sketch, regressor, *parts = pl.pallas_call(
        functools.partial(sketch_kernel, helpers),
        out_shape=[jax.ShapeDtypeStruct((rank, own_points), F32), block, block] + [sent] * (helpers - 2),
        out_specs=[HBM] + [VMEM] * helpers,
        scratch_shapes=[pltpu.VMEM((rank, own_points), F32), pltpu.SemaphoreType.DMA],
        compiler_params=PARAMS,
        name="sketch",
    )(mark, resident, points, *scaled)
    for part in swaps(parts, "help"):
        regressor = regressor + part.astype(F32)
    return sketch, regressor[None]


def solution(mesh):
    in_specs = (
        P(("shard", "help"), None),
        P(("shard", "help"), None),
        P(("shard", "help"), None),
        P(("shard", "help"), None),
        P("shard", None),
        P(None, ("shard", "help")),
    )
    out_specs = (P(None, ("shard", "help")), P(("shard", "help"), None, None))
    return jax.shard_map(shards, mesh=mesh, in_specs=in_specs, out_specs=out_specs, check_vma=False)
```

```python
import functools

import jax
import jax.numpy as jnp
from jax import lax
from jax.experimental import pallas as pl
from jax.experimental.pallas import tpu as pltpu
from jax.sharding import PartitionSpec as P

F32 = jnp.float32
BF16 = jnp.bfloat16
LANES = 128
TILE = 16
CHUNKS = 4
INNER = 2

ANY = pl.BlockSpec(memory_space=pl.ANY)
VMEM = pl.BlockSpec(memory_space=pltpu.VMEM)
VMEM = pl.BlockSpec(memory_space=pltpu.VMEM)
HBM = pl.BlockSpec(memory_space=pltpu.HBM)
PARAMS = pltpu.CompilerParams(vmem_limit_bytes=32 * 1024 * 1024)


def in_hbm(value):
    return pltpu.with_memory_space_constraint(value, pltpu.HBM)


def contract(a, b, dims):
    return lax.dot_general(a, b, (dims, ((), ())), preferred_element_type=F32)


def halves(value):
    high = value.astype(BF16)
    return high, (value - high.astype(F32)).astype(BF16)


def slabs(ref, rows, width):
    return jnp.concatenate([ref[k * rows : (k + 1) * rows, :] for k in range(width // LANES)], axis=1)


def lift_kernel(helpers, *refs):
    rows_hbm, group_hbm, local_hbm, ids_hbm, test_hbm, points_hbm = refs[:6]
    packed_ref, mark_ref, resident_ref = refs[6:9]
    outs = refs[9 : 9 + helpers]
    group_ref, local_ref, ids_ref, test_ref, points_ref, sems = refs[9 + helpers :]
    helper = lax.axis_index("help")
    asked, width = rows_hbm.shape
    rank, count = test_ref.shape
    piece = count // CHUNKS
    pairs = [(ids_hbm, ids_ref), (test_hbm, test_ref)]
    for k in range(CHUNKS):
        part = pl.ds(k * piece, piece)
        pairs.append((points_hbm.at[part], points_ref.at[part]))
    pairs += [(group_hbm, group_ref), (local_hbm, local_ref)]
    for k in range(width // LANES):
        pairs.append((rows_hbm.at[:, pl.ds(k * LANES, LANES)], packed_ref.at[pl.ds(k * asked, asked)]))
    copies = [pltpu.make_async_copy(*pair, sems.at[k]) for k, pair in enumerate(pairs)]
    for copy in copies:
        copy.start()
    copies[0].wait()
    everyone = ids_ref[...]
    mark = ids_ref[:, pl.ds(pl.multiple_of(helper * count, LANES), count)] ^ helper
    mark_ref[...] = mark
    for d in range(helpers):
        many = jnp.sum((everyone == (helper ^ d)).astype(F32), axis=1, keepdims=True)
        resident_ref[d : d + 1, :] = jnp.broadcast_to(many, (1, LANES))
    copies[1].wait()
    test = test_ref[...]
    rows = jnp.concatenate([jnp.where(mark == d, test, jnp.zeros((), BF16)) for d in range(helpers)], axis=0)
    total = None
    for k in range(CHUNKS):
        copies[2 + k].wait()
        part = slice(k * piece, (k + 1) * piece)
        more = contract(rows[:, part], points_ref[part, :], ((1,), (0,)))
        total = more if total is None else total + more
    for d, out in enumerate(outs):
        out[...] = total[d * rank : (d + 1) * rank].astype(out.dtype)
    for copy in copies[2 + CHUNKS :]:
        copy.wait()
    cluster = (group_ref[...] * helpers + local_ref[...]).astype(F32)
    line = [cluster[k : k + 1, j : j + LANES] for k in (0, 1) for j in range(0, asked, LANES)]
    line.append(jnp.zeros((TILE - len(line), LANES), F32))
    packed_ref[asked * width // LANES :, :] = jnp.concatenate(line, axis=0).astype(BF16)


def join_kernel(*refs):
    *parts, out = refs
    total = parts[0][...]
    for part in parts[1:]:
        total = total + part[...].astype(F32)
    out[...] = total.astype(out.dtype)


def stack_kernel(*refs):
    *parts, _, out = refs
    rank = parts[0].shape[0]
    for k, part in enumerate(parts):
        out[k * rank : (k + 1) * rank, :] = part[...]


def gate_kernel(*refs):
    pass


def gate(values, *others):
    return pl.pallas_call(
        gate_kernel,
        out_shape=[jax.ShapeDtypeStruct(value.shape, value.dtype) for value in values],
        in_specs=[ANY] * (len(values) + len(others)),
        out_specs=[ANY] * len(values),
        input_output_aliases={k: k for k in range(len(values))},
        compiler_params=pltpu.CompilerParams(vmem_limit_bytes=1 << 20),
        cost_estimate=pl.CostEstimate(flops=5 * 10**9, bytes_accessed=10**5, transcendentals=0),
        name="gate",
    )(*values, *others)


def score_kernel(planes, helpers, blocks, mine_ref, theirs_ref, *refs):
    queries, rest = refs[:blocks], refs[blocks:]
    shard, helper = lax.axis_index("shard"), lax.axis_index("help")
    span, width = mine_ref.shape
    rank = span // planes
    count = (queries[0].shape[0] - TILE) * LANES // width
    pieces = count // LANES
    lifter = jnp.concatenate([mine_ref[...], theirs_ref[...]], axis=0)
    clusters = [
        ((shard ^ (INNER * d)) * helpers + (helper ^ side)).astype(F32) for side in (0, 1) for d in range(planes)
    ]
    total, tally = None, [None] * len(clusters)
    for q_ref in queries:
        rows = slabs(q_ref, count, width)
        tile = q_ref[count * width // LANES :, :].astype(F32)
        first, second = (
            jnp.concatenate([tile[k * pieces + j : k * pieces + j + 1] for j in range(pieces)], axis=1) for k in (0, 1)
        )
        lifted = contract(lifter, rows, ((1,), (1,)))
        kept = []
        for k, cluster in enumerate(clusters):
            hit = (first == cluster) | (second == cluster)
            kept.append(jnp.where(hit, lifted[k * rank : (k + 1) * rank], 0.0))
            here = hit.astype(F32)
            tally[k] = here if tally[k] is None else tally[k] + here
        high, low = halves(jnp.concatenate(kept, axis=0))
        part = contract(high, rows, ((1,), (0,))) + contract(low, rows, ((1,), (0,)))
        total = part if total is None else total + part
    named = jnp.concatenate(
        [jnp.broadcast_to(jnp.sum(t, axis=1, keepdims=True), (rank, LANES)) for t in tally], axis=0
    )
    if len(rest) == 1:
        rest[0][:, :width] = total
        rest[0][:, width:] = named
    else:
        before, *outs = rest
        for side, out in enumerate(outs):
            part = slice(side * span, (side + 1) * span)
            out[:, :width] = before[part, :width] + total[part]
            out[:, width:] = before[part, width:] + named[part]


def fold_kernel(planes, mine_ref, theirs_ref, own_ref, *send_refs):
    rank, wide = own_ref.shape
    width = wide - LANES
    line = lax.broadcasted_iota(jnp.int32, (TILE, LANES), 0)
    for d in range(planes):
        part = slice(d * rank, (d + 1) * rank)
        total = mine_ref[part, :] + theirs_ref[part, :]
        if d == 0:
            own_ref[...] = total
        else:
            ref = send_refs[d - 1]
            for k in range(width // LANES):
                ref[k * rank : (k + 1) * rank, :] = total[:, k * LANES : (k + 1) * LANES].astype(BF16)
            named = total[:TILE, width:]
            many = jnp.floor(named * (1.0 / 256.0))
            rest = named - 256.0 * many
            ref[rank * width // LANES :, :] = jnp.where(line == 0, many, jnp.where(line == 1, rest, 0.0)).astype(BF16)


def scale_kernel(resident_ref, own_ref, *refs):
    *parts, out_ref = refs
    rank, width = out_ref.shape
    total = own_ref[:, :width]
    queried = own_ref[0:1, width : width + 1]
    for part in parts:
        total = total + slabs(part, rank, width).astype(F32)
        tile = part[rank * width // LANES :, :].astype(F32)
        queried = queried + 256.0 * tile[0:1, 0:1] + tile[1:2, 0:1]
    resident = resident_ref[0:1, 0:1]
    factor = lax.rsqrt((queried + 1.0) * (queried + resident)) * (1.0 / width)
    out_ref[...] = (total * factor).astype(out_ref.dtype)


def sketch_kernel(helpers, mark_ref, resident_ref, points_ref, *refs):
    scaled, sketch_hbm, outs = refs[:helpers], refs[helpers], refs[helpers + 1 : -2]
    sketch_ref, sem = refs[-2:]
    rank, count = sketch_ref.shape
    mark = mark_ref[...]
    points = points_ref[...]
    product = contract(jnp.concatenate([s[...] for s in scaled], axis=0), points, ((1,), (1,)))
    sketch = product[:rank]
    for d in range(1, helpers):
        sketch = jnp.where(mark == d, product[d * rank : (d + 1) * rank], sketch)
    sketch_ref[...] = sketch
    leaving = pltpu.make_async_copy(sketch_ref, sketch_hbm, sem)
    leaving.start()
    rounded = sketch.astype(BF16)
    rows = [jnp.where(mark == d, rounded, jnp.zeros((), BF16)) for d in range(helpers)]
    summed = contract(jnp.concatenate(rows, axis=0), points, ((1,), (0,)))
    for d, out in enumerate(outs):
        block = summed[d * rank : (d + 1) * rank] * lax.rsqrt(resident_ref[d : d + 1, 0:1])
        out[...] = block.astype(out.dtype)
    leaving.wait()


def swap(value, axis, d):
    return lax.ppermute(value, axis, [(i, i ^ d) for i in range(lax.axis_size(axis))])


def swaps(values, axis, unit=1):
    return [swap(value, axis, unit * d) for d, value in reversed([*enumerate(values, 1)])]


def shards(queries, probe_group, probe_local, points, point_cluster, test_matrix):
    groups = lax.axis_size("shard")
    helpers = lax.axis_size("help")
    planes = groups // INNER
    count = queries.shape[0]
    rank = test_matrix.shape[0]
    own_points, width = points.shape
    block = jax.ShapeDtypeStruct((rank, width), F32)
    sent = jax.ShapeDtypeStruct((rank, width), BF16)

    packed, mark, resident, own, *parts = pl.pallas_call(
        functools.partial(lift_kernel, helpers),
        out_shape=[
            jax.ShapeDtypeStruct((count * width // LANES + TILE, LANES), BF16),
            jax.ShapeDtypeStruct((1, own_points), jnp.int32),
            jax.ShapeDtypeStruct((8, LANES), F32),
            block,
            block,
        ]
        + [sent] * (helpers - 2),
        in_specs=[HBM] * 6,
        scratch_shapes=[
            pltpu.VMEM((2, count), jnp.int32),
            pltpu.VMEM((2, count), jnp.int32),
            pltpu.VMEM(point_cluster.shape, jnp.int32),
            pltpu.VMEM(test_matrix.shape, BF16),
            pltpu.VMEM(points.shape, BF16),
            pltpu.SemaphoreType.DMA((4 + CHUNKS + width // LANES,)),
        ],
        compiler_params=PARAMS,
        name="lift",
    )(*[in_hbm(a) for a in (queries, probe_group.T, probe_local.T, point_cluster, test_matrix, points)])
    lifter = pl.pallas_call(
        join_kernel,
        out_shape=sent,
        compiler_params=PARAMS,
        cost_estimate=pl.CostEstimate(flops=4 * 10**9, bytes_accessed=10**5, transcendentals=0),
        name="join",
    )(own, *swaps(parts, "help"))
    lifters = [lifter] + [swap(lifter, "shard", INNER * d) for d in range(1, planes)]
    index, axes = range(groups * helpers), ("shard", "help")
    one = [(i, i ^ (2 if i % 2 == 0 else helpers)) for i in index]
    two = [(i, i ^ (helpers if i % 2 == 0 else 2)) for i in index]
    far = lax.ppermute(packed, axes, one)
    (near,) = gate([lax.ppermute(packed, axes, two)], lifters[-1])
    across = lax.ppermute(near, axes, one)

    mine = pl.pallas_call(
        stack_kernel,
        out_shape=jax.ShapeDtypeStruct((planes * rank, width), BF16),
        in_specs=[VMEM] * planes + [ANY],
        compiler_params=PARAMS,
        cost_estimate=pl.CostEstimate(flops=25 * 10**8, bytes_accessed=10**5, transcendentals=0),
        name="stack",
    )(*lifters, far)
    theirs = swap(mine, "help", 1)

    wide = width + LANES
    begun = pl.pallas_call(
        functools.partial(score_kernel, planes, helpers, 3),
        out_shape=jax.ShapeDtypeStruct((2 * planes * rank, wide), F32),
        compiler_params=PARAMS,
        name="score",
    )(mine, theirs, packed, near, far)
    moments, passed = pl.pallas_call(
        functools.partial(score_kernel, planes, helpers, 1),
        out_shape=[jax.ShapeDtypeStruct((planes * rank, wide), F32)] * 2,
        compiler_params=PARAMS,
        name="score_last",
    )(mine, theirs, across, begun)
    folded = pl.pallas_call(
        functools.partial(fold_kernel, planes),
        out_shape=[jax.ShapeDtypeStruct((rank, wide), F32)]
        + [jax.ShapeDtypeStruct((rank * width // LANES + TILE, LANES), BF16)] * (planes - 1),
        compiler_params=PARAMS,
        name="fold",
    )(moments, swap(passed, "help", 1))
    moments = [folded[0]] + swaps(folded[1:], "shard", INNER)

    scaled = pl.pallas_call(
        scale_kernel,
        out_shape=jax.ShapeDtypeStruct((rank, width), BF16),
        compiler_params=PARAMS,
        name="scale",
    )(resident, *moments)
    scaled = [scaled] + [swap(scaled, "help", d) for d in range(1, helpers)]

    sketch, regressor, *parts = pl.pallas_call(
        functools.partial(sketch_kernel, helpers),
        out_shape=[jax.ShapeDtypeStruct((rank, own_points), F32), block, block] + [sent] * (helpers - 2),
        out_specs=[HBM] + [VMEM] * helpers,
        scratch_shapes=[pltpu.VMEM((rank, own_points), F32), pltpu.SemaphoreType.DMA],
        compiler_params=PARAMS,
        name="sketch",
    )(mark, resident, points, *scaled)
    for part in swaps(parts, "help"):
        regressor = regressor + part.astype(F32)
    return sketch, regressor[None]


def solution(mesh):
    in_specs = (
        P(("shard", "help"), None),
        P(("shard", "help"), None),
        P(("shard", "help"), None),
        P(("shard", "help"), None),
        P("shard", None),
        P(None, ("shard", "help")),
    )
    out_specs = (P(None, ("shard", "help")), P(("shard", "help"), None, None))
    return jax.shard_map(shards, mesh=mesh, in_specs=in_specs, out_specs=out_specs, check_vma=False)
```

```python
import functools

import jax
import jax.numpy as jnp
from jax import lax
from jax.experimental import pallas as pl
from jax.experimental.pallas import tpu as pltpu
from jax.sharding import PartitionSpec as P

F32 = jnp.float32
BF16 = jnp.bfloat16
LANES = 128
TILE = 16
CHUNKS = 4
INNER = 2

ANY = pl.BlockSpec(memory_space=pl.ANY)
VMEM = pl.BlockSpec(memory_space=pltpu.VMEM)
VMEM = pl.BlockSpec(memory_space=pltpu.VMEM)
HBM = pl.BlockSpec(memory_space=pltpu.HBM)
PARAMS = pltpu.CompilerParams(vmem_limit_bytes=32 * 1024 * 1024)


def in_hbm(value):
    return pltpu.with_memory_space_constraint(value, pltpu.HBM)


def contract(a, b, dims):
    return lax.dot_general(a, b, (dims, ((), ())), preferred_element_type=F32)


def halves(value):
    high = value.astype(BF16)
    return high, (value - high.astype(F32)).astype(BF16)


def slabs(ref, rows, width):
    return jnp.concatenate([ref[k * rows : (k + 1) * rows, :] for k in range(width // LANES)], axis=1)


def lift_kernel(helpers, *refs):
    rows_hbm, group_hbm, local_hbm, ids_hbm, test_hbm, points_hbm = refs[:6]
    packed_ref, mark_ref, resident_ref = refs[6:9]
    outs = refs[9 : 9 + helpers]
    group_ref, local_ref, ids_ref, test_ref, points_ref, sems = refs[9 + helpers :]
    helper = lax.axis_index("help")
    asked, width = rows_hbm.shape
    rank, count = test_ref.shape
    piece = count // CHUNKS
    pairs = [(ids_hbm, ids_ref), (test_hbm, test_ref)]
    for k in range(CHUNKS):
        part = pl.ds(k * piece, piece)
        pairs.append((points_hbm.at[part], points_ref.at[part]))
    pairs += [(group_hbm, group_ref), (local_hbm, local_ref)]
    for k in range(width // LANES):
        pairs.append((rows_hbm.at[:, pl.ds(k * LANES, LANES)], packed_ref.at[pl.ds(k * asked, asked)]))
    copies = [pltpu.make_async_copy(*pair, sems.at[k]) for k, pair in enumerate(pairs)]
    for copy in copies:
        copy.start()
    copies[0].wait()
    everyone = ids_ref[...]
    mark = ids_ref[:, pl.ds(pl.multiple_of(helper * count, LANES), count)] ^ helper
    mark_ref[...] = mark
    for d in range(helpers):
        many = jnp.sum((everyone == (helper ^ d)).astype(F32), axis=1, keepdims=True)
        resident_ref[d : d + 1, :] = jnp.broadcast_to(many, (1, LANES))
    copies[1].wait()
    test = test_ref[...]
    rows = jnp.concatenate([jnp.where(mark == d, test, jnp.zeros((), BF16)) for d in range(helpers)], axis=0)
    total = None
    for k in range(CHUNKS):
        copies[2 + k].wait()
        part = slice(k * piece, (k + 1) * piece)
        more = contract(rows[:, part], points_ref[part, :], ((1,), (0,)))
        total = more if total is None else total + more
    for d, out in enumerate(outs):
        out[...] = total[d * rank : (d + 1) * rank].astype(out.dtype)
    for copy in copies[2 + CHUNKS :]:
        copy.wait()
    cluster = (group_ref[...] * helpers + local_ref[...]).astype(F32)
    line = [cluster[k : k + 1, j : j + LANES] for k in (0, 1) for j in range(0, asked, LANES)]
    line.append(jnp.zeros((TILE - len(line), LANES), F32))
    packed_ref[asked * width // LANES :, :] = jnp.concatenate(line, axis=0).astype(BF16)


def join_kernel(*refs):
    *parts, out = refs
    total = parts[0][...]
    for part in parts[1:]:
        total = total + part[...].astype(F32)
    out[...] = total.astype(out.dtype)


def stack_kernel(*refs):
    *parts, _, out = refs
    rank = parts[0].shape[0]
    for k, part in enumerate(parts):
        out[k * rank : (k + 1) * rank, :] = part[...]


def gate_kernel(*refs):
    pass


def gate(values, *others):
    return pl.pallas_call(
        gate_kernel,
        out_shape=[jax.ShapeDtypeStruct(value.shape, value.dtype) for value in values],
        in_specs=[ANY] * (len(values) + len(others)),
        out_specs=[ANY] * len(values),
        input_output_aliases={k: k for k in range(len(values))},
        compiler_params=pltpu.CompilerParams(vmem_limit_bytes=1 << 20),
        cost_estimate=pl.CostEstimate(flops=5 * 10**9, bytes_accessed=10**5, transcendentals=0),
        name="gate",
    )(*values, *others)


def score_kernel(planes, helpers, blocks, mine_ref, theirs_ref, *refs):
    queries, rest = refs[:blocks], refs[blocks:]
    shard, helper = lax.axis_index("shard"), lax.axis_index("help")
    span, width = mine_ref.shape
    rank = span // planes
    count = (queries[0].shape[0] - TILE) * LANES // width
    pieces = count // LANES
    lifter = jnp.concatenate([mine_ref[...], theirs_ref[...]], axis=0)
    clusters = [
        ((shard ^ (INNER * d)) * helpers + (helper ^ side)).astype(F32) for side in (0, 1) for d in range(planes)
    ]
    total, tally = None, [None] * len(clusters)
    for q_ref in queries:
        rows = slabs(q_ref, count, width)
        tile = q_ref[count * width // LANES :, :].astype(F32)
        first, second = (
            jnp.concatenate([tile[k * pieces + j : k * pieces + j + 1] for j in range(pieces)], axis=1) for k in (0, 1)
        )
        lifted = contract(lifter, rows, ((1,), (1,)))
        kept = []
        for k, cluster in enumerate(clusters):
            hit = (first == cluster) | (second == cluster)
            kept.append(jnp.where(hit, lifted[k * rank : (k + 1) * rank], 0.0))
            here = hit.astype(F32)
            tally[k] = here if tally[k] is None else tally[k] + here
        high, low = halves(jnp.concatenate(kept, axis=0))
        part = contract(high, rows, ((1,), (0,)))
        if blocks > 1:
            part = part + contract(low, rows, ((1,), (0,)))
        total = part if total is None else total + part
    named = jnp.concatenate(
        [jnp.broadcast_to(jnp.sum(t, axis=1, keepdims=True), (rank, LANES)) for t in tally], axis=0
    )
    if len(rest) == 1:
        rest[0][:, :width] = total
        rest[0][:, width:] = named
    else:
        before, *outs = rest
        for side, out in enumerate(outs):
            part = slice(side * span, (side + 1) * span)
            out[:, :width] = (before[part, :width] + total[part]).astype(out.dtype)
            counts = before[part, width:] + named[part]
            out[:, width:] = (counts if out.dtype == F32 else digits(counts)).astype(out.dtype)


def digits(counts):
    high = jnp.floor(counts * (1.0 / 256.0))
    line = lax.broadcasted_iota(jnp.int32, counts.shape, 0)
    return jnp.where(line % 2 == 0, high, counts - 256.0 * high)


def fold_kernel(planes, mine_ref, theirs_ref, own_ref, *send_refs):
    rank, wide = own_ref.shape
    width = wide - LANES
    for d in range(planes):
        part = slice(d * rank, (d + 1) * rank)
        theirs = theirs_ref[part, :].astype(F32)
        total = mine_ref[part, :width] + theirs[:, :width]
        named = mine_ref[part, width:] + 256.0 * theirs[0:1, width:] + theirs[1:2, width:]
        if d == 0:
            own_ref[:, :width] = total
            own_ref[:, width:] = named
        else:
            ref = send_refs[d - 1]
            for k in range(width // LANES):
                ref[k * rank : (k + 1) * rank, :] = total[:, k * LANES : (k + 1) * LANES].astype(BF16)
            ref[rank * width // LANES :, :] = digits(named[:TILE]).astype(BF16)


def scale_kernel(resident_ref, own_ref, *refs):
    *parts, wide_ref, out_ref = refs
    rank, width = out_ref.shape
    total = own_ref[:, :width]
    queried = own_ref[0:1, width : width + 1]
    for part in parts:
        total = total + slabs(part, rank, width).astype(F32)
        tile = part[rank * width // LANES :, :].astype(F32)
        queried = queried + 256.0 * tile[0:1, 0:1] + tile[1:2, 0:1]
    resident = resident_ref[0:1, 0:1]
    factor = lax.rsqrt((queried + 1.0) * (queried + resident)) * (1.0 / width)
    wide_ref[...] = total * factor
    out_ref[...] = (total * factor).astype(BF16)


def sketch_kernel(helpers, mark_ref, resident_ref, points_ref, *refs):
    scaled, sketch_hbm, outs = refs[:helpers], refs[helpers], refs[helpers + 1 : -2]
    sketch_ref, sem = refs[-2:]
    rank, count = sketch_ref.shape
    mark = mark_ref[...]
    points = points_ref[...]
    blocks, rests = [], []
    for s in scaled:
        if s.dtype == F32:
            high, low = halves(s[...])
            blocks.append(high)
            rests.append(low)
        else:
            blocks.append(s[...])
    product = contract(jnp.concatenate(blocks + rests, axis=0), points, ((1,), (1,)))
    whole = [product[k * rank : (k + 1) * rank] for k in range(helpers)]
    for k in range(len(rests)):
        whole[k] = whole[k] + product[(helpers + k) * rank : (helpers + k + 1) * rank]
    sketch = whole[0]
    for d in range(1, helpers):
        sketch = jnp.where(mark == d, whole[d], sketch)
    sketch_ref[...] = sketch
    leaving = pltpu.make_async_copy(sketch_ref, sketch_hbm, sem)
    leaving.start()
    rounded = sketch.astype(BF16)
    rows = [jnp.where(mark == d, rounded, jnp.zeros((), BF16)) for d in range(helpers)]
    summed = contract(jnp.concatenate(rows, axis=0), points, ((1,), (0,)))
    for d, out in enumerate(outs):
        block = summed[d * rank : (d + 1) * rank] * lax.rsqrt(resident_ref[d : d + 1, 0:1])
        out[...] = block.astype(out.dtype)
    leaving.wait()


def swap(value, axis, d):
    return lax.ppermute(value, axis, [(i, i ^ d) for i in range(lax.axis_size(axis))])


def swaps(values, axis, unit=1):
    return [swap(value, axis, unit * d) for d, value in reversed([*enumerate(values, 1)])]


def shards(queries, probe_group, probe_local, points, point_cluster, test_matrix):
    groups = lax.axis_size("shard")
    helpers = lax.axis_size("help")
    planes = groups // INNER
    count = queries.shape[0]
    rank = test_matrix.shape[0]
    own_points, width = points.shape
    block = jax.ShapeDtypeStruct((rank, width), F32)
    sent = jax.ShapeDtypeStruct((rank, width), BF16)

    packed, mark, resident, own, *parts = pl.pallas_call(
        functools.partial(lift_kernel, helpers),
        out_shape=[
            jax.ShapeDtypeStruct((count * width // LANES + TILE, LANES), BF16),
            jax.ShapeDtypeStruct((1, own_points), jnp.int32),
            jax.ShapeDtypeStruct((8, LANES), F32),
            block,
            block,
        ]
        + [sent] * (helpers - 2),
        in_specs=[HBM] * 6,
        scratch_shapes=[
            pltpu.VMEM((2, count), jnp.int32),
            pltpu.VMEM((2, count), jnp.int32),
            pltpu.VMEM(point_cluster.shape, jnp.int32),
            pltpu.VMEM(test_matrix.shape, BF16),
            pltpu.VMEM(points.shape, BF16),
            pltpu.SemaphoreType.DMA((4 + CHUNKS + width // LANES,)),
        ],
        compiler_params=PARAMS,
        name="lift",
    )(*[in_hbm(a) for a in (queries, probe_group.T, probe_local.T, point_cluster, test_matrix, points)])
    lifter = pl.pallas_call(
        join_kernel,
        out_shape=sent,
        compiler_params=PARAMS,
        cost_estimate=pl.CostEstimate(flops=40*10**8, bytes_accessed=10**5, transcendentals=0),
        name="join",
    )(own, *swaps(parts, "help"))
    lifters = [lifter] + [swap(lifter, "shard", INNER * d) for d in range(1, planes)]
    index, axes = range(groups * helpers), ("shard", "help")
    one = [(i, i ^ (2 if i % 2 == 0 else helpers)) for i in index]
    two = [(i, i ^ (helpers if i % 2 == 0 else 2)) for i in index]
    far = lax.ppermute(packed, axes, one)
    (near,) = gate([lax.ppermute(packed, axes, two)], lifters[-1])
    across = lax.ppermute(near, axes, one)

    mine = pl.pallas_call(
        stack_kernel,
        out_shape=jax.ShapeDtypeStruct((planes * rank, width), BF16),
        in_specs=[VMEM] * planes + [ANY],
        compiler_params=PARAMS,
        cost_estimate=pl.CostEstimate(flops=25 * 10**8, bytes_accessed=10**5, transcendentals=0),
        name="stack",
    )(*lifters, far)
    theirs = swap(mine, "help", 1)

    wide = width + LANES
    begun = pl.pallas_call(
        functools.partial(score_kernel, planes, helpers, 3),
        out_shape=jax.ShapeDtypeStruct((2 * planes * rank, wide), F32),
        compiler_params=PARAMS,
        name="score",
    )(mine, theirs, packed, near, far)
    moments, passed = pl.pallas_call(
        functools.partial(score_kernel, planes, helpers, 1),
        out_shape=[jax.ShapeDtypeStruct((planes * rank, wide), kind) for kind in (F32, BF16)],
        compiler_params=PARAMS,
        name="score_last",
    )(mine, theirs, across, begun)
    folded = pl.pallas_call(
        functools.partial(fold_kernel, planes),
        out_shape=[jax.ShapeDtypeStruct((rank, wide), F32)]
        + [jax.ShapeDtypeStruct((rank * width // LANES + TILE, LANES), BF16)] * (planes - 1),
        compiler_params=PARAMS,
        name="fold",
    )(moments, swap(passed, "help", 1))
    moments = [folded[0]] + swaps(folded[1:], "shard", INNER)

    exact, scaled = pl.pallas_call(
        scale_kernel,
        out_shape=[block, sent],
        compiler_params=PARAMS,
        name="scale",
    )(resident, *moments)
    scaled = [exact, swap(exact, "help", 1)] + [swap(scaled, "help", d) for d in range(2, helpers)]

    sketch, regressor, *parts = pl.pallas_call(
        functools.partial(sketch_kernel, helpers),
        out_shape=[jax.ShapeDtypeStruct((rank, own_points), F32), block, block] + [sent] * (helpers - 2),
        out_specs=[HBM] + [VMEM] * helpers,
        scratch_shapes=[pltpu.VMEM((rank, own_points), F32), pltpu.SemaphoreType.DMA],
        compiler_params=PARAMS,
        name="sketch",
    )(mark, resident, points, *scaled)
    for part in swaps(parts, "help"):
        regressor = regressor + part.astype(F32)
    return sketch, regressor[None]


def solution(mesh):
    in_specs = (
        P(("shard", "help"), None),
        P(("shard", "help"), None),
        P(("shard", "help"), None),
        P(("shard", "help"), None),
        P("shard", None),
        P(None, ("shard", "help")),
    )
    out_specs = (P(None, ("shard", "help")), P(("shard", "help"), None, None))
    return jax.shard_map(shards, mesh=mesh, in_specs=in_specs, out_specs=out_specs, check_vma=False)
```

```python
import functools

import jax
import jax.numpy as jnp
from jax import lax
from jax.experimental import pallas as pl
from jax.experimental.pallas import tpu as pltpu
from jax.sharding import PartitionSpec as P

F32 = jnp.float32
BF16 = jnp.bfloat16
LANES = 128
TILE = 16
CHUNKS = 4
INNER = 2

ANY = pl.BlockSpec(memory_space=pl.ANY)
VMEM = pl.BlockSpec(memory_space=pltpu.VMEM)
VMEM = pl.BlockSpec(memory_space=pltpu.VMEM)
HBM = pl.BlockSpec(memory_space=pltpu.HBM)
PARAMS = pltpu.CompilerParams(vmem_limit_bytes=32 * 1024 * 1024)


def in_hbm(value):
    return pltpu.with_memory_space_constraint(value, pltpu.HBM)


def contract(a, b, dims):
    return lax.dot_general(a, b, (dims, ((), ())), preferred_element_type=F32)


def halves(value):
    high = value.astype(BF16)
    return high, (value - high.astype(F32)).astype(BF16)


def slabs(ref, rows, width):
    return jnp.concatenate([ref[k * rows : (k + 1) * rows, :] for k in range(width // LANES)], axis=1)


def lift_kernel(helpers, *refs):
    rows_hbm, group_hbm, local_hbm, ids_hbm, test_hbm, points_hbm = refs[:6]
    packed_ref, mark_ref, resident_ref = refs[6:9]
    outs = refs[9 : 9 + helpers]
    group_ref, local_ref, ids_ref, test_ref, points_ref, sems = refs[9 + helpers :]
    helper = lax.axis_index("help")
    asked, width = rows_hbm.shape
    rank, count = test_ref.shape
    piece = count // CHUNKS
    pairs = [(ids_hbm, ids_ref), (test_hbm, test_ref)]
    for k in range(CHUNKS):
        part = pl.ds(k * piece, piece)
        pairs.append((points_hbm.at[part], points_ref.at[part]))
    pairs += [(group_hbm, group_ref), (local_hbm, local_ref)]
    for k in range(width // LANES):
        pairs.append((rows_hbm.at[:, pl.ds(k * LANES, LANES)], packed_ref.at[pl.ds(k * asked, asked)]))
    copies = [pltpu.make_async_copy(*pair, sems.at[k]) for k, pair in enumerate(pairs)]
    for copy in copies:
        copy.start()
    copies[0].wait()
    everyone = ids_ref[...]
    mark = ids_ref[:, pl.ds(pl.multiple_of(helper * count, LANES), count)] ^ helper
    mark_ref[...] = mark
    for d in range(helpers):
        many = jnp.sum((everyone == (helper ^ d)).astype(F32), axis=1, keepdims=True)
        resident_ref[d : d + 1, :] = jnp.broadcast_to(many, (1, LANES))
    copies[1].wait()
    test = test_ref[...]
    rows = jnp.concatenate([jnp.where(mark == d, test, jnp.zeros((), BF16)) for d in range(helpers)], axis=0)
    total = None
    for k in range(CHUNKS):
        copies[2 + k].wait()
        part = slice(k * piece, (k + 1) * piece)
        more = contract(rows[:, part], points_ref[part, :], ((1,), (0,)))
        total = more if total is None else total + more
    for d, out in enumerate(outs):
        out[...] = total[d * rank : (d + 1) * rank].astype(out.dtype)
    for copy in copies[2 + CHUNKS :]:
        copy.wait()
    cluster = (group_ref[...] * helpers + local_ref[...]).astype(F32)
    line = [cluster[k : k + 1, j : j + LANES] for k in (0, 1) for j in range(0, asked, LANES)]
    line.append(jnp.zeros((TILE - len(line), LANES), F32))
    packed_ref[asked * width // LANES :, :] = jnp.concatenate(line, axis=0).astype(BF16)


def join_kernel(*refs):
    *parts, out = refs
    total = parts[0][...]
    for part in parts[1:]:
        total = total + part[...].astype(F32)
    out[...] = total.astype(out.dtype)


def stack_kernel(*refs):
    *parts, _, out = refs
    rank = parts[0].shape[0]
    for k, part in enumerate(parts):
        out[k * rank : (k + 1) * rank, :] = part[...]


def gate_kernel(*refs):
    pass


def gate(values, *others):
    return pl.pallas_call(
        gate_kernel,
        out_shape=[jax.ShapeDtypeStruct(value.shape, value.dtype) for value in values],
        in_specs=[ANY] * (len(values) + len(others)),
        out_specs=[ANY] * len(values),
        input_output_aliases={k: k for k in range(len(values))},
        compiler_params=pltpu.CompilerParams(vmem_limit_bytes=1 << 20),
        cost_estimate=pl.CostEstimate(flops=5 * 10**9, bytes_accessed=10**5, transcendentals=0),
        name="gate",
    )(*values, *others)


def score_kernel(planes, helpers, blocks, pieces, mine_ref, theirs_ref, *refs):
    queries, rest = refs[: blocks * pieces], refs[blocks * pieces :]
    if pieces > 1:
        queries = [jnp.concatenate([ref[...] for ref in queries], axis=0)]
    shard, helper = lax.axis_index("shard"), lax.axis_index("help")
    span, width = mine_ref.shape
    rank = span // planes
    count = (queries[0].shape[0] - TILE) * LANES // width
    lanes = count // LANES
    lifter = jnp.concatenate([mine_ref[...], theirs_ref[...]], axis=0)
    clusters = [
        ((shard ^ (INNER * d)) * helpers + (helper ^ side)).astype(F32) for side in (0, 1) for d in range(planes)
    ]
    total, tally = None, [None] * len(clusters)
    for q_ref in queries:
        rows = slabs(q_ref, count, width)
        tile = q_ref[count * width // LANES :, :].astype(F32)
        first, second = (
            jnp.concatenate([tile[k * lanes + j : k * lanes + j + 1] for j in range(lanes)], axis=1) for k in (0, 1)
        )
        lifted = contract(lifter, rows, ((1,), (1,)))
        kept = []
        for k, cluster in enumerate(clusters):
            hit = (first == cluster) | (second == cluster)
            kept.append(jnp.where(hit, lifted[k * rank : (k + 1) * rank], 0.0))
            here = hit.astype(F32)
            tally[k] = here if tally[k] is None else tally[k] + here
        high, low = halves(jnp.concatenate(kept, axis=0))
        part = contract(high, rows, ((1,), (0,)))
        if blocks > 1:
            part = part + contract(low, rows, ((1,), (0,)))
        total = part if total is None else total + part
    named = jnp.concatenate(
        [jnp.broadcast_to(jnp.sum(t, axis=1, keepdims=True), (rank, LANES)) for t in tally], axis=0
    )
    if len(rest) == 1:
        rest[0][:, :width] = total
        rest[0][:, width:] = named
    else:
        before, *outs = rest
        for side, out in enumerate(outs):
            part = slice(side * span, (side + 1) * span)
            out[:, :width] = (before[part, :width] + total[part]).astype(out.dtype)
            counts = before[part, width:] + named[part]
            out[:, width:] = (counts if out.dtype == F32 else digits(counts)).astype(out.dtype)


def digits(counts):
    high = jnp.floor(counts * (1.0 / 256.0))
    line = lax.broadcasted_iota(jnp.int32, counts.shape, 0)
    return jnp.where(line % 2 == 0, high, counts - 256.0 * high)


def fold_kernel(planes, mine_ref, theirs_ref, own_ref, *send_refs):
    rank, wide = own_ref.shape
    width = wide - LANES
    for d in range(planes):
        part = slice(d * rank, (d + 1) * rank)
        theirs = theirs_ref[part, :].astype(F32)
        total = mine_ref[part, :width] + theirs[:, :width]
        named = mine_ref[part, width:] + 256.0 * theirs[0:1, width:] + theirs[1:2, width:]
        if d == 0:
            own_ref[:, :width] = total
            own_ref[:, width:] = named
        else:
            ref = send_refs[d - 1]
            for k in range(width // LANES):
                ref[k * rank : (k + 1) * rank, :] = total[:, k * LANES : (k + 1) * LANES].astype(BF16)
            ref[rank * width // LANES :, :] = digits(named[:TILE]).astype(BF16)


def scale_kernel(resident_ref, own_ref, *refs):
    *parts, wide_ref, out_ref = refs
    rank, width = out_ref.shape
    total = own_ref[:, :width]
    queried = own_ref[0:1, width : width + 1]
    for part in parts:
        total = total + slabs(part, rank, width).astype(F32)
        tile = part[rank * width // LANES :, :].astype(F32)
        queried = queried + 256.0 * tile[0:1, 0:1] + tile[1:2, 0:1]
    resident = resident_ref[0:1, 0:1]
    factor = lax.rsqrt((queried + 1.0) * (queried + resident)) * (1.0 / width)
    wide_ref[...] = total * factor
    out_ref[...] = (total * factor).astype(BF16)


def sketch_kernel(helpers, mark_ref, resident_ref, points_ref, *refs):
    scaled, sketch_hbm, outs = refs[:helpers], refs[helpers], refs[helpers + 1 : -2]
    sketch_ref, sem = refs[-2:]
    rank, count = sketch_ref.shape
    mark = mark_ref[...]
    points = points_ref[...]
    blocks, rests = [], []
    for s in scaled:
        if s.dtype == F32:
            high, low = halves(s[...])
            blocks.append(high)
            rests.append(low)
        else:
            blocks.append(s[...])
    product = contract(jnp.concatenate(blocks + rests, axis=0), points, ((1,), (1,)))
    whole = [product[k * rank : (k + 1) * rank] for k in range(helpers)]
    for k in range(len(rests)):
        whole[k] = whole[k] + product[(helpers + k) * rank : (helpers + k + 1) * rank]
    sketch = whole[0]
    for d in range(1, helpers):
        sketch = jnp.where(mark == d, whole[d], sketch)
    sketch_ref[...] = sketch
    leaving = pltpu.make_async_copy(sketch_ref, sketch_hbm, sem)
    leaving.start()
    rounded = sketch.astype(BF16)
    rows = [jnp.where(mark == d, rounded, jnp.zeros((), BF16)) for d in range(helpers)]
    summed = contract(jnp.concatenate(rows, axis=0), points, ((1,), (0,)))
    for d, out in enumerate(outs):
        block = summed[d * rank : (d + 1) * rank] * lax.rsqrt(resident_ref[d : d + 1, 0:1])
        out[...] = block.astype(out.dtype)
    leaving.wait()


def swap(value, axis, d):
    return lax.ppermute(value, axis, [(i, i ^ d) for i in range(lax.axis_size(axis))])


def swaps(values, axis, unit=1):
    return [swap(value, axis, unit * d) for d, value in reversed([*enumerate(values, 1)])]


def shards(queries, probe_group, probe_local, points, point_cluster, test_matrix):
    groups = lax.axis_size("shard")
    helpers = lax.axis_size("help")
    planes = groups // INNER
    count = queries.shape[0]
    rank = test_matrix.shape[0]
    own_points, width = points.shape
    block = jax.ShapeDtypeStruct((rank, width), F32)
    sent = jax.ShapeDtypeStruct((rank, width), BF16)

    packed, mark, resident, own, *parts = pl.pallas_call(
        functools.partial(lift_kernel, helpers),
        out_shape=[
            jax.ShapeDtypeStruct((count * width // LANES + TILE, LANES), BF16),
            jax.ShapeDtypeStruct((1, own_points), jnp.int32),
            jax.ShapeDtypeStruct((8, LANES), F32),
            block,
            block,
        ]
        + [sent] * (helpers - 2),
        in_specs=[HBM] * 6,
        scratch_shapes=[
            pltpu.VMEM((2, count), jnp.int32),
            pltpu.VMEM((2, count), jnp.int32),
            pltpu.VMEM(point_cluster.shape, jnp.int32),
            pltpu.VMEM(test_matrix.shape, BF16),
            pltpu.VMEM(points.shape, BF16),
            pltpu.SemaphoreType.DMA((4 + CHUNKS + width // LANES,)),
        ],
        compiler_params=PARAMS,
        name="lift",
    )(*[in_hbm(a) for a in (queries, probe_group.T, probe_local.T, point_cluster, test_matrix, points)])
    lifter = pl.pallas_call(
        join_kernel,
        out_shape=sent,
        compiler_params=PARAMS,
        cost_estimate=pl.CostEstimate(flops=4 * 10**9, bytes_accessed=10**5, transcendentals=0),
        name="join",
    )(own, *swaps(parts, "help"))
    lifters = [lifter] + [swap(lifter, "shard", INNER * d) for d in range(1, planes)]
    index, axes = range(groups * helpers), ("shard", "help")
    one = [(i, i ^ (2 if i % 2 == 0 else helpers)) for i in index]
    two = [(i, i ^ (helpers if i % 2 == 0 else 2)) for i in index]
    far = lax.ppermute(packed, axes, one)
    (near,) = gate([lax.ppermute(packed, axes, two)], lifters[-1])
    cut = width // LANES * 2 // 3 * count
    across = [lax.ppermute(near[:cut], axes, one), lax.ppermute(far[cut:], axes, two)]

    mine = pl.pallas_call(
        stack_kernel,
        out_shape=jax.ShapeDtypeStruct((planes * rank, width), BF16),
        in_specs=[VMEM] * planes + [ANY],
        compiler_params=PARAMS,
        cost_estimate=pl.CostEstimate(flops=25 * 10**8, bytes_accessed=10**5, transcendentals=0),
        name="stack",
    )(*lifters, far)
    theirs = swap(mine, "help", 1)

    wide = width + LANES
    begun = pl.pallas_call(
        functools.partial(score_kernel, planes, helpers, 3, 1),
        out_shape=jax.ShapeDtypeStruct((2 * planes * rank, wide), F32),
        compiler_params=PARAMS,
        name="score",
    )(mine, theirs, packed, near, far)
    moments, passed = pl.pallas_call(
        functools.partial(score_kernel, planes, helpers, 1, 2),
        out_shape=[jax.ShapeDtypeStruct((planes * rank, wide), kind) for kind in (F32, BF16)],
        compiler_params=PARAMS,
        name="score_last",
    )(mine, theirs, *across, begun)
    folded = pl.pallas_call(
        functools.partial(fold_kernel, planes),
        out_shape=[jax.ShapeDtypeStruct((rank, wide), F32)]
        + [jax.ShapeDtypeStruct((rank * width // LANES + TILE, LANES), BF16)] * (planes - 1),
        compiler_params=PARAMS,
        name="fold",
    )(moments, swap(passed, "help", 1))
    moments = [folded[0]] + swaps(folded[1:], "shard", INNER)

    exact, scaled = pl.pallas_call(
        scale_kernel,
        out_shape=[block, sent],
        compiler_params=PARAMS,
        name="scale",
    )(resident, *moments)
    scaled = [exact, swap(exact, "help", 1)] + [swap(scaled, "help", d) for d in range(2, helpers)]

    sketch, regressor, *parts = pl.pallas_call(
        functools.partial(sketch_kernel, helpers),
        out_shape=[jax.ShapeDtypeStruct((rank, own_points), F32), block, block] + [sent] * (helpers - 2),
        out_specs=[HBM] + [VMEM] * helpers,
        scratch_shapes=[pltpu.VMEM((rank, own_points), F32), pltpu.SemaphoreType.DMA],
        compiler_params=PARAMS,
        name="sketch",
    )(mark, resident, points, *scaled)
    for part in swaps(parts, "help"):
        regressor = regressor + part.astype(F32)
    return sketch, regressor[None]


def solution(mesh):
    in_specs = (
        P(("shard", "help"), None),
        P(("shard", "help"), None),
        P(("shard", "help"), None),
        P(("shard", "help"), None),
        P("shard", None),
        P(None, ("shard", "help")),
    )
    out_specs = (P(None, ("shard", "help")), P(("shard", "help"), None, None))
    return jax.shard_map(shards, mesh=mesh, in_specs=in_specs, out_specs=out_specs, check_vma=False)
```

```python
import functools

import jax
import jax.numpy as jnp
from jax import lax
from jax.experimental import pallas as pl
from jax.experimental.pallas import tpu as pltpu
from jax.sharding import PartitionSpec as P

F32 = jnp.float32
BF16 = jnp.bfloat16
LANES = 128
TILE = 16
CHUNKS = 4
INNER = 2

ANY = pl.BlockSpec(memory_space=pl.ANY)
VMEM = pl.BlockSpec(memory_space=pltpu.VMEM)
VMEM = pl.BlockSpec(memory_space=pltpu.VMEM)
HBM = pl.BlockSpec(memory_space=pltpu.HBM)
PARAMS = pltpu.CompilerParams(vmem_limit_bytes=32 * 1024 * 1024)


def in_hbm(value):
    return pltpu.with_memory_space_constraint(value, pltpu.HBM)


def contract(a, b, dims):
    return lax.dot_general(a, b, (dims, ((), ())), preferred_element_type=F32)


def halves(value):
    high = value.astype(BF16)
    return high, (value - high.astype(F32)).astype(BF16)


def slabs(ref, rows, width):
    return jnp.concatenate([ref[k * rows : (k + 1) * rows, :] for k in range(width // LANES)], axis=1)


def lift_kernel(helpers, *refs):
    rows_hbm, group_hbm, local_hbm, ids_hbm, test_hbm, points_hbm = refs[:6]
    packed_ref, mark_ref, resident_ref = refs[6:9]
    outs = refs[9 : 9 + helpers]
    group_ref, local_ref, ids_ref, test_ref, points_ref, sems = refs[9 + helpers :]
    helper = lax.axis_index("help")
    asked, width = rows_hbm.shape
    rank, count = test_ref.shape
    piece = count // CHUNKS
    pairs = [(ids_hbm, ids_ref), (test_hbm, test_ref)]
    for k in range(CHUNKS):
        part = pl.ds(k * piece, piece)
        pairs.append((points_hbm.at[part], points_ref.at[part]))
    pairs += [(group_hbm, group_ref), (local_hbm, local_ref)]
    for k in range(width // LANES):
        pairs.append((rows_hbm.at[:, pl.ds(k * LANES, LANES)], packed_ref.at[pl.ds(k * asked, asked)]))
    copies = [pltpu.make_async_copy(*pair, sems.at[k]) for k, pair in enumerate(pairs)]
    for copy in copies:
        copy.start()
    copies[0].wait()
    everyone = ids_ref[...]
    mark = ids_ref[:, pl.ds(pl.multiple_of(helper * count, LANES), count)] ^ helper
    mark_ref[...] = mark
    for d in range(helpers):
        many = jnp.sum((everyone == (helper ^ d)).astype(F32), axis=1, keepdims=True)
        resident_ref[d : d + 1, :] = jnp.broadcast_to(many, (1, LANES))
    copies[1].wait()
    test = test_ref[...]
    rows = jnp.concatenate([jnp.where(mark == d, test, jnp.zeros((), BF16)) for d in range(helpers)], axis=0)
    total = None
    for k in range(CHUNKS):
        copies[2 + k].wait()
        part = slice(k * piece, (k + 1) * piece)
        more = contract(rows[:, part], points_ref[part, :], ((1,), (0,)))
        total = more if total is None else total + more
    for d, out in enumerate(outs):
        out[...] = total[d * rank : (d + 1) * rank].astype(out.dtype)
    for copy in copies[2 + CHUNKS :]:
        copy.wait()
    cluster = (group_ref[...] * helpers + local_ref[...]).astype(F32)
    line = [cluster[k : k + 1, j : j + LANES] for k in (0, 1) for j in range(0, asked, LANES)]
    line.append(jnp.zeros((TILE - len(line), LANES), F32))
    packed_ref[asked * width // LANES :, :] = jnp.concatenate(line, axis=0).astype(BF16)


def join_kernel(*refs):
    *parts, out = refs
    total = parts[0][...]
    for part in parts[1:]:
        total = total + part[...].astype(F32)
    out[...] = total.astype(out.dtype)


def stack_kernel(*refs):
    *parts, _, out = refs
    rank = parts[0].shape[0]
    for k, part in enumerate(parts):
        out[k * rank : (k + 1) * rank, :] = part[...]


def gate_kernel(*refs):
    pass


def gate(values, *others):
    return pl.pallas_call(
        gate_kernel,
        out_shape=[jax.ShapeDtypeStruct(value.shape, value.dtype) for value in values],
        in_specs=[ANY] * (len(values) + len(others)),
        out_specs=[ANY] * len(values),
        input_output_aliases={k: k for k in range(len(values))},
        compiler_params=pltpu.CompilerParams(vmem_limit_bytes=1 << 20),
        cost_estimate=pl.CostEstimate(flops=5 * 10**9, bytes_accessed=10**5, transcendentals=0),
        name="gate",
    )(*values, *others)


def score_kernel(planes, helpers, blocks, mine_ref, theirs_ref, *refs):
    queries, rest = refs[:blocks], refs[blocks:]
    shard, helper = lax.axis_index("shard"), lax.axis_index("help")
    span, width = mine_ref.shape
    rank = span // planes
    count = (queries[0].shape[0] - TILE) * LANES // width
    pieces = count // LANES
    lifter = jnp.concatenate([mine_ref[...], theirs_ref[...]], axis=0)
    clusters = [
        ((shard ^ (INNER * d)) * helpers + (helper ^ side)).astype(F32) for side in (0, 1) for d in range(planes)
    ]
    total, tally = None, [None] * len(clusters)
    for q_ref in queries:
        rows = slabs(q_ref, count, width)
        tile = q_ref[count * width // LANES :, :].astype(F32)
        first, second = (
            jnp.concatenate([tile[k * pieces + j : k * pieces + j + 1] for j in range(pieces)], axis=1) for k in (0, 1)
        )
        lifted = contract(lifter, rows, ((1,), (1,)))
        kept = []
        for k, cluster in enumerate(clusters):
            hit = (first == cluster) | (second == cluster)
            kept.append(jnp.where(hit, lifted[k * rank : (k + 1) * rank], 0.0))
            here = hit.astype(F32)
            tally[k] = here if tally[k] is None else tally[k] + here
        high, low = halves(jnp.concatenate(kept, axis=0))
        part = contract(high, rows, ((1,), (0,)))
        if blocks > 1:
            part = part + contract(low, rows, ((1,), (0,)))
        total = part if total is None else total + part
    named = jnp.concatenate(
        [jnp.broadcast_to(jnp.sum(t, axis=1, keepdims=True), (rank, LANES)) for t in tally], axis=0
    )
    if len(rest) == 1:
        rest[0][:, :width] = total
        rest[0][:, width:] = named
    else:
        before, *outs = rest
        for side, out in enumerate(outs):
            part = slice(side * span, (side + 1) * span)
            out[:, :width] = (before[part, :width] + total[part]).astype(out.dtype)
            counts = before[part, width:] + named[part]
            out[:, width:] = (counts if out.dtype == F32 else digits(counts)).astype(out.dtype)


def digits(counts):
    high = jnp.floor(counts * (1.0 / 256.0))
    line = lax.broadcasted_iota(jnp.int32, counts.shape, 0)
    return jnp.where(line % 2 == 0, high, counts - 256.0 * high)


def fold_kernel(planes, mine_ref, theirs_ref, own_ref, *send_refs):
    rank, wide = own_ref.shape
    width = wide - LANES
    for d in range(planes):
        part = slice(d * rank, (d + 1) * rank)
        theirs = theirs_ref[part, :].astype(F32)
        total = mine_ref[part, :width] + theirs[:, :width]
        named = mine_ref[part, width:] + 256.0 * theirs[0:1, width:] + theirs[1:2, width:]
        if d == 0:
            own_ref[:, :width] = total
            own_ref[:, width:] = named
        else:
            ref = send_refs[d - 1]
            for k in range(width // LANES):
                ref[k * rank : (k + 1) * rank, :] = total[:, k * LANES : (k + 1) * LANES].astype(BF16)
            ref[rank * width // LANES :, :] = digits(named[:TILE]).astype(BF16)


def scale_kernel(resident_ref, own_ref, *refs):
    *parts, wide_ref, out_ref = refs
    rank, width = out_ref.shape
    total = own_ref[:, :width]
    queried = own_ref[0:1, width : width + 1]
    for part in parts:
        total = total + slabs(part, rank, width).astype(F32)
        tile = part[rank * width // LANES :, :].astype(F32)
        queried = queried + 256.0 * tile[0:1, 0:1] + tile[1:2, 0:1]
    resident = resident_ref[0:1, 0:1]
    factor = lax.rsqrt((queried + 1.0) * (queried + resident)) * (1.0 / width)
    wide_ref[...] = total * factor
    out_ref[...] = (total * factor).astype(BF16)


def sketch_kernel(helpers, mark_ref, resident_ref, points_ref, *refs):
    scaled, sketch_hbm, outs = refs[:helpers], refs[helpers], refs[helpers + 1 : -2]
    sketch_ref, sem = refs[-2:]
    rank, count = sketch_ref.shape
    piece = count // CHUNKS
    blocks, rests = [], []
    for s in scaled:
        if s.dtype == F32:
            high, low = halves(s[...])
            blocks.append(high)
            rests.append(low)
        else:
            blocks.append(s[...])
    lifter = jnp.concatenate(blocks + rests, axis=0)
    leaving = pltpu.make_async_copy(sketch_ref, sketch_hbm, sem)
    summed = None
    for j in range(CHUNKS):
        part = slice(j * piece, (j + 1) * piece)
        mark = mark_ref[:, part]
        points = points_ref[part, :]
        product = contract(lifter, points, ((1,), (1,)))
        whole = [product[k * rank : (k + 1) * rank] for k in range(helpers)]
        for k in range(len(rests)):
            whole[k] = whole[k] + product[(helpers + k) * rank : (helpers + k + 1) * rank]
        sketch = whole[0]
        for d in range(1, helpers):
            sketch = jnp.where(mark == d, whole[d], sketch)
        sketch_ref[:, part] = sketch
        if j == CHUNKS - 1:
            leaving.start()
        rounded = sketch.astype(BF16)
        rows = [jnp.where(mark == d, rounded, jnp.zeros((), BF16)) for d in range(helpers)]
        more = contract(jnp.concatenate(rows, axis=0), points, ((1,), (0,)))
        summed = more if summed is None else summed + more
    for d, out in enumerate(outs):
        block = summed[d * rank : (d + 1) * rank] * lax.rsqrt(resident_ref[d : d + 1, 0:1])
        out[...] = block.astype(out.dtype)
    leaving.wait()


def swap(value, axis, d):
    return lax.ppermute(value, axis, [(i, i ^ d) for i in range(lax.axis_size(axis))])


def swaps(values, axis, unit=1):
    return [swap(value, axis, unit * d) for d, value in reversed([*enumerate(values, 1)])]


def shards(queries, probe_group, probe_local, points, point_cluster, test_matrix):
    groups = lax.axis_size("shard")
    helpers = lax.axis_size("help")
    planes = groups // INNER
    count = queries.shape[0]
    rank = test_matrix.shape[0]
    own_points, width = points.shape
    block = jax.ShapeDtypeStruct((rank, width), F32)
    sent = jax.ShapeDtypeStruct((rank, width), BF16)

    packed, mark, resident, own, *parts = pl.pallas_call(
        functools.partial(lift_kernel, helpers),
        out_shape=[
            jax.ShapeDtypeStruct((count * width // LANES + TILE, LANES), BF16),
            jax.ShapeDtypeStruct((1, own_points), jnp.int32),
            jax.ShapeDtypeStruct((8, LANES), F32),
            block,
            block,
        ]
        + [sent] * (helpers - 2),
        in_specs=[HBM] * 6,
        scratch_shapes=[
            pltpu.VMEM((2, count), jnp.int32),
            pltpu.VMEM((2, count), jnp.int32),
            pltpu.VMEM(point_cluster.shape, jnp.int32),
            pltpu.VMEM(test_matrix.shape, BF16),
            pltpu.VMEM(points.shape, BF16),
            pltpu.SemaphoreType.DMA((4 + CHUNKS + width // LANES,)),
        ],
        compiler_params=PARAMS,
        name="lift",
    )(*[in_hbm(a) for a in (queries, probe_group.T, probe_local.T, point_cluster, test_matrix, points)])
    lifter = pl.pallas_call(
        join_kernel,
        out_shape=sent,
        compiler_params=PARAMS,
        cost_estimate=pl.CostEstimate(flops=4 * 10**9, bytes_accessed=10**5, transcendentals=0),
        name="join",
    )(own, *swaps(parts, "help"))
    lifters = [lifter] + [swap(lifter, "shard", INNER * d) for d in range(1, planes)]
    index, axes = range(groups * helpers), ("shard", "help")
    one = [(i, i ^ (2 if i % 2 == 0 else helpers)) for i in index]
    two = [(i, i ^ (helpers if i % 2 == 0 else 2)) for i in index]
    far = lax.ppermute(packed, axes, one)
    (near,) = gate([lax.ppermute(packed, axes, two)], lifters[-1])
    across = lax.ppermute(near, axes, one)

    mine = pl.pallas_call(
        stack_kernel,
        out_shape=jax.ShapeDtypeStruct((planes * rank, width), BF16),
        in_specs=[VMEM] * planes + [ANY],
        compiler_params=PARAMS,
        cost_estimate=pl.CostEstimate(flops=25 * 10**8, bytes_accessed=10**5, transcendentals=0),
        name="stack",
    )(*lifters, far)
    theirs = swap(mine, "help", 1)

    wide = width + LANES
    begun = pl.pallas_call(
        functools.partial(score_kernel, planes, helpers, 3),
        out_shape=jax.ShapeDtypeStruct((2 * planes * rank, wide), F32),
        compiler_params=PARAMS,
        name="score",
    )(mine, theirs, packed, near, far)
    moments, passed = pl.pallas_call(
        functools.partial(score_kernel, planes, helpers, 1),
        out_shape=[jax.ShapeDtypeStruct((planes * rank, wide), kind) for kind in (F32, BF16)],
        compiler_params=PARAMS,
        name="score_last",
    )(mine, theirs, across, begun)
    folded = pl.pallas_call(
        functools.partial(fold_kernel, planes),
        out_shape=[jax.ShapeDtypeStruct((rank, wide), F32)]
        + [jax.ShapeDtypeStruct((rank * width // LANES + TILE, LANES), BF16)] * (planes - 1),
        compiler_params=PARAMS,
        name="fold",
    )(moments, swap(passed, "help", 1))
    moments = [folded[0]] + swaps(folded[1:], "shard", INNER)

    exact, scaled = pl.pallas_call(
        scale_kernel,
        out_shape=[block, sent],
        compiler_params=PARAMS,
        name="scale",
    )(resident, *moments)
    scaled = [exact, swap(exact, "help", 1)] + [swap(scaled, "help", d) for d in range(2, helpers)]

    sketch, regressor, *parts = pl.pallas_call(
        functools.partial(sketch_kernel, helpers),
        out_shape=[jax.ShapeDtypeStruct((rank, own_points), F32), block, block] + [sent] * (helpers - 2),
        out_specs=[HBM] + [VMEM] * helpers,
        scratch_shapes=[pltpu.VMEM((rank, own_points), F32), pltpu.SemaphoreType.DMA],
        compiler_params=PARAMS,
        name="sketch",
    )(mark, resident, points, *scaled)
    for part in swaps(parts, "help"):
        regressor = regressor + part.astype(F32)
    return sketch, regressor[None]


def solution(mesh):
    in_specs = (
        P(("shard", "help"), None),
        P(("shard", "help"), None),
        P(("shard", "help"), None),
        P(("shard", "help"), None),
        P("shard", None),
        P(None, ("shard", "help")),
    )
    out_specs = (P(None, ("shard", "help")), P(("shard", "help"), None, None))
    return jax.shard_map(shards, mesh=mesh, in_specs=in_specs, out_specs=out_specs, check_vma=False)
```

```python
import functools

import jax
import jax.numpy as jnp
from jax import lax
from jax.experimental import pallas as pl
from jax.experimental.pallas import tpu as pltpu
from jax.sharding import PartitionSpec as P

F32 = jnp.float32
BF16 = jnp.bfloat16
LANES = 128
TILE = 16
CHUNKS = 4
INNER = 2

ANY = pl.BlockSpec(memory_space=pl.ANY)
VMEM = pl.BlockSpec(memory_space=pltpu.VMEM)
VMEM = pl.BlockSpec(memory_space=pltpu.VMEM)
HBM = pl.BlockSpec(memory_space=pltpu.HBM)
PARAMS = pltpu.CompilerParams(vmem_limit_bytes=32 * 1024 * 1024)


def in_hbm(value):
    return pltpu.with_memory_space_constraint(value, pltpu.HBM)


def contract(a, b, dims):
    return lax.dot_general(a, b, (dims, ((), ())), preferred_element_type=F32)


def halves(value):
    high = value.astype(BF16)
    return high, (value - high.astype(F32)).astype(BF16)


def slabs(ref, rows, width):
    return jnp.concatenate([ref[k * rows : (k + 1) * rows, :] for k in range(width // LANES)], axis=1)


def lift_kernel(helpers, *refs):
    rows_hbm, group_hbm, local_hbm, ids_hbm, test_hbm, points_hbm = refs[:6]
    packed_ref, mark_ref, resident_ref = refs[6:9]
    outs = refs[9 : 9 + helpers]
    group_ref, local_ref, ids_ref, test_ref, points_ref, sems = refs[9 + helpers :]
    helper = lax.axis_index("help")
    asked, width = rows_hbm.shape
    rank, count = test_ref.shape
    piece = count // CHUNKS
    pairs = [(ids_hbm, ids_ref), (test_hbm, test_ref)]
    for k in range(CHUNKS):
        part = pl.ds(k * piece, piece)
        pairs.append((points_hbm.at[part], points_ref.at[part]))
    pairs += [(group_hbm, group_ref), (local_hbm, local_ref)]
    for k in range(width // LANES):
        pairs.append((rows_hbm.at[:, pl.ds(k * LANES, LANES)], packed_ref.at[pl.ds(k * asked, asked)]))
    copies = [pltpu.make_async_copy(*pair, sems.at[k]) for k, pair in enumerate(pairs)]
    for copy in copies:
        copy.start()
    copies[0].wait()
    everyone = ids_ref[...]
    mark = ids_ref[:, pl.ds(pl.multiple_of(helper * count, LANES), count)] ^ helper
    mark_ref[...] = mark
    for d in range(helpers):
        many = jnp.sum((everyone == (helper ^ d)).astype(F32), axis=1, keepdims=True)
        resident_ref[d : d + 1, :] = jnp.broadcast_to(many, (1, LANES))
    copies[1].wait()
    test = test_ref[...]
    rows = jnp.concatenate([jnp.where(mark == d, test, jnp.zeros((), BF16)) for d in range(helpers)], axis=0)
    total = None
    for k in range(CHUNKS):
        copies[2 + k].wait()
        part = slice(k * piece, (k + 1) * piece)
        more = contract(rows[:, part], points_ref[part, :], ((1,), (0,)))
        total = more if total is None else total + more
    for d, out in enumerate(outs):
        out[...] = total[d * rank : (d + 1) * rank].astype(out.dtype)
    for copy in copies[2 + CHUNKS :]:
        copy.wait()
    cluster = (group_ref[...] * helpers + local_ref[...]).astype(F32)
    line = [cluster[k : k + 1, j : j + LANES] for k in (0, 1) for j in range(0, asked, LANES)]
    line.append(jnp.zeros((TILE - len(line), LANES), F32))
    packed_ref[asked * width // LANES :, :] = jnp.concatenate(line, axis=0).astype(BF16)


def join_kernel(*refs):
    *parts, out = refs
    total = parts[0][...]
    for part in parts[1:]:
        total = total + part[...].astype(F32)
    out[...] = total.astype(out.dtype)


def stack_kernel(*refs):
    *parts, _, out = refs
    rank = parts[0].shape[0]
    for k, part in enumerate(parts):
        out[k * rank : (k + 1) * rank, :] = part[...]


def gate_kernel(*refs):
    pass


def gate(values, *others):
    return pl.pallas_call(
        gate_kernel,
        out_shape=[jax.ShapeDtypeStruct(value.shape, value.dtype) for value in values],
        in_specs=[ANY] * (len(values) + len(others)),
        out_specs=[ANY] * len(values),
        input_output_aliases={k: k for k in range(len(values))},
        compiler_params=pltpu.CompilerParams(vmem_limit_bytes=1 << 20),
        cost_estimate=pl.CostEstimate(flops=37 * 10**8, bytes_accessed=10**5, transcendentals=0),
        name="gate",
    )(*values, *others)


def score_kernel(planes, helpers, blocks, mine_ref, theirs_ref, *refs):
    queries, rest = refs[:blocks], refs[blocks:]
    shard, helper = lax.axis_index("shard"), lax.axis_index("help")
    span, width = mine_ref.shape
    rank = span // planes
    count = (queries[0].shape[0] - TILE) * LANES // width
    pieces = count // LANES
    lifter = jnp.concatenate([mine_ref[...], theirs_ref[...]], axis=0)
    clusters = [
        ((shard ^ (INNER * d)) * helpers + (helper ^ side)).astype(F32) for side in (0, 1) for d in range(planes)
    ]
    total, tally = None, [None] * len(clusters)
    for q_ref in queries:
        rows = slabs(q_ref, count, width)
        tile = q_ref[count * width // LANES :, :].astype(F32)
        first, second = (
            jnp.concatenate([tile[k * pieces + j : k * pieces + j + 1] for j in range(pieces)], axis=1) for k in (0, 1)
        )
        lifted = contract(lifter, rows, ((1,), (1,)))
        kept = []
        for k, cluster in enumerate(clusters):
            hit = (first == cluster) | (second == cluster)
            kept.append(jnp.where(hit, lifted[k * rank : (k + 1) * rank], 0.0))
            here = hit.astype(F32)
            tally[k] = here if tally[k] is None else tally[k] + here
        high, low = halves(jnp.concatenate(kept, axis=0))
        part = contract(high, rows, ((1,), (0,)))
        if blocks > 1:
            part = part + contract(low, rows, ((1,), (0,)))
        total = part if total is None else total + part
    named = jnp.concatenate(
        [jnp.broadcast_to(jnp.sum(t, axis=1, keepdims=True), (rank, LANES)) for t in tally], axis=0
    )
    if len(rest) == 1:
        rest[0][:, :width] = total
        rest[0][:, width:] = named
    else:
        before, *outs = rest
        for side, out in enumerate(outs):
            part = slice(side * span, (side + 1) * span)
            out[:, :width] = (before[part, :width] + total[part]).astype(out.dtype)
            counts = before[part, width:] + named[part]
            out[:, width:] = (counts if out.dtype == F32 else digits(counts)).astype(out.dtype)


def digits(counts):
    high = jnp.floor(counts * (1.0 / 256.0))
    line = lax.broadcasted_iota(jnp.int32, counts.shape, 0)
    return jnp.where(line % 2 == 0, high, counts - 256.0 * high)


def fold_kernel(planes, mine_ref, theirs_ref, own_ref, *send_refs):
    rank, wide = own_ref.shape
    width = wide - LANES
    for d in range(planes):
        part = slice(d * rank, (d + 1) * rank)
        theirs = theirs_ref[part, :].astype(F32)
        total = mine_ref[part, :width] + theirs[:, :width]
        named = mine_ref[part, width:] + 256.0 * theirs[0:1, width:] + theirs[1:2, width:]
        if d == 0:
            own_ref[:, :width] = total
            own_ref[:, width:] = named
        else:
            ref = send_refs[d - 1]
            for k in range(width // LANES):
                ref[k * rank : (k + 1) * rank, :] = total[:, k * LANES : (k + 1) * LANES].astype(BF16)
            ref[rank * width // LANES :, :] = digits(named[:TILE]).astype(BF16)


def scale_kernel(resident_ref, own_ref, *refs):
    *parts, wide_ref, out_ref = refs
    rank, width = out_ref.shape
    total = own_ref[:, :width]
    queried = own_ref[0:1, width : width + 1]
    for part in parts:
        total = total + slabs(part, rank, width).astype(F32)
        tile = part[rank * width // LANES :, :].astype(F32)
        queried = queried + 256.0 * tile[0:1, 0:1] + tile[1:2, 0:1]
    resident = resident_ref[0:1, 0:1]
    factor = lax.rsqrt((queried + 1.0) * (queried + resident)) * (1.0 / width)
    wide_ref[...] = total * factor
    out_ref[...] = (total * factor).astype(BF16)


def sketch_kernel(helpers, mark_ref, resident_ref, points_ref, *refs):
    scaled, sketch_hbm, outs = refs[:helpers], refs[helpers], refs[helpers + 1 : -2]
    sketch_ref, sem = refs[-2:]
    rank, count = sketch_ref.shape
    mark = mark_ref[...]
    points = points_ref[...]
    blocks, rests = [], []
    for s in scaled:
        if s.dtype == F32:
            high, low = halves(s[...])
            blocks.append(high)
            rests.append(low)
        else:
            blocks.append(s[...])
    product = contract(jnp.concatenate(blocks + rests, axis=0), points, ((1,), (1,)))
    whole = [product[k * rank : (k + 1) * rank] for k in range(helpers)]
    for k in range(len(rests)):
        whole[k] = whole[k] + product[(helpers + k) * rank : (helpers + k + 1) * rank]
    sketch = whole[0]
    for d in range(1, helpers):
        sketch = jnp.where(mark == d, whole[d], sketch)
    sketch_ref[...] = sketch
    leaving = pltpu.make_async_copy(sketch_ref, sketch_hbm, sem)
    leaving.start()
    rounded = sketch.astype(BF16)
    rows = [jnp.where(mark == d, rounded, jnp.zeros((), BF16)) for d in range(helpers)]
    summed = contract(jnp.concatenate(rows, axis=0), points, ((1,), (0,)))
    for d, out in enumerate(outs):
        block = summed[d * rank : (d + 1) * rank] * lax.rsqrt(resident_ref[d : d + 1, 0:1])
        out[...] = block.astype(out.dtype)
    leaving.wait()


def swap(value, axis, d):
    return lax.ppermute(value, axis, [(i, i ^ d) for i in range(lax.axis_size(axis))])


def swaps(values, axis, unit=1):
    return [swap(value, axis, unit * d) for d, value in reversed([*enumerate(values, 1)])]


def shards(queries, probe_group, probe_local, points, point_cluster, test_matrix):
    groups = lax.axis_size("shard")
    helpers = lax.axis_size("help")
    planes = groups // INNER
    count = queries.shape[0]
    rank = test_matrix.shape[0]
    own_points, width = points.shape
    block = jax.ShapeDtypeStruct((rank, width), F32)
    sent = jax.ShapeDtypeStruct((rank, width), BF16)

    packed, mark, resident, own, *parts = pl.pallas_call(
        functools.partial(lift_kernel, helpers),
        out_shape=[
            jax.ShapeDtypeStruct((count * width // LANES + TILE, LANES), BF16),
            jax.ShapeDtypeStruct((1, own_points), jnp.int32),
            jax.ShapeDtypeStruct((8, LANES), F32),
            block,
            block,
        ]
        + [sent] * (helpers - 2),
        in_specs=[HBM] * 6,
        scratch_shapes=[
            pltpu.VMEM((2, count), jnp.int32),
            pltpu.VMEM((2, count), jnp.int32),
            pltpu.VMEM(point_cluster.shape, jnp.int32),
            pltpu.VMEM(test_matrix.shape, BF16),
            pltpu.VMEM(points.shape, BF16),
            pltpu.SemaphoreType.DMA((4 + CHUNKS + width // LANES,)),
        ],
        compiler_params=PARAMS,
        name="lift",
    )(*[in_hbm(a) for a in (queries, probe_group.T, probe_local.T, point_cluster, test_matrix, points)])
    lifter = pl.pallas_call(
        join_kernel,
        out_shape=sent,
        compiler_params=PARAMS,
        cost_estimate=pl.CostEstimate(flops=35 * 10**8, bytes_accessed=10**5, transcendentals=0),
        name="join",
    )(own, *swaps(parts, "help"))
    lifters = [lifter] + [swap(lifter, "shard", INNER * d) for d in range(1, planes)]
    index, axes = range(groups * helpers), ("shard", "help")
    one = [(i, i ^ (2 if i % 2 == 0 else helpers)) for i in index]
    two = [(i, i ^ (helpers if i % 2 == 0 else 2)) for i in index]
    far = lax.ppermute(packed, axes, one)
    (near,) = gate([lax.ppermute(packed, axes, two)], lifters[-1])
    across = lax.ppermute(near, axes, one)

    mine = pl.pallas_call(
        stack_kernel,
        out_shape=jax.ShapeDtypeStruct((planes * rank, width), BF16),
        in_specs=[VMEM] * planes + [ANY],
        compiler_params=PARAMS,
        cost_estimate=pl.CostEstimate(flops=25*10**8, bytes_accessed=10**5, transcendentals=0),
        name="stack",
    )(*lifters, far)
    theirs = swap(mine, "help", 1)

    wide = width + LANES
    begun = pl.pallas_call(
        functools.partial(score_kernel, planes, helpers, 3),
        out_shape=jax.ShapeDtypeStruct((2 * planes * rank, wide), F32),
        compiler_params=PARAMS,
        name="score",
    )(mine, theirs, packed, near, far)
    moments, passed = pl.pallas_call(
        functools.partial(score_kernel, planes, helpers, 1),
        out_shape=[jax.ShapeDtypeStruct((planes * rank, wide), kind) for kind in (F32, BF16)],
        compiler_params=PARAMS,
        name="score_last",
    )(mine, theirs, across, begun)
    folded = pl.pallas_call(
        functools.partial(fold_kernel, planes),
        out_shape=[jax.ShapeDtypeStruct((rank, wide), F32)]
        + [jax.ShapeDtypeStruct((rank * width // LANES + TILE, LANES), BF16)] * (planes - 1),
        compiler_params=PARAMS,
        name="fold",
    )(moments, swap(passed, "help", 1))
    moments = [folded[0]] + swaps(folded[1:], "shard", INNER)

    exact, scaled = pl.pallas_call(
        scale_kernel,
        out_shape=[block, sent],
        compiler_params=PARAMS,
        name="scale",
    )(resident, *moments)
    scaled = [exact, swap(exact, "help", 1)] + [swap(scaled, "help", d) for d in range(2, helpers)]

    sketch, regressor, *parts = pl.pallas_call(
        functools.partial(sketch_kernel, helpers),
        out_shape=[jax.ShapeDtypeStruct((rank, own_points), F32), block, block] + [sent] * (helpers - 2),
        out_specs=[HBM] + [VMEM] * helpers,
        scratch_shapes=[pltpu.VMEM((rank, own_points), F32), pltpu.SemaphoreType.DMA],
        compiler_params=PARAMS,
        name="sketch",
    )(mark, resident, points, *scaled)
    for part in swaps(parts, "help"):
        regressor = regressor + part.astype(F32)
    return sketch, regressor[None]


def solution(mesh):
    in_specs = (
        P(("shard", "help"), None),
        P(("shard", "help"), None),
        P(("shard", "help"), None),
        P(("shard", "help"), None),
        P("shard", None),
        P(None, ("shard", "help")),
    )
    out_specs = (P(None, ("shard", "help")), P(("shard", "help"), None, None))
    return jax.shard_map(shards, mesh=mesh, in_specs=in_specs, out_specs=out_specs, check_vma=False)
```

```python
import functools

import jax
import jax.numpy as jnp
from jax import lax
from jax.experimental import pallas as pl
from jax.experimental.pallas import tpu as pltpu
from jax.sharding import PartitionSpec as P

F32 = jnp.float32
BF16 = jnp.bfloat16
LANES = 128
TILE = 16
CHUNKS = 4
INNER = 2

ANY = pl.BlockSpec(memory_space=pl.ANY)
VMEM = pl.BlockSpec(memory_space=pltpu.VMEM)
VMEM = pl.BlockSpec(memory_space=pltpu.VMEM)
HBM = pl.BlockSpec(memory_space=pltpu.HBM)
PARAMS = pltpu.CompilerParams(vmem_limit_bytes=32 * 1024 * 1024)


def in_hbm(value):
    return pltpu.with_memory_space_constraint(value, pltpu.HBM)


def contract(a, b, dims):
    return lax.dot_general(a, b, (dims, ((), ())), preferred_element_type=F32)


def halves(value):
    high = value.astype(BF16)
    return high, (value - high.astype(F32)).astype(BF16)


def slabs(ref, rows, width):
    return jnp.concatenate([ref[k * rows : (k + 1) * rows, :] for k in range(width // LANES)], axis=1)


def lift_kernel(helpers, *refs):
    rows_hbm, group_hbm, local_hbm, ids_hbm, test_hbm, points_hbm = refs[:6]
    packed_ref, mark_ref, resident_ref = refs[6:9]
    outs = refs[9 : 9 + helpers]
    group_ref, local_ref, ids_ref, test_ref, points_ref, sems = refs[9 + helpers :]
    helper = lax.axis_index("help")
    asked, width = rows_hbm.shape
    rank, count = test_ref.shape
    piece = count // CHUNKS
    pairs = [(ids_hbm, ids_ref), (test_hbm, test_ref)]
    for k in range(CHUNKS):
        part = pl.ds(k * piece, piece)
        pairs.append((points_hbm.at[part], points_ref.at[part]))
    pairs += [(group_hbm, group_ref), (local_hbm, local_ref)]
    for k in range(width // LANES):
        pairs.append((rows_hbm.at[:, pl.ds(k * LANES, LANES)], packed_ref.at[pl.ds(k * asked, asked)]))
    copies = [pltpu.make_async_copy(*pair, sems.at[k]) for k, pair in enumerate(pairs)]
    for copy in copies:
        copy.start()
    copies[0].wait()
    everyone = ids_ref[...]
    mark = ids_ref[:, pl.ds(pl.multiple_of(helper * count, LANES), count)] ^ helper
    mark_ref[...] = mark
    for d in range(helpers):
        many = jnp.sum((everyone == (helper ^ d)).astype(F32), axis=1, keepdims=True)
        resident_ref[d : d + 1, :] = jnp.broadcast_to(many, (1, LANES))
    copies[1].wait()
    test = test_ref[...]
    rows = jnp.concatenate([jnp.where(mark == d, test, jnp.zeros((), BF16)) for d in range(helpers)], axis=0)
    total = None
    for k in range(CHUNKS):
        copies[2 + k].wait()
        part = slice(k * piece, (k + 1) * piece)
        more = contract(rows[:, part], points_ref[part, :], ((1,), (0,)))
        total = more if total is None else total + more
    for d, out in enumerate(outs):
        out[...] = total[d * rank : (d + 1) * rank].astype(out.dtype)
    for copy in copies[2 + CHUNKS :]:
        copy.wait()
    cluster = (group_ref[...] * helpers + local_ref[...]).astype(F32)
    line = [cluster[k : k + 1, j : j + LANES] for k in (0, 1) for j in range(0, asked, LANES)]
    line.append(jnp.zeros((TILE - len(line), LANES), F32))
    packed_ref[asked * width // LANES :, :] = jnp.concatenate(line, axis=0).astype(BF16)


def join_kernel(*refs):
    *parts, out = refs
    total = parts[0][...]
    for part in parts[1:]:
        total = total + part[...].astype(F32)
    out[...] = total.astype(out.dtype)


def stack_kernel(*refs):
    *parts, _, out = refs
    rank = parts[0].shape[0]
    for k, part in enumerate(parts):
        out[k * rank : (k + 1) * rank, :] = part[...]


def gate_kernel(*refs):
    pass


def gate(values, *others):
    return pl.pallas_call(
        gate_kernel,
        out_shape=[jax.ShapeDtypeStruct(value.shape, value.dtype) for value in values],
        in_specs=[ANY] * (len(values) + len(others)),
        out_specs=[ANY] * len(values),
        input_output_aliases={k: k for k in range(len(values))},
        compiler_params=pltpu.CompilerParams(vmem_limit_bytes=1 << 20),
        cost_estimate=pl.CostEstimate(flops=5 * 10**9, bytes_accessed=10**5, transcendentals=0),
        name="gate",
    )(*values, *others)


def score_kernel(planes, helpers, blocks, mine_ref, theirs_ref, *refs):
    queries, rest = refs[:blocks], refs[blocks:]
    shard, helper = lax.axis_index("shard"), lax.axis_index("help")
    span, width = mine_ref.shape
    rank = span // planes
    count = (queries[0].shape[0] - TILE) * LANES // width
    pieces = count // LANES
    lifter = jnp.concatenate([mine_ref[...], theirs_ref[...]], axis=0)
    clusters = [
        ((shard ^ (INNER * d)) * helpers + (helper ^ side)).astype(F32) for side in (0, 1) for d in range(planes)
    ]
    total, tally = None, [None] * len(clusters)
    for q_ref in queries:
        rows = slabs(q_ref, count, width)
        tile = q_ref[count * width // LANES :, :].astype(F32)
        first, second = (
            jnp.concatenate([tile[k * pieces + j : k * pieces + j + 1] for j in range(pieces)], axis=1) for k in (0, 1)
        )
        lifted = contract(lifter, rows, ((1,), (1,)))
        kept = []
        for k, cluster in enumerate(clusters):
            hit = (first == cluster) | (second == cluster)
            kept.append(jnp.where(hit, lifted[k * rank : (k + 1) * rank], 0.0))
            here = hit.astype(F32)
            tally[k] = here if tally[k] is None else tally[k] + here
        high, low = halves(jnp.concatenate(kept, axis=0))
        part = contract(high, rows, ((1,), (0,)))
        if blocks > 1:
            part = part + contract(low, rows, ((1,), (0,)))
        total = part if total is None else total + part
    named = jnp.concatenate(
        [jnp.broadcast_to(jnp.sum(t, axis=1, keepdims=True), (rank, LANES)) for t in tally], axis=0
    )
    if len(rest) == 1:
        rest[0][:, :width] = total
        rest[0][:, width:] = named
    else:
        before, *outs = rest
        for side, out in enumerate(outs):
            part = slice(side * span, (side + 1) * span)
            out[:, :width] = (before[part, :width] + total[part]).astype(out.dtype)
            counts = before[part, width:] + named[part]
            out[:, width:] = (counts if out.dtype == F32 else digits(counts)).astype(out.dtype)


def digits(counts):
    high = jnp.floor(counts * (1.0 / 256.0))
    line = lax.broadcasted_iota(jnp.int32, counts.shape, 0)
    return jnp.where(line % 2 == 0, high, counts - 256.0 * high)


def fold_kernel(planes, mine_ref, theirs_ref, own_ref, *send_refs):
    rank, wide = own_ref.shape
    width = wide - LANES
    for d in range(planes):
        part = slice(d * rank, (d + 1) * rank)
        theirs = theirs_ref[part, :].astype(F32)
        total = mine_ref[part, :width] + theirs[:, :width]
        named = mine_ref[part, width:] + 256.0 * theirs[0:1, width:] + theirs[1:2, width:]
        if d == 0:
            own_ref[:, :width] = total
            own_ref[:, width:] = named
        else:
            ref = send_refs[d - 1]
            for k in range(width // LANES):
                ref[k * rank : (k + 1) * rank, :] = total[:, k * LANES : (k + 1) * LANES].astype(BF16)
            ref[rank * width // LANES :, :] = digits(named[:TILE]).astype(BF16)


def scale_kernel(resident_ref, own_ref, *refs):
    *parts, wide_ref, out_ref = refs
    rank, width = out_ref.shape
    total = own_ref[:, :width]
    queried = own_ref[0:1, width : width + 1]
    for part in parts:
        total = total + slabs(part, rank, width).astype(F32)
        tile = part[rank * width // LANES :, :].astype(F32)
        queried = queried + 256.0 * tile[0:1, 0:1] + tile[1:2, 0:1]
    resident = resident_ref[0:1, 0:1]
    factor = lax.rsqrt((queried + 1.0) * (queried + resident)) * (1.0 / width)
    wide_ref[...] = total * factor
    out_ref[...] = (total * factor).astype(BF16)


def sketch_kernel(helpers, mark_ref, resident_ref, points_ref, *refs):
    scaled, sketch_hbm, outs = refs[:helpers], refs[helpers], refs[helpers + 1 : -2]
    sketch_ref, sem = refs[-2:]
    rank, count = sketch_ref.shape
    mark = mark_ref[...]
    points = points_ref[...]
    blocks, rests = [], []
    for s in scaled:
        if s.dtype == F32:
            high, low = halves(s[...])
            blocks.append(high)
            rests.append(low)
        else:
            blocks.append(s[...])
    product = contract(jnp.concatenate(blocks + rests, axis=0), points, ((1,), (1,)))
    whole = [product[k * rank : (k + 1) * rank] for k in range(helpers)]
    for k in range(len(rests)):
        whole[k] = whole[k] + product[(helpers + k) * rank : (helpers + k + 1) * rank]
    sketch = whole[0]
    for d in range(1, helpers):
        sketch = jnp.where(mark == d, whole[d], sketch)
    sketch_ref[...] = sketch
    leaving = pltpu.make_async_copy(sketch_ref, sketch_hbm, sem)
    leaving.start()
    rounded = sketch.astype(BF16)
    rows = [jnp.where(mark == d, rounded, jnp.zeros((), BF16)) for d in range(helpers)]
    summed = contract(jnp.concatenate(rows, axis=0), points, ((1,), (0,)))
    for d, out in enumerate(outs):
        block = summed[d * rank : (d + 1) * rank] * lax.rsqrt(resident_ref[d : d + 1, 0:1])
        out[...] = block.astype(out.dtype)
    leaving.wait()


def swap(value, axis, d):
    return lax.ppermute(value, axis, [(i, i ^ d) for i in range(lax.axis_size(axis))])


def swaps(values, axis, unit=1):
    return [swap(value, axis, unit * d) for d, value in reversed([*enumerate(values, 1)])]


def shards(queries, probe_group, probe_local, points, point_cluster, test_matrix):
    groups = lax.axis_size("shard")
    helpers = lax.axis_size("help")
    planes = groups // INNER
    count = queries.shape[0]
    rank = test_matrix.shape[0]
    own_points, width = points.shape
    block = jax.ShapeDtypeStruct((rank, width), F32)
    sent = jax.ShapeDtypeStruct((rank, width), BF16)

    packed, mark, resident, own, *parts = pl.pallas_call(
        functools.partial(lift_kernel, helpers),
        out_shape=[
            jax.ShapeDtypeStruct((count * width // LANES + TILE, LANES), BF16),
            jax.ShapeDtypeStruct((1, own_points), jnp.int32),
            jax.ShapeDtypeStruct((8, LANES), F32),
            block,
            block,
        ]
        + [sent] * (helpers - 2),
        in_specs=[HBM] * 6,
        scratch_shapes=[
            pltpu.VMEM((2, count), jnp.int32),
            pltpu.VMEM((2, count), jnp.int32),
            pltpu.VMEM(point_cluster.shape, jnp.int32),
            pltpu.VMEM(test_matrix.shape, BF16),
            pltpu.VMEM(points.shape, BF16),
            pltpu.SemaphoreType.DMA((4 + CHUNKS + width // LANES,)),
        ],
        compiler_params=PARAMS,
        name="lift",
    )(*[in_hbm(a) for a in (queries, probe_group.T, probe_local.T, point_cluster, test_matrix, points)])
    lifter = pl.pallas_call(
        join_kernel,
        out_shape=sent,
        compiler_params=PARAMS,
        cost_estimate=pl.CostEstimate(flops=4 * 10**9, bytes_accessed=10**5, transcendentals=0),
        name="join",
    )(own, *swaps(parts, "help"))
    lifters = [lifter] + [swap(lifter, "shard", INNER * d) for d in range(1, planes)]
    index, axes = range(groups * helpers), ("shard", "help")
    one = [(i, i ^ (helpers if i % 2 == 0 else 2)) for i in index]
    two = [(i, i ^ (2 if i % 2 == 0 else helpers)) for i in index]
    far = lax.ppermute(packed, axes, one)
    (near,) = gate([lax.ppermute(packed, axes, two)], lifters[-1])
    across = lax.ppermute(near, axes, one)

    mine = pl.pallas_call(
        stack_kernel,
        out_shape=jax.ShapeDtypeStruct((planes * rank, width), BF16),
        in_specs=[VMEM] * planes + [ANY],
        compiler_params=PARAMS,
        cost_estimate=pl.CostEstimate(flops=25 * 10**8, bytes_accessed=10**5, transcendentals=0),
        name="stack",
    )(*lifters, far)
    theirs = swap(mine, "help", 1)

    wide = width + LANES
    begun = pl.pallas_call(
        functools.partial(score_kernel, planes, helpers, 3),
        out_shape=jax.ShapeDtypeStruct((2 * planes * rank, wide), F32),
        compiler_params=PARAMS,
        name="score",
    )(mine, theirs, packed, near, far)
    moments, passed = pl.pallas_call(
        functools.partial(score_kernel, planes, helpers, 1),
        out_shape=[jax.ShapeDtypeStruct((planes * rank, wide), kind) for kind in (F32, BF16)],
        compiler_params=PARAMS,
        name="score_last",
    )(mine, theirs, across, begun)
    folded = pl.pallas_call(
        functools.partial(fold_kernel, planes),
        out_shape=[jax.ShapeDtypeStruct((rank, wide), F32)]
        + [jax.ShapeDtypeStruct((rank * width // LANES + TILE, LANES), BF16)] * (planes - 1),
        compiler_params=PARAMS,
        name="fold",
    )(moments, swap(passed, "help", 1))
    moments = [folded[0]] + swaps(folded[1:], "shard", INNER)

    exact, scaled = pl.pallas_call(
        scale_kernel,
        out_shape=[block, sent],
        compiler_params=PARAMS,
        name="scale",
    )(resident, *moments)
    scaled = [exact, swap(exact, "help", 1)] + [swap(scaled, "help", d) for d in range(2, helpers)]

    sketch, regressor, *parts = pl.pallas_call(
        functools.partial(sketch_kernel, helpers),
        out_shape=[jax.ShapeDtypeStruct((rank, own_points), F32), block, block] + [sent] * (helpers - 2),
        out_specs=[HBM] + [VMEM] * helpers,
        scratch_shapes=[pltpu.VMEM((rank, own_points), F32), pltpu.SemaphoreType.DMA],
        compiler_params=PARAMS,
        name="sketch",
    )(mark, resident, points, *scaled)
    for part in swaps(parts, "help"):
        regressor = regressor + part.astype(F32)
    return sketch, regressor[None]


def solution(mesh):
    in_specs = (
        P(("shard", "help"), None),
        P(("shard", "help"), None),
        P(("shard", "help"), None),
        P(("shard", "help"), None),
        P("shard", None),
        P(None, ("shard", "help")),
    )
    out_specs = (P(None, ("shard", "help")), P(("shard", "help"), None, None))
    return jax.shard_map(shards, mesh=mesh, in_specs=in_specs, out_specs=out_specs, check_vma=False)
```

```python
import functools

import jax
import jax.numpy as jnp
from jax import lax
from jax.experimental import pallas as pl
from jax.experimental.pallas import tpu as pltpu
from jax.sharding import PartitionSpec as P

F32 = jnp.float32
BF16 = jnp.bfloat16
LANES = 128
TILE = 16
CHUNKS = 4
INNER = 2

ANY = pl.BlockSpec(memory_space=pl.ANY)
VMEM = pl.BlockSpec(memory_space=pltpu.VMEM)
VMEM = pl.BlockSpec(memory_space=pltpu.VMEM)
HBM = pl.BlockSpec(memory_space=pltpu.HBM)
PARAMS = pltpu.CompilerParams(vmem_limit_bytes=32 * 1024 * 1024)


def in_hbm(value):
    return pltpu.with_memory_space_constraint(value, pltpu.HBM)


def contract(a, b, dims):
    return lax.dot_general(a, b, (dims, ((), ())), preferred_element_type=F32)


def halves(value):
    high = value.astype(BF16)
    return high, (value - high.astype(F32)).astype(BF16)


def slabs(ref, rows, width):
    return jnp.concatenate([ref[k * rows : (k + 1) * rows, :] for k in range(width // LANES)], axis=1)


def lift_kernel(helpers, *refs):
    rows_hbm, group_hbm, local_hbm, ids_hbm, test_hbm, points_hbm = refs[:6]
    packed_ref, mark_ref, resident_ref = refs[6:9]
    outs = refs[9 : 9 + helpers]
    group_ref, local_ref, ids_ref, test_ref, points_ref, sems = refs[9 + helpers :]
    helper = lax.axis_index("help")
    asked, width = rows_hbm.shape
    rank, count = test_ref.shape
    piece = count // CHUNKS
    pairs = [(ids_hbm, ids_ref), (test_hbm, test_ref)]
    for k in range(CHUNKS):
        part = pl.ds(k * piece, piece)
        pairs.append((points_hbm.at[part], points_ref.at[part]))
    pairs += [(group_hbm, group_ref), (local_hbm, local_ref)]
    for k in range(width // LANES):
        pairs.append((rows_hbm.at[:, pl.ds(k * LANES, LANES)], packed_ref.at[pl.ds(k * asked, asked)]))
    copies = [pltpu.make_async_copy(*pair, sems.at[k]) for k, pair in enumerate(pairs)]
    for copy in copies:
        copy.start()
    copies[0].wait()
    everyone = ids_ref[...]
    mark = ids_ref[:, pl.ds(pl.multiple_of(helper * count, LANES), count)] ^ helper
    mark_ref[...] = mark
    for d in range(helpers):
        many = jnp.sum((everyone == (helper ^ d)).astype(F32), axis=1, keepdims=True)
        resident_ref[d : d + 1, :] = jnp.broadcast_to(many, (1, LANES))
    copies[1].wait()
    test = test_ref[...]
    rows = jnp.concatenate([jnp.where(mark == d, test, jnp.zeros((), BF16)) for d in range(helpers)], axis=0)
    total = None
    for k in range(CHUNKS):
        copies[2 + k].wait()
        part = slice(k * piece, (k + 1) * piece)
        more = contract(rows[:, part], points_ref[part, :], ((1,), (0,)))
        total = more if total is None else total + more
    for d, out in enumerate(outs):
        out[...] = total[d * rank : (d + 1) * rank].astype(out.dtype)
    for copy in copies[2 + CHUNKS :]:
        copy.wait()
    cluster = (group_ref[...] * helpers + local_ref[...]).astype(F32)
    line = [cluster[k : k + 1, j : j + LANES] for k in (0, 1) for j in range(0, asked, LANES)]
    line.append(jnp.zeros((TILE - len(line), LANES), F32))
    packed_ref[asked * width // LANES :, :] = jnp.concatenate(line, axis=0).astype(BF16)


def join_kernel(*refs):
    *parts, out = refs
    total = parts[0][...]
    for part in parts[1:]:
        total = total + part[...].astype(F32)
    out[...] = total.astype(out.dtype)


def stack_kernel(*refs):
    *parts, _, out = refs
    rank = parts[0].shape[0]
    for k, part in enumerate(parts):
        out[k * rank : (k + 1) * rank, :] = part[...]


def gate_kernel(*refs):
    pass


def gate(values, *others):
    return pl.pallas_call(
        gate_kernel,
        out_shape=[jax.ShapeDtypeStruct(value.shape, value.dtype) for value in values],
        in_specs=[ANY] * (len(values) + len(others)),
        out_specs=[ANY] * len(values),
        input_output_aliases={k: k for k in range(len(values))},
        compiler_params=pltpu.CompilerParams(vmem_limit_bytes=1 << 20),
        cost_estimate=pl.CostEstimate(flops=5 * 10**9, bytes_accessed=10**5, transcendentals=0),
        name="gate",
    )(*values, *others)


def score_kernel(planes, helpers, blocks, pieces, mine_ref, theirs_ref, *refs):
    queries, rest = refs[: blocks * pieces], refs[blocks * pieces :]
    if pieces > 1:
        queries = [jnp.concatenate([ref[...] for ref in queries], axis=0)]
    shard, helper = lax.axis_index("shard"), lax.axis_index("help")
    span, width = mine_ref.shape
    rank = span // planes
    count = (queries[0].shape[0] - TILE) * LANES // width
    lanes = count // LANES
    lifter = jnp.concatenate([mine_ref[...], theirs_ref[...]], axis=0)
    clusters = [
        ((shard ^ (INNER * d)) * helpers + (helper ^ side)).astype(F32) for side in (0, 1) for d in range(planes)
    ]
    total, tally = None, [None] * len(clusters)
    for q_ref in queries:
        rows = slabs(q_ref, count, width)
        tile = q_ref[count * width // LANES :, :].astype(F32)
        first, second = (
            jnp.concatenate([tile[k * lanes + j : k * lanes + j + 1] for j in range(lanes)], axis=1) for k in (0, 1)
        )
        lifted = contract(lifter, rows, ((1,), (1,)))
        kept = []
        for k, cluster in enumerate(clusters):
            hit = (first == cluster) | (second == cluster)
            kept.append(jnp.where(hit, lifted[k * rank : (k + 1) * rank], 0.0))
            here = hit.astype(F32)
            tally[k] = here if tally[k] is None else tally[k] + here
        high, low = halves(jnp.concatenate(kept, axis=0))
        part = contract(high, rows, ((1,), (0,)))
        if blocks > 1:
            part = part + contract(low, rows, ((1,), (0,)))
        total = part if total is None else total + part
    named = jnp.concatenate(
        [jnp.broadcast_to(jnp.sum(t, axis=1, keepdims=True), (rank, LANES)) for t in tally], axis=0
    )
    if len(rest) == 1:
        rest[0][:, :width] = total
        rest[0][:, width:] = named
    else:
        before, *outs = rest
        for side, out in enumerate(outs):
            part = slice(side * span, (side + 1) * span)
            out[:, :width] = (before[part, :width] + total[part]).astype(out.dtype)
            counts = before[part, width:] + named[part]
            out[:, width:] = (counts if out.dtype == F32 else digits(counts)).astype(out.dtype)


def digits(counts):
    high = jnp.floor(counts * (1.0 / 256.0))
    line = lax.broadcasted_iota(jnp.int32, counts.shape, 0)
    return jnp.where(line % 2 == 0, high, counts - 256.0 * high)


def fold_kernel(planes, mine_ref, theirs_ref, own_ref, *send_refs):
    rank, wide = own_ref.shape
    width = wide - LANES
    for d in range(planes):
        part = slice(d * rank, (d + 1) * rank)
        theirs = theirs_ref[part, :].astype(F32)
        total = mine_ref[part, :width] + theirs[:, :width]
        named = mine_ref[part, width:] + 256.0 * theirs[0:1, width:] + theirs[1:2, width:]
        if d == 0:
            own_ref[:, :width] = total
            own_ref[:, width:] = named
        else:
            ref = send_refs[d - 1]
            for k in range(width // LANES):
                ref[k * rank : (k + 1) * rank, :] = total[:, k * LANES : (k + 1) * LANES].astype(BF16)
            ref[rank * width // LANES :, :] = digits(named[:TILE]).astype(BF16)


def scale_kernel(resident_ref, own_ref, *refs):
    *parts, wide_ref, out_ref = refs
    rank, width = out_ref.shape
    total = own_ref[:, :width]
    queried = own_ref[0:1, width : width + 1]
    for part in parts:
        total = total + slabs(part, rank, width).astype(F32)
        tile = part[rank * width // LANES :, :].astype(F32)
        queried = queried + 256.0 * tile[0:1, 0:1] + tile[1:2, 0:1]
    resident = resident_ref[0:1, 0:1]
    factor = lax.rsqrt((queried + 1.0) * (queried + resident)) * (1.0 / width)
    wide_ref[...] = total * factor
    out_ref[...] = (total * factor).astype(BF16)


def sketch_kernel(helpers, mark_ref, resident_ref, points_ref, *refs):
    scaled, sketch_hbm, outs = refs[:helpers], refs[helpers], refs[helpers + 1 : -2]
    sketch_ref, sem = refs[-2:]
    rank, count = sketch_ref.shape
    mark = mark_ref[...]
    points = points_ref[...]
    blocks, rests = [], []
    for s in scaled:
        if s.dtype == F32:
            high, low = halves(s[...])
            blocks.append(high)
            rests.append(low)
        else:
            blocks.append(s[...])
    product = contract(jnp.concatenate(blocks + rests, axis=0), points, ((1,), (1,)))
    whole = [product[k * rank : (k + 1) * rank] for k in range(helpers)]
    for k in range(len(rests)):
        whole[k] = whole[k] + product[(helpers + k) * rank : (helpers + k + 1) * rank]
    sketch = whole[0]
    for d in range(1, helpers):
        sketch = jnp.where(mark == d, whole[d], sketch)
    sketch_ref[...] = sketch
    leaving = pltpu.make_async_copy(sketch_ref, sketch_hbm, sem)
    leaving.start()
    rounded = sketch.astype(BF16)
    rows = [jnp.where(mark == d, rounded, jnp.zeros((), BF16)) for d in range(helpers)]
    summed = contract(jnp.concatenate(rows, axis=0), points, ((1,), (0,)))
    for d, out in enumerate(outs):
        block = summed[d * rank : (d + 1) * rank] * lax.rsqrt(resident_ref[d : d + 1, 0:1])
        out[...] = block.astype(out.dtype)
    leaving.wait()


def swap(value, axis, d):
    return lax.ppermute(value, axis, [(i, i ^ d) for i in range(lax.axis_size(axis))])


def swaps(values, axis, unit=1):
    return [swap(value, axis, unit * d) for d, value in reversed([*enumerate(values, 1)])]


def shards(queries, probe_group, probe_local, points, point_cluster, test_matrix):
    groups = lax.axis_size("shard")
    helpers = lax.axis_size("help")
    planes = groups // INNER
    count = queries.shape[0]
    rank = test_matrix.shape[0]
    own_points, width = points.shape
    block = jax.ShapeDtypeStruct((rank, width), F32)
    sent = jax.ShapeDtypeStruct((rank, width), BF16)

    packed, mark, resident, own, *parts = pl.pallas_call(
        functools.partial(lift_kernel, helpers),
        out_shape=[
            jax.ShapeDtypeStruct((count * width // LANES + TILE, LANES), BF16),
            jax.ShapeDtypeStruct((1, own_points), jnp.int32),
            jax.ShapeDtypeStruct((8, LANES), F32),
            block,
            block,
        ]
        + [sent] * (helpers - 2),
        in_specs=[HBM] * 6,
        scratch_shapes=[
            pltpu.VMEM((2, count), jnp.int32),
            pltpu.VMEM((2, count), jnp.int32),
            pltpu.VMEM(point_cluster.shape, jnp.int32),
            pltpu.VMEM(test_matrix.shape, BF16),
            pltpu.VMEM(points.shape, BF16),
            pltpu.SemaphoreType.DMA((4 + CHUNKS + width // LANES,)),
        ],
        compiler_params=PARAMS,
        name="lift",
    )(*[in_hbm(a) for a in (queries, probe_group.T, probe_local.T, point_cluster, test_matrix, points)])
    lifter = pl.pallas_call(
        join_kernel,
        out_shape=sent,
        compiler_params=PARAMS,
        cost_estimate=pl.CostEstimate(flops=4 * 10**9, bytes_accessed=10**5, transcendentals=0),
        name="join",
    )(own, *swaps(parts, "help"))
    lifters = [lifter] + [swap(lifter, "shard", INNER * d) for d in range(1, planes)]
    index, axes = range(groups * helpers), ("shard", "help")
    one = [(i, i ^ (helpers if i % 2 == 0 else 2)) for i in index]
    two = [(i, i ^ (2 if i % 2 == 0 else helpers)) for i in index]
    far = lax.ppermute(packed, axes, one)
    (near,) = gate([lax.ppermute(packed, axes, two)], lifters[-1])
    cut = width // LANES // 2 * count
    across = [lax.ppermute(near[:cut], axes, one), lax.ppermute(far[cut:], axes, two)]

    mine = pl.pallas_call(
        stack_kernel,
        out_shape=jax.ShapeDtypeStruct((planes * rank, width), BF16),
        in_specs=[VMEM] * planes + [ANY],
        compiler_params=PARAMS,
        cost_estimate=pl.CostEstimate(flops=25 * 10**8, bytes_accessed=10**5, transcendentals=0),
        name="stack",
    )(*lifters, far)
    theirs = swap(mine, "help", 1)

    wide = width + LANES
    begun = pl.pallas_call(
        functools.partial(score_kernel, planes, helpers, 3, 1),
        out_shape=jax.ShapeDtypeStruct((2 * planes * rank, wide), F32),
        compiler_params=PARAMS,
        name="score",
    )(mine, theirs, packed, near, far)
    moments, passed = pl.pallas_call(
        functools.partial(score_kernel, planes, helpers, 1, 2),
        out_shape=[jax.ShapeDtypeStruct((planes * rank, wide), kind) for kind in (F32, BF16)],
        compiler_params=PARAMS,
        name="score_last",
    )(mine, theirs, *across, begun)
    folded = pl.pallas_call(
        functools.partial(fold_kernel, planes),
        out_shape=[jax.ShapeDtypeStruct((rank, wide), F32)]
        + [jax.ShapeDtypeStruct((rank * width // LANES + TILE, LANES), BF16)] * (planes - 1),
        compiler_params=PARAMS,
        name="fold",
    )(moments, swap(passed, "help", 1))
    moments = [folded[0]] + swaps(folded[1:], "shard", INNER)

    exact, scaled = pl.pallas_call(
        scale_kernel,
        out_shape=[block, sent],
        compiler_params=PARAMS,
        name="scale",
    )(resident, *moments)
    scaled = [exact, swap(exact, "help", 1)] + [swap(scaled, "help", d) for d in range(2, helpers)]

    sketch, regressor, *parts = pl.pallas_call(
        functools.partial(sketch_kernel, helpers),
        out_shape=[jax.ShapeDtypeStruct((rank, own_points), F32), block, block] + [sent] * (helpers - 2),
        out_specs=[HBM] + [VMEM] * helpers,
        scratch_shapes=[pltpu.VMEM((rank, own_points), F32), pltpu.SemaphoreType.DMA],
        compiler_params=PARAMS,
        name="sketch",
    )(mark, resident, points, *scaled)
    for part in swaps(parts, "help"):
        regressor = regressor + part.astype(F32)
    return sketch, regressor[None]


def solution(mesh):
    in_specs = (
        P(("shard", "help"), None),
        P(("shard", "help"), None),
        P(("shard", "help"), None),
        P(("shard", "help"), None),
        P("shard", None),
        P(None, ("shard", "help")),
    )
    out_specs = (P(None, ("shard", "help")), P(("shard", "help"), None, None))
    return jax.shard_map(shards, mesh=mesh, in_specs=in_specs, out_specs=out_specs, check_vma=False)
```

```python
import functools

import jax
import jax.numpy as jnp
from jax import lax
from jax.experimental import pallas as pl
from jax.experimental.pallas import tpu as pltpu
from jax.sharding import PartitionSpec as P

F32 = jnp.float32
BF16 = jnp.bfloat16
LANES = 128
TILE = 16
CHUNKS = 2
INNER = 2

ANY = pl.BlockSpec(memory_space=pl.ANY)
VMEM = pl.BlockSpec(memory_space=pltpu.VMEM)
VMEM = pl.BlockSpec(memory_space=pltpu.VMEM)
HBM = pl.BlockSpec(memory_space=pltpu.HBM)
PARAMS = pltpu.CompilerParams(vmem_limit_bytes=32 * 1024 * 1024)


def in_hbm(value):
    return pltpu.with_memory_space_constraint(value, pltpu.HBM)


def contract(a, b, dims):
    return lax.dot_general(a, b, (dims, ((), ())), preferred_element_type=F32)


def halves(value):
    high = value.astype(BF16)
    return high, (value - high.astype(F32)).astype(BF16)


def slabs(ref, rows, width):
    return jnp.concatenate([ref[k * rows : (k + 1) * rows, :] for k in range(width // LANES)], axis=1)


def lift_kernel(helpers, *refs):
    rows_hbm, group_hbm, local_hbm, ids_hbm, test_hbm, points_hbm = refs[:6]
    packed_ref, mark_ref, resident_ref = refs[6:9]
    outs = refs[9 : 9 + helpers]
    group_ref, local_ref, ids_ref, test_ref, points_ref, sems = refs[9 + helpers :]
    helper = lax.axis_index("help")
    asked, width = rows_hbm.shape
    rank, count = test_ref.shape
    piece = count // CHUNKS
    pairs = [(ids_hbm, ids_ref), (test_hbm, test_ref)]
    for k in range(CHUNKS):
        part = pl.ds(k * piece, piece)
        pairs.append((points_hbm.at[part], points_ref.at[part]))
    pairs += [(group_hbm, group_ref), (local_hbm, local_ref)]
    for k in range(width // LANES):
        pairs.append((rows_hbm.at[:, pl.ds(k * LANES, LANES)], packed_ref.at[pl.ds(k * asked, asked)]))
    copies = [pltpu.make_async_copy(*pair, sems.at[k]) for k, pair in enumerate(pairs)]
    for copy in copies:
        copy.start()
    copies[0].wait()
    everyone = ids_ref[...]
    mark = ids_ref[:, pl.ds(pl.multiple_of(helper * count, LANES), count)] ^ helper
    mark_ref[...] = mark
    for d in range(helpers):
        many = jnp.sum((everyone == (helper ^ d)).astype(F32), axis=1, keepdims=True)
        resident_ref[d : d + 1, :] = jnp.broadcast_to(many, (1, LANES))
    copies[1].wait()
    test = test_ref[...]
    rows = jnp.concatenate([jnp.where(mark == d, test, jnp.zeros((), BF16)) for d in range(helpers)], axis=0)
    total = None
    for k in range(CHUNKS):
        copies[2 + k].wait()
        part = slice(k * piece, (k + 1) * piece)
        more = contract(rows[:, part], points_ref[part, :], ((1,), (0,)))
        total = more if total is None else total + more
    for d, out in enumerate(outs):
        out[...] = total[d * rank : (d + 1) * rank].astype(out.dtype)
    for copy in copies[2 + CHUNKS :]:
        copy.wait()
    cluster = (group_ref[...] * helpers + local_ref[...]).astype(F32)
    line = [cluster[k : k + 1, j : j + LANES] for k in (0, 1) for j in range(0, asked, LANES)]
    line.append(jnp.zeros((TILE - len(line), LANES), F32))
    packed_ref[asked * width // LANES :, :] = jnp.concatenate(line, axis=0).astype(BF16)


def join_kernel(*refs):
    *parts, out = refs
    total = parts[0][...]
    for part in parts[1:]:
        total = total + part[...].astype(F32)
    out[...] = total.astype(out.dtype)


def stack_kernel(*refs):
    *parts, _, out = refs
    rank = parts[0].shape[0]
    for k, part in enumerate(parts):
        out[k * rank : (k + 1) * rank, :] = part[...]


def gate_kernel(*refs):
    pass


def gate(values, *others):
    return pl.pallas_call(
        gate_kernel,
        out_shape=[jax.ShapeDtypeStruct(value.shape, value.dtype) for value in values],
        in_specs=[ANY] * (len(values) + len(others)),
        out_specs=[ANY] * len(values),
        input_output_aliases={k: k for k in range(len(values))},
        compiler_params=pltpu.CompilerParams(vmem_limit_bytes=1 << 20),
        cost_estimate=pl.CostEstimate(flops=5 * 10**9, bytes_accessed=10**5, transcendentals=0),
        name="gate",
    )(*values, *others)


def score_kernel(planes, helpers, blocks, mine_ref, theirs_ref, *refs):
    queries, rest = refs[:blocks], refs[blocks:]
    shard, helper = lax.axis_index("shard"), lax.axis_index("help")
    span, width = mine_ref.shape
    rank = span // planes
    count = (queries[0].shape[0] - TILE) * LANES // width
    pieces = count // LANES
    lifter = jnp.concatenate([mine_ref[...], theirs_ref[...]], axis=0)
    clusters = [
        ((shard ^ (INNER * d)) * helpers + (helper ^ side)).astype(F32) for side in (0, 1) for d in range(planes)
    ]
    total, tally = None, [None] * len(clusters)
    for q_ref in queries:
        rows = slabs(q_ref, count, width)
        tile = q_ref[count * width // LANES :, :].astype(F32)
        first, second = (
            jnp.concatenate([tile[k * pieces + j : k * pieces + j + 1] for j in range(pieces)], axis=1) for k in (0, 1)
        )
        lifted = contract(lifter, rows, ((1,), (1,)))
        kept = []
        for k, cluster in enumerate(clusters):
            hit = (first == cluster) | (second == cluster)
            kept.append(jnp.where(hit, lifted[k * rank : (k + 1) * rank], 0.0))
            here = hit.astype(F32)
            tally[k] = here if tally[k] is None else tally[k] + here
        high, low = halves(jnp.concatenate(kept, axis=0))
        part = contract(high, rows, ((1,), (0,)))
        if blocks > 1:
            part = part + contract(low, rows, ((1,), (0,)))
        total = part if total is None else total + part
    named = jnp.concatenate(
        [jnp.broadcast_to(jnp.sum(t, axis=1, keepdims=True), (rank, LANES)) for t in tally], axis=0
    )
    if len(rest) == 1:
        rest[0][:, :width] = total
        rest[0][:, width:] = named
    else:
        before, *outs = rest
        for side, out in enumerate(outs):
            part = slice(side * span, (side + 1) * span)
            out[:, :width] = (before[part, :width] + total[part]).astype(out.dtype)
            counts = before[part, width:] + named[part]
            out[:, width:] = (counts if out.dtype == F32 else digits(counts)).astype(out.dtype)


def digits(counts):
    high = jnp.floor(counts * (1.0 / 256.0))
    line = lax.broadcasted_iota(jnp.int32, counts.shape, 0)
    return jnp.where(line % 2 == 0, high, counts - 256.0 * high)


def fold_kernel(planes, mine_ref, theirs_ref, own_ref, *send_refs):
    rank, wide = own_ref.shape
    width = wide - LANES
    for d in range(planes):
        part = slice(d * rank, (d + 1) * rank)
        theirs = theirs_ref[part, :].astype(F32)
        total = mine_ref[part, :width] + theirs[:, :width]
        named = mine_ref[part, width:] + 256.0 * theirs[0:1, width:] + theirs[1:2, width:]
        if d == 0:
            own_ref[:, :width] = total
            own_ref[:, width:] = named
        else:
            ref = send_refs[d - 1]
            for k in range(width // LANES):
                ref[k * rank : (k + 1) * rank, :] = total[:, k * LANES : (k + 1) * LANES].astype(BF16)
            ref[rank * width // LANES :, :] = digits(named[:TILE]).astype(BF16)


def scale_kernel(resident_ref, own_ref, *refs):
    *parts, wide_ref, out_ref = refs
    rank, width = out_ref.shape
    total = own_ref[:, :width]
    queried = own_ref[0:1, width : width + 1]
    for part in parts:
        total = total + slabs(part, rank, width).astype(F32)
        tile = part[rank * width // LANES :, :].astype(F32)
        queried = queried + 256.0 * tile[0:1, 0:1] + tile[1:2, 0:1]
    resident = resident_ref[0:1, 0:1]
    factor = lax.rsqrt((queried + 1.0) * (queried + resident)) * (1.0 / width)
    wide_ref[...] = total * factor
    out_ref[...] = (total * factor).astype(BF16)


def sketch_kernel(helpers, mark_ref, resident_ref, points_ref, *refs):
    scaled, sketch_hbm, outs = refs[:helpers], refs[helpers], refs[helpers + 1 : -2]
    sketch_ref, sem = refs[-2:]
    rank, count = sketch_ref.shape
    mark = mark_ref[...]
    points = points_ref[...]
    blocks, rests = [], []
    for s in scaled:
        if s.dtype == F32:
            high, low = halves(s[...])
            blocks.append(high)
            rests.append(low)
        else:
            blocks.append(s[...])
    product = contract(jnp.concatenate(blocks + rests, axis=0), points, ((1,), (1,)))
    whole = [product[k * rank : (k + 1) * rank] for k in range(helpers)]
    for k in range(len(rests)):
        whole[k] = whole[k] + product[(helpers + k) * rank : (helpers + k + 1) * rank]
    sketch = whole[0]
    for d in range(1, helpers):
        sketch = jnp.where(mark == d, whole[d], sketch)
    sketch_ref[...] = sketch
    leaving = pltpu.make_async_copy(sketch_ref, sketch_hbm, sem)
    leaving.start()
    rounded = sketch.astype(BF16)
    rows = [jnp.where(mark == d, rounded, jnp.zeros((), BF16)) for d in range(helpers)]
    summed = contract(jnp.concatenate(rows, axis=0), points, ((1,), (0,)))
    for d, out in enumerate(outs):
        block = summed[d * rank : (d + 1) * rank] * lax.rsqrt(resident_ref[d : d + 1, 0:1])
        out[...] = block.astype(out.dtype)
    leaving.wait()


def swap(value, axis, d):
    return lax.ppermute(value, axis, [(i, i ^ d) for i in range(lax.axis_size(axis))])


def swaps(values, axis, unit=1):
    return [swap(value, axis, unit * d) for d, value in reversed([*enumerate(values, 1)])]


def shards(queries, probe_group, probe_local, points, point_cluster, test_matrix):
    groups = lax.axis_size("shard")
    helpers = lax.axis_size("help")
    planes = groups // INNER
    count = queries.shape[0]
    rank = test_matrix.shape[0]
    own_points, width = points.shape
    block = jax.ShapeDtypeStruct((rank, width), F32)
    sent = jax.ShapeDtypeStruct((rank, width), BF16)

    packed, mark, resident, own, *parts = pl.pallas_call(
        functools.partial(lift_kernel, helpers),
        out_shape=[
            jax.ShapeDtypeStruct((count * width // LANES + TILE, LANES), BF16),
            jax.ShapeDtypeStruct((1, own_points), jnp.int32),
            jax.ShapeDtypeStruct((8, LANES), F32),
            block,
            block,
        ]
        + [sent] * (helpers - 2),
        in_specs=[HBM] * 6,
        scratch_shapes=[
            pltpu.VMEM((2, count), jnp.int32),
            pltpu.VMEM((2, count), jnp.int32),
            pltpu.VMEM(point_cluster.shape, jnp.int32),
            pltpu.VMEM(test_matrix.shape, BF16),
            pltpu.VMEM(points.shape, BF16),
            pltpu.SemaphoreType.DMA((4 + CHUNKS + width // LANES,)),
        ],
        compiler_params=PARAMS,
        name="lift",
    )(*[in_hbm(a) for a in (queries, probe_group.T, probe_local.T, point_cluster, test_matrix, points)])
    lifter = pl.pallas_call(
        join_kernel,
        out_shape=sent,
        compiler_params=PARAMS,
        cost_estimate=pl.CostEstimate(flops=4 * 10**9, bytes_accessed=10**5, transcendentals=0),
        name="join",
    )(own, *swaps(parts, "help"))
    lifters = [lifter] + [swap(lifter, "shard", INNER * d) for d in range(1, planes)]
    index, axes = range(groups * helpers), ("shard", "help")
    one = [(i, i ^ (helpers if i % 2 == 0 else 2)) for i in index]
    two = [(i, i ^ (2 if i % 2 == 0 else helpers)) for i in index]
    far = lax.ppermute(packed, axes, one)
    (near,) = gate([lax.ppermute(packed, axes, two)], lifters[-1])
    across = lax.ppermute(near, axes, one)

    mine = pl.pallas_call(
        stack_kernel,
        out_shape=jax.ShapeDtypeStruct((planes * rank, width), BF16),
        in_specs=[VMEM] * planes + [ANY],
        compiler_params=PARAMS,
        cost_estimate=pl.CostEstimate(flops=25 * 10**8, bytes_accessed=10**5, transcendentals=0),
        name="stack",
    )(*lifters, far)
    theirs = swap(mine, "help", 1)

    wide = width + LANES
    begun = pl.pallas_call(
        functools.partial(score_kernel, planes, helpers, 3),
        out_shape=jax.ShapeDtypeStruct((2 * planes * rank, wide), F32),
        compiler_params=PARAMS,
        name="score",
    )(mine, theirs, packed, near, far)
    moments, passed = pl.pallas_call(
        functools.partial(score_kernel, planes, helpers, 1),
        out_shape=[jax.ShapeDtypeStruct((planes * rank, wide), kind) for kind in (F32, BF16)],
        compiler_params=PARAMS,
        name="score_last",
    )(mine, theirs, across, begun)
    folded = pl.pallas_call(
        functools.partial(fold_kernel, planes),
        out_shape=[jax.ShapeDtypeStruct((rank, wide), F32)]
        + [jax.ShapeDtypeStruct((rank * width // LANES + TILE, LANES), BF16)] * (planes - 1),
        compiler_params=PARAMS,
        name="fold",
    )(moments, swap(passed, "help", 1))
    moments = [folded[0]] + swaps(folded[1:], "shard", INNER)

    exact, scaled = pl.pallas_call(
        scale_kernel,
        out_shape=[block, sent],
        compiler_params=PARAMS,
        name="scale",
    )(resident, *moments)
    scaled = [exact, swap(exact, "help", 1)] + [swap(scaled, "help", d) for d in range(2, helpers)]

    sketch, regressor, *parts = pl.pallas_call(
        functools.partial(sketch_kernel, helpers),
        out_shape=[jax.ShapeDtypeStruct((rank, own_points), F32), block, block] + [sent] * (helpers - 2),
        out_specs=[HBM] + [VMEM] * helpers,
        scratch_shapes=[pltpu.VMEM((rank, own_points), F32), pltpu.SemaphoreType.DMA],
        compiler_params=PARAMS,
        name="sketch",
    )(mark, resident, points, *scaled)
    for part in swaps(parts, "help"):
        regressor = regressor + part.astype(F32)
    return sketch, regressor[None]


def solution(mesh):
    in_specs = (
        P(("shard", "help"), None),
        P(("shard", "help"), None),
        P(("shard", "help"), None),
        P(("shard", "help"), None),
        P("shard", None),
        P(None, ("shard", "help")),
    )
    out_specs = (P(None, ("shard", "help")), P(("shard", "help"), None, None))
    return jax.shard_map(shards, mesh=mesh, in_specs=in_specs, out_specs=out_specs, check_vma=False)
```

```python
import functools

import jax
import jax.numpy as jnp
from jax import lax
from jax.experimental import pallas as pl
from jax.experimental.pallas import tpu as pltpu
from jax.sharding import PartitionSpec as P

F32 = jnp.float32
BF16 = jnp.bfloat16
LANES = 128
TILE = 16
CHUNKS = 4
INNER = 2

ANY = pl.BlockSpec(memory_space=pl.ANY)
VMEM = pl.BlockSpec(memory_space=pltpu.VMEM)
VMEM = pl.BlockSpec(memory_space=pltpu.VMEM)
HBM = pl.BlockSpec(memory_space=pltpu.HBM)
PARAMS = pltpu.CompilerParams(vmem_limit_bytes=32 * 1024 * 1024)


def in_hbm(value):
    return pltpu.with_memory_space_constraint(value, pltpu.HBM)


def contract(a, b, dims):
    return lax.dot_general(a, b, (dims, ((), ())), preferred_element_type=F32)


def halves(value):
    high = value.astype(BF16)
    return high, (value - high.astype(F32)).astype(BF16)


def slabs(ref, rows, width):
    return jnp.concatenate([ref[k * rows : (k + 1) * rows, :] for k in range(width // LANES)], axis=1)


def lift_kernel(helpers, *refs):
    rows_hbm, group_hbm, local_hbm, ids_hbm, test_hbm, points_hbm = refs[:6]
    packed_ref, mark_ref, resident_ref = refs[6:9]
    outs = refs[9 : 9 + helpers]
    group_ref, local_ref, ids_ref, test_ref, points_ref, sems = refs[9 + helpers :]
    helper = lax.axis_index("help")
    asked, width = rows_hbm.shape
    rank, count = test_ref.shape
    piece = count // CHUNKS
    pairs = [(ids_hbm, ids_ref), (test_hbm, test_ref)]
    for k in range(CHUNKS):
        part = pl.ds(k * piece, piece)
        pairs.append((points_hbm.at[part], points_ref.at[part]))
    pairs += [(group_hbm, group_ref), (local_hbm, local_ref)]
    for k in range(width // LANES):
        pairs.append((rows_hbm.at[:, pl.ds(k * LANES, LANES)], packed_ref.at[pl.ds(k * asked, asked)]))
    copies = [pltpu.make_async_copy(*pair, sems.at[k]) for k, pair in enumerate(pairs)]
    for copy in copies:
        copy.start()
    copies[0].wait()
    everyone = ids_ref[...]
    mark = ids_ref[:, pl.ds(pl.multiple_of(helper * count, LANES), count)] ^ helper
    mark_ref[...] = mark
    for d in range(helpers):
        many = jnp.sum((everyone == (helper ^ d)).astype(F32), axis=1, keepdims=True)
        resident_ref[d : d + 1, :] = jnp.broadcast_to(many, (1, LANES))
    copies[1].wait()
    test = test_ref[...]
    rows = jnp.concatenate([jnp.where(mark == d, test, jnp.zeros((), BF16)) for d in range(helpers)], axis=0)
    total = None
    for k in range(CHUNKS):
        copies[2 + k].wait()
        part = slice(k * piece, (k + 1) * piece)
        more = contract(rows[:, part], points_ref[part, :], ((1,), (0,)))
        total = more if total is None else total + more
    for d, out in enumerate(outs):
        out[...] = total[d * rank : (d + 1) * rank].astype(out.dtype)
    for copy in copies[2 + CHUNKS :]:
        copy.wait()
    cluster = (group_ref[...] * helpers + local_ref[...]).astype(F32)
    line = [cluster[k : k + 1, j : j + LANES] for k in (0, 1) for j in range(0, asked, LANES)]
    line.append(jnp.zeros((TILE - len(line), LANES), F32))
    packed_ref[asked * width // LANES :, :] = jnp.concatenate(line, axis=0).astype(BF16)


def join_kernel(*refs):
    *parts, out = refs
    total = parts[0][...]
    for part in parts[1:]:
        total = total + part[...].astype(F32)
    out[...] = total.astype(out.dtype)


def stack_kernel(*refs):
    *parts, _, out = refs
    rank = parts[0].shape[0]
    for k, part in enumerate(parts):
        out[k * rank : (k + 1) * rank, :] = part[...]


def gate_kernel(*refs):
    pass


def gate(values, *others):
    return pl.pallas_call(
        gate_kernel,
        out_shape=[jax.ShapeDtypeStruct(value.shape, value.dtype) for value in values],
        in_specs=[ANY] * (len(values) + len(others)),
        out_specs=[ANY] * len(values),
        input_output_aliases={k: k for k in range(len(values))},
        compiler_params=pltpu.CompilerParams(vmem_limit_bytes=1 << 20),
        cost_estimate=pl.CostEstimate(flops=5 * 10**9, bytes_accessed=10**5, transcendentals=0),
        name="gate",
    )(*values, *others)


def score_kernel(planes, helpers, blocks, mine_ref, theirs_ref, *refs):
    queries, rest = refs[:blocks], refs[blocks:]
    shard, helper = lax.axis_index("shard"), lax.axis_index("help")
    span, width = mine_ref.shape
    rank = span // planes
    count = (queries[0].shape[0] - TILE) * LANES // width
    pieces = count // LANES
    lifter = jnp.concatenate([mine_ref[...], theirs_ref[...]], axis=0)
    clusters = [
        ((shard ^ (INNER * d)) * helpers + (helper ^ side)).astype(F32) for side in (0, 1) for d in range(planes)
    ]
    total, tally = None, [None] * len(clusters)
    for q_ref in queries:
        rows = slabs(q_ref, count, width)
        tile = q_ref[count * width // LANES :, :].astype(F32)
        first, second = (
            jnp.concatenate([tile[k * pieces + j : k * pieces + j + 1] for j in range(pieces)], axis=1) for k in (0, 1)
        )
        lifted = contract(lifter, rows, ((1,), (1,)))
        kept = []
        for k, cluster in enumerate(clusters):
            hit = (first == cluster) | (second == cluster)
            kept.append(jnp.where(hit, lifted[k * rank : (k + 1) * rank], 0.0))
            here = hit.astype(F32)
            tally[k] = here if tally[k] is None else tally[k] + here
        high, low = halves(jnp.concatenate(kept, axis=0))
        part = contract(high, rows, ((1,), (0,)))
        if blocks > 1:
            part = part + contract(low, rows, ((1,), (0,)))
        total = part if total is None else total + part
    named = jnp.concatenate(
        [jnp.broadcast_to(jnp.sum(t, axis=1, keepdims=True), (rank, LANES)) for t in tally], axis=0
    )
    if len(rest) == 1:
        rest[0][:, :width] = total
        rest[0][:, width:] = named
    else:
        before, *outs = rest
        for side, out in enumerate(outs):
            part = slice(side * span, (side + 1) * span)
            out[:, :width] = (before[part, :width] + total[part]).astype(out.dtype)
            counts = before[part, width:] + named[part]
            out[:, width:] = (counts if out.dtype == F32 else digits(counts)).astype(out.dtype)


def digits(counts):
    high = jnp.floor(counts * (1.0 / 256.0))
    line = lax.broadcasted_iota(jnp.int32, counts.shape, 0)
    return jnp.where(line % 2 == 0, high, counts - 256.0 * high)


def fold_kernel(planes, mine_ref, theirs_ref, own_ref, *send_refs):
    rank, wide = own_ref.shape
    width = wide - LANES
    for d in range(planes):
        part = slice(d * rank, (d + 1) * rank)
        theirs = theirs_ref[part, :].astype(F32)
        total = mine_ref[part, :width] + theirs[:, :width]
        named = mine_ref[part, width:] + 256.0 * theirs[0:1, width:] + theirs[1:2, width:]
        if d == 0:
            own_ref[:, :width] = total
            own_ref[:, width:] = named
        else:
            ref = send_refs[d - 1]
            for k in range(width // LANES):
                ref[k * rank : (k + 1) * rank, :] = total[:, k * LANES : (k + 1) * LANES].astype(BF16)
            ref[rank * width // LANES :, :] = digits(named[:TILE]).astype(BF16)


def scale_kernel(resident_ref, own_ref, *refs):
    *parts, wide_ref, out_ref = refs
    rank, width = out_ref.shape
    total = own_ref[:, :width]
    queried = own_ref[0:1, width : width + 1]
    for part in parts:
        total = total + slabs(part, rank, width).astype(F32)
        tile = part[rank * width // LANES :, :].astype(F32)
        queried = queried + 256.0 * tile[0:1, 0:1] + tile[1:2, 0:1]
    resident = resident_ref[0:1, 0:1]
    factor = lax.rsqrt((queried + 1.0) * (queried + resident)) * (1.0 / width)
    wide_ref[...] = total * factor
    out_ref[...] = (total * factor).astype(BF16)


def sketch_kernel(helpers, mark_ref, resident_ref, points_ref, *refs):
    scaled, sketch_hbm, outs = refs[:helpers], refs[helpers], refs[helpers + 1 : -2]
    sketch_ref, sem = refs[-2:]
    rank, count = sketch_ref.shape
    mark = mark_ref[...]
    points = points_ref[...]
    blocks, rests = [], []
    for s in scaled:
        if s.dtype == F32:
            high, low = halves(s[...])
            blocks.append(high)
            rests.append(low)
        else:
            blocks.append(s[...])
    product = contract(jnp.concatenate(blocks + rests, axis=0), points, ((1,), (1,)))
    whole = [product[k * rank : (k + 1) * rank] for k in range(helpers)]
    for k in range(len(rests)):
        whole[k] = whole[k] + product[(helpers + k) * rank : (helpers + k + 1) * rank]
    sketch = whole[0]
    for d in range(1, helpers):
        sketch = jnp.where(mark == d, whole[d], sketch)
    sketch_ref[...] = sketch
    leaving = pltpu.make_async_copy(sketch_ref, sketch_hbm, sem)
    leaving.start()
    rounded = sketch.astype(BF16)
    rows = [jnp.where(mark == d, rounded, jnp.zeros((), BF16)) for d in range(helpers)]
    summed = contract(jnp.concatenate(rows, axis=0), points, ((1,), (0,)))
    for d, out in enumerate(outs):
        block = summed[d * rank : (d + 1) * rank] * lax.rsqrt(resident_ref[d : d + 1, 0:1])
        out[...] = block.astype(out.dtype)
    leaving.wait()


def swap(value, axis, d):
    return lax.ppermute(value, axis, [(i, i ^ d) for i in range(lax.axis_size(axis))])


def swaps(values, axis, unit=1):
    return [swap(value, axis, unit * d) for d, value in reversed([*enumerate(values, 1)])]


def shards(queries, probe_group, probe_local, points, point_cluster, test_matrix):
    groups = lax.axis_size("shard")
    helpers = lax.axis_size("help")
    planes = groups // INNER
    count = queries.shape[0]
    rank = test_matrix.shape[0]
    own_points, width = points.shape
    block = jax.ShapeDtypeStruct((rank, width), F32)
    sent = jax.ShapeDtypeStruct((rank, width), BF16)

    packed, mark, resident, own, *parts = pl.pallas_call(
        functools.partial(lift_kernel, helpers),
        out_shape=[
            jax.ShapeDtypeStruct((count * width // LANES + TILE, LANES), BF16),
            jax.ShapeDtypeStruct((1, own_points), jnp.int32),
            jax.ShapeDtypeStruct((8, LANES), F32),
            block,
            block,
        ]
        + [sent] * (helpers - 2),
        in_specs=[HBM] * 6,
        scratch_shapes=[
            pltpu.VMEM((2, count), jnp.int32),
            pltpu.VMEM((2, count), jnp.int32),
            pltpu.VMEM(point_cluster.shape, jnp.int32),
            pltpu.VMEM(test_matrix.shape, BF16),
            pltpu.VMEM(points.shape, BF16),
            pltpu.SemaphoreType.DMA((4 + CHUNKS + width // LANES,)),
        ],
        compiler_params=PARAMS,
        name="lift",
    )(*[in_hbm(a) for a in (queries, probe_group.T, probe_local.T, point_cluster, test_matrix, points)])
    lifter = pl.pallas_call(
        join_kernel,
        out_shape=sent,
        compiler_params=PARAMS,
        cost_estimate=pl.CostEstimate(flops=4 * 10**9, bytes_accessed=10**5, transcendentals=0),
        name="join",
    )(own, *swaps(parts, "help"))
    lifters = [lifter] + [swap(lifter, "shard", INNER * d) for d in range(1, planes)]
    index, axes = range(groups * helpers), ("shard", "help")
    one = [(i, i ^ (helpers if i % 2 == 0 else 2)) for i in index]
    two = [(i, i ^ (2 if i % 2 == 0 else helpers)) for i in index]
    far = lax.ppermute(packed, axes, one)
    (near,) = gate([lax.ppermute(packed, axes, two)], lifters[-1])
    across = lax.ppermute(near, axes, one)

    mine = pl.pallas_call(
        stack_kernel,
        out_shape=jax.ShapeDtypeStruct((planes * rank, width), BF16),
        in_specs=[VMEM] * planes + [ANY],
        compiler_params=PARAMS,
        cost_estimate=pl.CostEstimate(flops=25 * 10**8, bytes_accessed=10**5, transcendentals=0),
        name="stack",
    )(*lifters, far)
    theirs = swap(mine, "help", 1)

    wide = width + LANES
    begun = pl.pallas_call(
        functools.partial(score_kernel, planes, helpers, 3),
        out_shape=jax.ShapeDtypeStruct((2 * planes * rank, wide), F32),
        compiler_params=PARAMS,
        name="score",
    )(mine, theirs, packed, near, far)
    moments, passed = pl.pallas_call(
        functools.partial(score_kernel, planes, helpers, 1),
        out_shape=[jax.ShapeDtypeStruct((planes * rank, wide), kind) for kind in (F32, BF16)],
        compiler_params=PARAMS,
        name="score_last",
    )(mine, theirs, across, begun)
    folded = pl.pallas_call(
        functools.partial(fold_kernel, planes),
        out_shape=[jax.ShapeDtypeStruct((rank, wide), F32)]
        + [jax.ShapeDtypeStruct((rank * width // LANES + TILE, LANES), BF16)] * (planes - 1),
        compiler_params=PARAMS,
        name="fold",
    )(moments, swap(passed, "help", 1))
    moments = [folded[0]] + swaps(folded[1:], "shard", INNER)

    exact, scaled = pl.pallas_call(
        scale_kernel,
        out_shape=[block, sent],
        compiler_params=PARAMS,
        name="scale",
    )(resident, *moments)
    scaled = [exact, swap(exact, "help", 1)] + [swap(scaled, "help", d) for d in range(2, helpers)]

    sketch, regressor, *parts = pl.pallas_call(
        functools.partial(sketch_kernel, helpers),
        out_shape=[jax.ShapeDtypeStruct((rank, own_points), F32), block] + [sent] * (helpers - 1),
        out_specs=[HBM] + [VMEM] * helpers,
        scratch_shapes=[pltpu.VMEM((rank, own_points), F32), pltpu.SemaphoreType.DMA],
        compiler_params=PARAMS,
        name="sketch",
    )(mark, resident, points, *scaled)
    for part in swaps(parts, "help"):
        regressor = regressor + part.astype(F32)
    return sketch, regressor[None]


def solution(mesh):
    in_specs = (
        P(("shard", "help"), None),
        P(("shard", "help"), None),
        P(("shard", "help"), None),
        P(("shard", "help"), None),
        P("shard", None),
        P(None, ("shard", "help")),
    )
    out_specs = (P(None, ("shard", "help")), P(("shard", "help"), None, None))
    return jax.shard_map(shards, mesh=mesh, in_specs=in_specs, out_specs=out_specs, check_vma=False)
```
